32 devices in a mesh: rep: 4 (over y, x), own: 8 (over z, core).
Axes of the slice: x: 2, y: 2, z: 4, core: 2. Of those that a mesh axis runs over, the one named last changes fastest.
Arguments:
- owners: int32 [16, 1], replicated, may hold values from 0 to 7; in each aligned block of 16 rows (0 to 15, 16 to 31, ...) at most 4 rows name the same one
- inner_dense: float32 [4, 16, 65536], P('rep', None, 'own'), may hold values from -6 to 6
- anchor_dense: float32 [16, 65536], P(None, 'own'), may hold values from -6 to 6
- momentum_dense: float32 [32, 65536], P('own'), may hold values from -6 to 6
- inner_emb: float32 [4, 1600, 1024], P('rep', 'own'), may hold values from -6 to 6
- anchor_emb: float32 [1600, 1024], P('own'), may hold values from -6 to 6
- momentum_emb: float32 [1600, 64], P('own'), may hold values from -6 to 6
- basis: float32 [1024, 64], replicated, may hold values from -0.1875 to 0.1875
Outputs:
- new_dense: float32 [16, 65536], P(None, 'own')
- new_momentum_dense: float32 [32, 65536], P('own')
- new_emb: float32 [1600, 1024], P('own')
- new_momentum_emb: float32 [1600, 64], P('own')
The draws below stay inside these ranges and needn't reach their ends.
Inputs may be any that keep to these rules, and one draw needn't show every extreme that they name: `owners`: each owner position owns at most 4 blocks, and some position owns exactly 4.
All inputs are finite; a program needn't handle non-finite values.
Results may differ from the reference program's by a relative error of at most 0.00011.
Values sent between devices are 32-bit elements; how exact they have to be, the bound alone decides.
No kernel may reach another device: no remote copies, remote signals or barrier semaphores. Data moves between devices by JAX's collectives and lax.ppermute only.
A program may use at most 64 MiB of HBM per device.

```python
import math
import jax
import jax.numpy as jnp
import numpy as np
from jax import lax

D = 1024
UR = 64
RANK = 64
NUNITS = 16
SLOTS = 4
VOCAB = 1600
GROUPS = 4
N_OWN = 8


def levels(own_key, shape, shards, smallest, high):
    factor_of = 1.0
    for axis_at, parts in shards:
        steps = jax.random.uniform(jax.random.fold_in(jax.random.fold_in(own_key, 6), axis_at), (parts,), jnp.float32, smallest / len(shards), high / len(shards))
        factor_of = factor_of * jnp.repeat(jnp.exp(steps), shape[axis_at] // parts).reshape((-1,) + (1,) * (len(shape) - 1 - axis_at))
    return factor_of


def shared_out(stream_key, own, number, rows, number_of, top, most, slope):
    order = jax.random.permutation(stream_key, number_of)
    heavy_load, ordinary = load_shares(number_of, rows * top, most, slope, True), load_shares(number_of, rows * top, most, slope, False)
    places = jnp.arange(number_of)

    def named(tallies, rotation):
        used = int((tallies > 0).sum())
        fixed = max(1, used // 4)
        moved = fixed + (places - fixed + rotation * (used - fixed)) % max(1, number_of - fixed)
        return jnp.zeros((number_of,), jnp.int32).at[order[jnp.where(places < fixed, places, moved)]].set(jnp.asarray(tallies, jnp.int32))

    tallies = jnp.where(number % 4 == 0, named(heavy_load, number // 4), named(ordinary, number - number // 4 - 1))
    mixed = jax.random.permutation(jax.random.fold_in(own, 3), number_of)
    donor, sink = mixed[0:number_of // 2 * 2:2], mixed[1:number_of // 2 * 2:2]
    slack = jnp.minimum(tallies[donor] - 1, most - tallies[sink]) // 2
    slack = jnp.where((donor == order[0]) | (sink == order[0]) | (tallies[sink] == 0), 0, jnp.maximum(slack, 0))
    moved = jax.random.randint(jax.random.fold_in(own, 4), (number_of // 2,), 0, 1 << 20) % (slack + 1)
    tallies = tallies.at[donor].add(-moved).at[sink].add(moved)
    labels = jnp.searchsorted(jnp.cumsum(tallies), jnp.arange(rows * top), side="right").astype(jnp.int32)
    grid = labels.reshape(top, rows).T
    grid = grid[jax.random.permutation(jax.random.fold_in(own, 1), rows)]
    rotation = jax.random.randint(jax.random.fold_in(own, 2), (rows, 1), 0, top)
    return jnp.take_along_axis(grid, (jnp.arange(top)[None, :] + rotation) % top, axis=1)


def load_shares(amount, total, bound, skew, full):
    weights = [(1 << 20) // math.isqrt(grade ** skew) + 1 for grade in range(1, amount + 1)]
    largest = bound if full else min(bound, max(-(-total // amount), total * weights[0] // sum(weights)))
    least = 1 if total - largest >= amount - 1 else 0
    holding, surplus = [largest] + [least] * (amount - 1), total - largest - least * (amount - 1)
    while surplus > 0:
        movable = [i for i in range(1, amount) if holding[i] < largest] or [i for i in range(1, amount) if holding[i] < bound]
        whole, left = sum([weights[i] for i in movable]), surplus
        for i in movable:
            addition = min(bound - holding[i], max(1, left * weights[i] // whole), surplus)
            holding[i] = holding[i] + addition
            surplus = surplus - addition
    return np.array(holding)


def bell_draw(rng, extent, width, most, cuts=(), held_as=jnp.bfloat16):
    values = width * jax.random.normal(rng, extent, jnp.float32)
    if cuts:
        values = values * levels(rng, extent, cuts, -0.22, 0.18)
    return jnp.clip(values, -most, most).astype(held_as)


def setup_inputs(seed: int = 0) -> dict:
    streams_of = jax.random.split(jax.random.key(seed), 9)
    owners_keys = jax.random.split(jax.random.fold_in(streams_of[0], 1), NUNITS // NUNITS)
    owners_turns = jax.random.permutation(jax.random.fold_in(streams_of[0], 3), NUNITS // NUNITS)
    owners = jax.vmap(lambda own, number: shared_out(jax.random.fold_in(streams_of[0], 2), own, number, NUNITS, N_OWN, 1, SLOTS, 2))(owners_keys, owners_turns).reshape((NUNITS, 1))
    inner_dense = bell_draw(streams_of[1], (GROUPS, NUNITS, UR * D), 1.0, 6.0, ((0, 4), (2, 8)), jnp.float32)
    anchor_dense = bell_draw(streams_of[2], (NUNITS, UR * D), 1.0, 6.0, ((1, 8),), jnp.float32)
    momentum_dense = bell_draw(streams_of[3], (N_OWN * SLOTS, UR * D), 1.0, 6.0, ((0, 8),), jnp.float32)
    inner_emb = bell_draw(streams_of[4], (GROUPS, VOCAB, D), 1.0, 6.0, ((0, 4), (1, 8)), jnp.float32)
    anchor_emb = bell_draw(streams_of[5], (VOCAB, D), 1.0, 6.0, ((0, 8),), jnp.float32)
    momentum_emb = bell_draw(streams_of[6], (VOCAB, RANK), 1.0, 6.0, ((0, 8),), jnp.float32)
    basis = bell_draw(streams_of[7], (D, RANK), D ** -0.5, 0.1875, (), jnp.float32)
    return dict(owners=owners, inner_dense=inner_dense, anchor_dense=anchor_dense, momentum_dense=momentum_dense, inner_emb=inner_emb, anchor_emb=anchor_emb, momentum_emb=momentum_emb, basis=basis)


outer_rate = 0.7
momentum_decay = 0.9


def reference(owners, inner_dense, anchor_dense, momentum_dense, inner_emb, anchor_emb, momentum_emb, basis):
    owner_flat = owners[:, 0].astype(jnp.int32)
    onehot = (owner_flat[:, None] == jnp.arange(N_OWN, dtype=jnp.int32)[None, :]).astype(jnp.int32)
    running = jnp.cumsum(onehot, axis=0) - onehot
    slot_of = jnp.sum(running * onehot, axis=1).astype(jnp.int32)
    row_index = owner_flat * SLOTS + slot_of
    summed = jnp.zeros_like(anchor_dense)
    for group in range(GROUPS):
        summed = summed + (anchor_dense - inner_dense[group])
    mean_grad = summed / GROUPS
    grad_slots = jnp.zeros(momentum_dense.shape, anchor_dense.dtype).at[row_index].set(mean_grad)
    live_rows = jnp.zeros((momentum_dense.shape[0],), jnp.int32).at[row_index].set(1)
    new_momentum_dense = jnp.where(live_rows[:, None] > 0, momentum_decay * momentum_dense + grad_slots, 0.0)
    update = mean_grad + momentum_decay * new_momentum_dense[row_index]
    new_dense = anchor_dense - outer_rate * update
    factor_sum = jnp.zeros(momentum_emb.shape, anchor_emb.dtype)
    for group in range(GROUPS):
        factor_sum = factor_sum + jnp.dot(anchor_emb - inner_emb[group], basis, precision=lax.Precision.HIGHEST, preferred_element_type=jnp.float32)
    mean_factor = factor_sum / GROUPS
    new_momentum_emb = momentum_decay * momentum_emb + mean_factor
    emb_update = mean_factor + momentum_decay * new_momentum_emb
    new_emb = anchor_emb - outer_rate * jnp.dot(emb_update, basis.T, precision=lax.Precision.HIGHEST, preferred_element_type=jnp.float32)
    return (new_dense, new_momentum_dense, new_emb, new_momentum_emb)
```

```python
import functools

import jax
import jax.numpy as jnp
from jax import lax
from jax.experimental import pallas as pl
from jax.experimental.pallas import tpu as pltpu
from jax.sharding import PartitionSpec as P

outer_rate = 0.7
momentum_decay = 0.9
most_direct_chips = 8
f32 = jnp.float32
vmem_limit = 48 * 1024 * 1024


def on_chip(x):
    return pltpu.with_memory_space_constraint(x, pltpu.VMEM)


def kept(shape):
    return pltpu.VMEM(shape, f32)


def stored(shape):
    return jax.ShapeDtypeStruct(shape, f32)


def run(body, outs, operands, scalars=(), scratch=(), name=None):
    vmem = pl.BlockSpec(memory_space=pltpu.VMEM)
    smem = pl.BlockSpec(memory_space=pltpu.SMEM)
    return pl.pallas_call(
        body,
        out_shape=list(outs),
        in_specs=[smem] * len(scalars) + [vmem] * len(operands),
        out_specs=[vmem] * len(outs),
        scratch_shapes=list(scratch),
        compiler_params=pltpu.CompilerParams(vmem_limit_bytes=vmem_limit),
        name=name,
    )(*scalars, *operands)


def swap(x, axis, count, mask):
    return lax.ppermute(x, axis, [(i, i ^ mask) for i in range(count)])


def places(owners, owner_count, slot_count):
    owner_flat = owners[:, 0]
    onehot = (owner_flat[:, None] == jnp.arange(owner_count, dtype=jnp.int32)[None, :]).astype(
        jnp.int32
    )
    running = jnp.cumsum(onehot, axis=0) - onehot
    slot_of = jnp.sum(running * onehot, axis=1)
    row_of = owner_flat * slot_count + slot_of
    rows = jnp.arange(owner_count * slot_count, dtype=jnp.int32)
    named = (row_of[:, None] == rows[None, :]).astype(jnp.int32)
    block_of = jnp.sum(named * jnp.arange(owner_flat.shape[0], dtype=jnp.int32)[:, None], axis=0)
    return row_of, block_of, jnp.sum(onehot, axis=0)


def difference_body(part, groups, me, anchor, inner, *outs):
    for k in range(groups):
        at = pl.ds(pl.multiple_of((me[0] ^ k) * part, 128), part)
        outs[k][...] = anchor[:, at] - inner[0, :, at]


def momentum_body(part, groups, me, momentum, same, other):
    chips = same.shape[0]
    for chip in range(chips):
        for o, out in enumerate((same, other)):
            piece = 2 * chip + (me[2] ^ o)
            at = pl.multiple_of((piece * groups + me[0]) * part, 128)
            out[chip] = momentum[:, pl.ds(at, part)]


def mean_body(groups, me, block_of, *refs):
    parts, (mean, same, other) = refs[:groups], refs[groups:]
    total = parts[0][...]
    for ref in parts[1:]:
        total = total + ref[...]
    mean[...] = total / groups
    chips, slots, _ = same.shape

    def fill(chip, carry):
        for o, out in enumerate((same, other)):
            for s in range(slots):
                block = block_of[(2 * chip + (me[2] ^ o)) * slots + s]
                out[chip, pl.ds(s, 1), :] = mean[pl.ds(block, 1), :]
        return carry

    lax.fori_loop(0, chips, fill, 0, unroll=chips <= 8)


def pack_body(direct, me, same, other, *outs):
    if direct:
        for k, out in enumerate(outs):
            out[0] = same[me[1] ^ k]
            out[1] = other[me[1] ^ k]
    else:
        outs[0][:, 0] = same[...]
        outs[0][:, 1] = other[...]


def join_body(*refs):
    out = refs[-1]
    for k, ref in enumerate(refs[:-1]):
        out[k] = ref[...]


def dense_body(part, direct, me, row_of, anchor, mean, *refs):
    *received, out, rows = refs
    slots = received[0].shape[-2]
    blocks = mean.shape[0]
    if direct:
        for k, ref in enumerate(received):
            rows[k] = ref[...]
        table = rows
    else:
        table = received[0]

    def update(block, carry):
        row = row_of[block]
        owner = row // slots
        chip = (owner // 2) ^ me[1] if direct else owner // 2
        momentum = table[chip, (owner % 2) ^ me[2], pl.ds(row % slots, 1), :]
        mean_row = mean[pl.ds(block, 1), :]
        new_momentum = momentum_decay * momentum + mean_row
        out[pl.ds(block, 1), :] = out[pl.ds(block, 1), :] - outer_rate * (
            mean_row + momentum_decay * new_momentum
        )
        return carry

    out[...] = anchor[:, pl.ds(pl.multiple_of(me[0] * part, 128), part)]

    lax.fori_loop(0, blocks, update, 0, unroll=blocks <= 16)


def dense_out_body(part, me, *refs):
    out = refs[-1]
    for k, ref in enumerate(refs[:-1]):
        out[:, pl.ds(pl.multiple_of((me[0] ^ k) * part, 128), part)] = ref[...]


def momentum_out_body(part, direct, me, owned, momentum, *refs):
    out = refs[-1]
    groups = len(refs) - 1
    chips = refs[0].shape[0]
    slots = momentum.shape[0]
    live = lax.broadcasted_iota(jnp.int32, (slots, part), 0) < owned[me[1] * 2 + me[2]]

    def fill(k, carry):
        chip = me[1] ^ k if direct else k
        for o in range(2):
            piece = 2 * chip + (me[2] ^ o)
            for g in range(groups):
                at = pl.ds(pl.multiple_of((piece * groups + (me[0] ^ g)) * part, 128), part)
                out[:, at] = jnp.where(
                    live, momentum_decay * momentum[:, at] + refs[g][k, o], 0.0
                )
        return carry

    lax.fori_loop(0, chips, fill, 0, unroll=chips <= 8)


def dot(a, b, contract):
    return lax.dot_general(
        a,
        b,
        ((contract), ((), ())),
        precision=lax.Precision.HIGHEST,
        preferred_element_type=f32,
    )


def factor_body(anchor, inner, basis_t, out):
    out[...] = dot(basis_t[...], anchor[...] - inner[0], ((1,), (1,)))


def embedding_body(groups, anchor, momentum_t, basis_t, *refs):
    parts, (new_emb, new_momentum_t) = refs[:groups], refs[groups:]
    total = parts[0][...]
    for ref in parts[1:]:
        total = total + ref[...]
    mean = total / groups
    moved = momentum_decay * momentum_t[...] + mean
    new_momentum_t[...] = moved
    update = mean + momentum_decay * moved
    new_emb[...] = anchor[...] - outer_rate * dot(update, basis_t[...], ((0,), (0,)))


def over_chips(same, other, me, chips, owner_count):
    other = swap(other, "own", owner_count, 1)
    shape = (2,) + same.shape[1:]
    if chips <= most_direct_chips:
        outs = run(
            functools.partial(pack_body, True),
            [kept(shape)] * chips,
            [on_chip(same), on_chip(other)],
            [me],
            name="pack",
        )
        return [outs[0]] + [swap(outs[k], "own", owner_count, 2 * k) for k in range(1, chips)]
    (packed,) = run(
        functools.partial(pack_body, False),
        [stored((chips,) + shape)],
        [same, other],
        [me],
        name="pack",
    )
    groups = [list(range(core, owner_count, 2)) for core in range(2)]
    return [
        lax.all_to_all(
            packed, "own", split_axis=0, concat_axis=0, axis_index_groups=groups, tiled=True
        )
    ]


def per_device(
    owners, inner_dense, anchor_dense, momentum_dense, inner_emb, anchor_emb, momentum_emb, basis
):
    owner_count = lax.axis_size("own")
    groups = lax.axis_size("rep")
    chips = owner_count // 2
    direct = chips <= most_direct_chips
    slot_count = momentum_dense.shape[0]
    blocks, piece_len = anchor_dense.shape
    part = piece_len // groups
    position = lax.axis_index("own")
    me = jnp.stack([lax.axis_index("rep"), position // 2, position % 2]).astype(jnp.int32)
    row_of, block_of, owned = places(owners, owner_count, slot_count)

    parts = run(
        functools.partial(difference_body, part, groups),
        [kept((blocks, part))] * groups,
        [anchor_dense, inner_dense],
        [me],
        name="difference",
    )
    parts = [parts[0]] + [swap(parts[k], "rep", groups, k) for k in range(1, groups)]

    chunk = (chips, slot_count, part)
    same, other = run(
        functools.partial(momentum_body, part, groups),
        [kept(chunk)] * 2,
        [momentum_dense],
        [me],
        name="momentum_pieces",
    )
    momentum_rows = over_chips(same, other, me, chips, owner_count)

    rows = anchor_emb.shape[0]
    rank = basis.shape[1]
    basis_t = basis.T
    (factor,) = run(
        factor_body, [kept((rank, rows))], [anchor_emb, inner_emb, basis_t], name="factor"
    )
    factors = [factor] + [swap(factor, "rep", groups, k) for k in range(1, groups)]

    mean, same, other = run(
        functools.partial(mean_body, groups),
        [kept((blocks, part)), kept(chunk), kept(chunk)],
        [on_chip(x) for x in parts],
        [me, block_of],
        name="mean",
    )
    table = (chips, 2, slot_count, part)
    gradient_rows = over_chips(same, other, me, chips, owner_count)

    (dense,) = run(
        functools.partial(dense_body, part, direct),
        [kept((blocks, part))],
        [anchor_dense, on_chip(mean)] + [on_chip(x) for x in momentum_rows],
        [me, row_of],
        [pltpu.VMEM(table if direct else (8, 128), f32)],
        name="dense",
    )
    dense = [dense] + [swap(dense, "rep", groups, k) for k in range(1, groups)]

    if direct:
        (gradient,) = run(
            join_body, [kept(table)], [on_chip(x) for x in gradient_rows], name="join"
        )
    else:
        (gradient,) = gradient_rows
    gradient = [gradient] + [swap(gradient, "rep", groups, k) for k in range(1, groups)]

    (new_dense,) = run(
        functools.partial(dense_out_body, part),
        [stored((blocks, piece_len))],
        [on_chip(x) for x in dense],
        [me],
        name="dense_out",
    )
    new_emb, new_momentum_t = run(
        functools.partial(embedding_body, groups),
        [stored(anchor_emb.shape), stored((rank, rows))],
        [anchor_emb, momentum_emb.T, basis_t] + [on_chip(x) for x in factors],
        name="embedding",
    )
    (new_momentum_dense,) = run(
        functools.partial(momentum_out_body, part, direct),
        [stored(momentum_dense.shape)],
        [momentum_dense] + [on_chip(x) for x in gradient],
        [me, owned],
        name="momentum_out",
    )
    return (new_dense, new_momentum_dense, new_emb, new_momentum_t.T)


def solution(mesh):
    placed = (
        P(),
        P("rep", None, "own"),
        P(None, "own"),
        P("own", None),
        P("rep", "own", None),
        P("own", None),
        P("own", None),
        P(),
    )
    return jax.shard_map(
        per_device,
        mesh=mesh,
        in_specs=placed,
        out_specs=(P(None, "own"), P("own", None), P("own", None), P("own", None)),
        check_vma=False,
    )
```

```python
import functools

import jax
import jax.numpy as jnp
from jax import lax
from jax.experimental import pallas as pl
from jax.experimental.pallas import tpu as pltpu
from jax.sharding import PartitionSpec as P

outer_rate = 0.7
momentum_decay = 0.9
most_direct_chips = 8
f32 = jnp.float32
vmem_limit = 48 * 1024 * 1024


def on_chip(x):
    return pltpu.with_memory_space_constraint(x, pltpu.VMEM)


def kept(shape):
    return pltpu.VMEM(shape, f32)


def stored(shape):
    return jax.ShapeDtypeStruct(shape, f32)


def in_scalars(x):
    return pltpu.with_memory_space_constraint(x, pltpu.SMEM)


def in_hbm(x):
    return pltpu.with_memory_space_constraint(x, pltpu.HBM)


vmem = pl.BlockSpec(memory_space=pltpu.VMEM)
smem = pl.BlockSpec(memory_space=pltpu.SMEM)
anywhere = pl.BlockSpec(memory_space=pl.ANY)


def run(body, outs, operands, scalars=(), scratch=(), far=(), out_specs=None, name=None):
    return pl.pallas_call(
        body,
        out_shape=list(outs),
        in_specs=[smem] * len(scalars) + [anywhere] * len(far) + [vmem] * len(operands),
        out_specs=out_specs or [vmem] * len(outs),
        scratch_shapes=list(scratch),
        compiler_params=pltpu.CompilerParams(vmem_limit_bytes=vmem_limit),
        name=name,
    )(*[in_scalars(x) for x in scalars], *[in_hbm(x) for x in far], *operands)


def swap(x, axis, count, mask):
    return lax.ppermute(x, axis, [(i, i ^ mask) for i in range(count)])


def place():
    position = lax.axis_index("own")
    return lax.axis_index("rep"), lax.shift_right_logical(position, 1), position & 1


def column(index, part):
    return pl.ds(pl.multiple_of(index * part, 128), part)


def places_body(slots, owners, row_of, block_of, owned):
    blocks, owner_count = row_of.shape[0], owned.shape[0]

    def clear(i, carry):
        block_of[i] = 0
        return carry

    def clear_count(i, carry):
        owned[i] = 0
        return carry

    def name(u, carry):
        owner = owners[u]
        slot = owned[owner]
        row = owner * slots + slot
        row_of[u] = row
        block_of[row] = u
        owned[owner] = slot + 1
        return carry

    lax.fori_loop(0, block_of.shape[0], clear, 0)
    lax.fori_loop(0, owner_count, clear_count, 0)
    lax.fori_loop(0, blocks, name, 0)


def start_body(groups, part, anchor, inner, momentum, *refs):
    outs, (quarter, same, other, held), (far, near, sem) = (
        refs[:groups],
        refs[groups : groups + 4],
        refs[groups + 4 :],
    )
    rep, chip, core = place()
    copies = []
    for k in (*range(1, groups), 0):
        at = column(rep ^ k, part)
        pair = (
            pltpu.make_async_copy(anchor.at[:, at], far.at[k], sem.at[k]),
            pltpu.make_async_copy(inner.at[0, :, at], near.at[k], sem.at[groups + k]),
        )
        for copy in pair:
            copy.start()
        copies.append((k, pair))
    whole = pltpu.make_async_copy(momentum, held, sem.at[2 * groups])
    whole.start()
    for k, pair in copies:
        for copy in pair:
            copy.wait()
        outs[k][...] = far[k] - near[k]
        if k == 0:
            quarter[...] = far[0]
    whole.wait()

    def take(to, carry):
        for o, out in enumerate((same, other)):
            piece = 2 * to + (core ^ o)
            out[to] = held[:, column(piece * groups + rep, part)]
        return carry

    lax.fori_loop(0, same.shape[0], take, 0, unroll=same.shape[0] <= 8)


def mean_body(groups, block_of, *refs):
    parts, (mean, same, other) = refs[:groups], refs[groups:]
    _, _, core = place()
    total = parts[0][...]
    for ref in parts[1:]:
        total = total + ref[...]
    mean[...] = total / groups
    chips, slots, _ = same.shape

    def fill(chip, carry):
        for o, out in enumerate((same, other)):
            for s in range(slots):
                block = block_of[(2 * chip + (core ^ o)) * slots + s]
                out[chip, pl.ds(s, 1), :] = mean[pl.ds(block, 1), :]
        return carry

    lax.fori_loop(0, chips, fill, 0, unroll=chips <= 8)


def pack_body(direct, same, other, *outs):
    _, chip, _ = place()
    if direct:
        for k, out in enumerate(outs):
            out[0] = same[chip ^ k]
            out[1] = other[chip ^ k]
    else:
        outs[0][:, 0] = same[...]
        outs[0][:, 1] = other[...]


def join_body(*refs):
    out = refs[-1]
    for k, ref in enumerate(refs[:-1]):
        out[k] = ref[...]


def tiles(rows, columns):
    return [
        (i, min(8, rows - i), j, min(128, columns - j))
        for i in range(0, rows, 8)
        for j in range(0, columns, 128)
    ]


def dense_body(direct, row_of, quarter, mean, factor, *refs):
    *received, out, rows, work = refs
    _, here, core = place()
    slots = received[0].shape[-2]
    blocks, part = mean.shape
    if direct:
        for k, ref in enumerate(received):
            rows[k] = ref[...]
        table = rows
    else:
        table = received[0]

    def update(block, carry):
        row = row_of[block]
        owner = row // slots
        chip = (owner // 2) ^ here if direct else owner // 2
        momentum = table[chip, (owner % 2) ^ core, pl.ds(row % slots, 1), :]
        mean_row = mean[pl.ds(block, 1), :]
        new_momentum = momentum_decay * momentum + mean_row
        work[pl.ds(block, 1), :] = quarter[pl.ds(block, 1), :] - outer_rate * (
            mean_row + momentum_decay * new_momentum
        )
        return carry

    lax.fori_loop(0, blocks, update, 0, unroll=blocks <= 16)
    at = 0
    for ref in (work, factor):
        for i, height, j, width in tiles(*ref.shape):
            out[at : at + height, :width] = ref[i : i + height, j : j + width]
            at += 8


def dense_out_body(part, *refs):
    out = refs[-1]
    rep, _, _ = place()
    blocks = out.shape[0]
    for k, ref in enumerate(refs[:-1]):
        for t, (i, height, j, width) in enumerate(tiles(blocks, part)):
            at = pl.multiple_of((rep ^ k) * part, 128) + j
            out[i : i + height, pl.ds(pl.multiple_of(at, 128), width)] = ref[
                8 * t : 8 * t + height, :width
            ]


def momentum_out_body(part, direct, owned, momentum, *refs):
    out = refs[-1]
    rep, here, core = place()
    groups = len(refs) - 1
    chips = refs[0].shape[0]
    slots = momentum.shape[0]
    live = lax.broadcasted_iota(jnp.int32, (slots, part), 0) < owned[here * 2 + core]

    def fill(k, carry):
        chip = here ^ k if direct else k
        for o in range(2):
            piece = 2 * chip + (core ^ o)
            for g in range(groups):
                at = column(piece * groups + (rep ^ g), part)
                out[:, at] = jnp.where(
                    live, momentum_decay * momentum[:, at] + refs[g][k, o], 0.0
                )
        return carry

    lax.fori_loop(0, chips, fill, 0, unroll=chips <= 8)


def dot(a, b, contract):
    return lax.dot_general(
        a,
        b,
        ((contract), ((), ())),
        precision=lax.Precision.HIGHEST,
        preferred_element_type=f32,
    )


def factor_body(anchor, inner, basis_t, out):
    out[...] = dot(basis_t[...], anchor[...] - inner[0], ((1,), (1,)))


def embedding_body(groups, skip, anchor, momentum_t, basis_t, *refs):
    parts, (new_emb, new_momentum_t, mean) = refs[:groups], refs[groups:]
    for t, (i, height, j, width) in enumerate(tiles(*mean.shape)):
        at = slice(skip + 8 * t, skip + 8 * t + height)
        total = parts[0][at, :width]
        for ref in parts[1:]:
            total = total + ref[at, :width]
        mean[i : i + height, j : j + width] = total / groups
    moved = momentum_decay * momentum_t[...] + mean[...]
    new_momentum_t[...] = moved
    update = mean[...] + momentum_decay * moved
    new_emb[...] = anchor[...] - outer_rate * dot(update, basis_t[...], ((0,), (0,)))


def over_chips(same, other, chips, owner_count, name):
    other = swap(other, "own", owner_count, 1)
    shape = (2,) + same.shape[1:]
    if chips <= most_direct_chips:
        outs = run(
            functools.partial(pack_body, True),
            [kept(shape)] * chips,
            [on_chip(same), on_chip(other)],
            name=name,
        )
        return [outs[0]] + [swap(outs[k], "own", owner_count, 2 * k) for k in range(1, chips)]
    (packed,) = run(
        functools.partial(pack_body, False),
        [stored((chips,) + shape)],
        [same, other],
        name=name,
    )
    groups = [list(range(core, owner_count, 2)) for core in range(2)]
    return [
        lax.all_to_all(
            packed, "own", split_axis=0, concat_axis=0, axis_index_groups=groups, tiled=True
        )
    ]


def per_device(
    owners, inner_dense, anchor_dense, momentum_dense, inner_emb, anchor_emb, momentum_emb, basis
):
    owner_count = lax.axis_size("own")
    groups = lax.axis_size("rep")
    chips = owner_count // 2
    direct = chips <= most_direct_chips
    slot_count = momentum_dense.shape[0]
    blocks, piece_len = anchor_dense.shape
    part = piece_len // groups
    rows, rank = momentum_emb.shape
    chunk = (chips, slot_count, part)
    table = (chips, 2, slot_count, part)

    *parts, quarter, same, other, momentum = run(
        functools.partial(start_body, groups, part),
        [kept((blocks, part))] * (groups + 1) + [kept(chunk)] * 2 + [kept(momentum_dense.shape)],
        [],
        far=[anchor_dense, inner_dense, momentum_dense],
        scratch=[
            pltpu.VMEM((groups, blocks, part), f32),
            pltpu.VMEM((groups, blocks, part), f32),
            pltpu.SemaphoreType.DMA((2 * groups + 1,)),
        ],
        name="start",
    )
    parts = [parts[0]] + [swap(parts[k], "rep", groups, k) for k in range(1, groups)]
    momentum_rows = over_chips(same, other, chips, owner_count, "pack_momentum")

    row_of, block_of, owned = run(
        functools.partial(places_body, slot_count),
        [
            pltpu.SMEM((blocks,), jnp.int32),
            pltpu.SMEM((owner_count * slot_count,), jnp.int32),
            pltpu.SMEM((owner_count,), jnp.int32),
        ],
        [],
        scalars=[owners[:, 0]],
        out_specs=[smem] * 3,
        name="places",
    )
    basis_t = basis.T
    (factor,) = run(
        factor_body, [kept((rank, rows))], [anchor_emb, inner_emb, basis_t], name="factor"
    )

    mean, same, other = run(
        functools.partial(mean_body, groups),
        [kept((blocks, part)), kept(chunk), kept(chunk)],
        [on_chip(x) for x in parts],
        [block_of],
        name="mean",
    )
    gradient_rows = over_chips(same, other, chips, owner_count, "pack_mean")

    skip = 8 * len(tiles(blocks, part))
    (dense,) = run(
        functools.partial(dense_body, direct),
        [kept((skip + 8 * len(tiles(rank, rows)), 128))],
        [on_chip(x) for x in (quarter, mean, factor, *momentum_rows)],
        [row_of],
        [
            pltpu.VMEM(table if direct else (8, 128), f32),
            pltpu.VMEM((blocks, part), f32),
        ],
        name="dense",
    )
    dense = [dense] + [swap(dense, "rep", groups, k) for k in range(1, groups)]

    if direct:
        (gradient,) = run(
            join_body, [kept(table)], [on_chip(x) for x in gradient_rows], name="join"
        )
    else:
        (gradient,) = gradient_rows
    gradient = [gradient] + [swap(gradient, "rep", groups, k) for k in range(1, groups)]

    (new_dense,) = run(
        functools.partial(dense_out_body, part),
        [stored((blocks, piece_len))],
        [on_chip(x) for x in dense],
        name="dense_out",
    )
    new_emb, new_momentum_t = run(
        functools.partial(embedding_body, groups, skip),
        [stored(anchor_emb.shape), stored((rank, rows))],
        [anchor_emb, momentum_emb.T, basis_t] + [on_chip(x) for x in dense],
        scratch=[pltpu.VMEM((rank, rows), f32)],
        name="embedding",
    )
    (new_momentum_dense,) = run(
        functools.partial(momentum_out_body, part, direct),
        [stored(momentum_dense.shape)],
        [on_chip(momentum)] + [on_chip(x) for x in gradient],
        [owned],
        name="momentum_out",
    )
    return (new_dense, new_momentum_dense, new_emb, new_momentum_t.T)


def solution(mesh):
    placed = (
        P(),
        P("rep", None, "own"),
        P(None, "own"),
        P("own", None),
        P("rep", "own", None),
        P("own", None),
        P("own", None),
        P(),
    )
    return jax.shard_map(
        per_device,
        mesh=mesh,
        in_specs=placed,
        out_specs=(P(None, "own"), P("own", None), P("own", None), P("own", None)),
        check_vma=False,
    )
```

```python
import functools

import jax
import jax.numpy as jnp
from jax import lax
from jax.experimental import pallas as pl
from jax.experimental.pallas import tpu as pltpu
from jax.sharding import PartitionSpec as P

outer_rate = 0.7
momentum_decay = 0.9
most_direct_chips = 8
f32 = jnp.float32
vmem_limit = 48 * 1024 * 1024


def on_chip(x):
    return pltpu.with_memory_space_constraint(x, pltpu.VMEM)


def kept(shape):
    return pltpu.VMEM(shape, f32)


def stored(shape):
    return jax.ShapeDtypeStruct(shape, f32)


def in_scalars(x):
    return pltpu.with_memory_space_constraint(x, pltpu.SMEM)


def in_hbm(x):
    return pltpu.with_memory_space_constraint(x, pltpu.HBM)


vmem = pl.BlockSpec(memory_space=pltpu.VMEM)
smem = pl.BlockSpec(memory_space=pltpu.SMEM)
anywhere = pl.BlockSpec(memory_space=pl.ANY)


def run(
    body, outs, operands, scalars=(), scratch=(), far=(), after=(), out_specs=None, name=None
):
    skip = len(after)

    def whole(*refs):
        body(*refs[skip:])

    return pl.pallas_call(
        whole,
        out_shape=list(outs),
        in_specs=[anywhere] * skip
        + [smem] * len(scalars)
        + [anywhere] * len(far)
        + [vmem] * len(operands),
        out_specs=out_specs or [vmem] * len(outs),
        scratch_shapes=list(scratch),
        compiler_params=pltpu.CompilerParams(vmem_limit_bytes=vmem_limit),
        name=name,
    )(
        *[on_chip(x) for x in after],
        *[in_scalars(x) for x in scalars],
        *[in_hbm(x) for x in far],
        *operands,
    )


def swap(x, axis, count, mask):
    return lax.ppermute(x, axis, [(i, i ^ mask) for i in range(count)])


def place():
    position = lax.axis_index("own")
    return lax.axis_index("rep"), lax.shift_right_logical(position, 1), position & 1


def column(index, part):
    return pl.ds(pl.multiple_of(index * part, 128), part)


def name_places(slots, owners, row_of, block_of, owned):
    blocks, owner_count = row_of.shape[0], owned.shape[0]

    def clear(i, carry):
        block_of[i] = 0
        return carry

    def clear_count(i, carry):
        owned[i] = 0
        return carry

    def name(u, carry):
        owner = owners[u]
        slot = owned[owner]
        row = owner * slots + slot
        row_of[u] = row
        block_of[row] = u
        owned[owner] = slot + 1
        return carry

    short = blocks <= 16
    lax.fori_loop(0, block_of.shape[0], clear, 0, unroll=short)
    lax.fori_loop(0, owner_count, clear_count, 0, unroll=short)
    lax.fori_loop(0, blocks, name, 0, unroll=short)


def start_body(groups, part, owners, anchor, inner, momentum, *refs):
    outs, (quarter, same, other, held), named, (own, far, near, sem) = (
        refs[:groups],
        refs[groups : groups + 4],
        refs[groups + 4 : groups + 7],
        refs[groups + 7 :],
    )
    rep, chip, core = place()
    listed = pltpu.make_async_copy(owners, own, sem.at[2 * groups + 1])
    listed.start()
    copies = []
    for k in (*range(1, groups), 0):
        at = column(rep ^ k, part)
        pair = (
            pltpu.make_async_copy(anchor.at[:, at], far.at[k], sem.at[k]),
            pltpu.make_async_copy(inner.at[0, :, at], near.at[k], sem.at[groups + k]),
        )
        for copy in pair:
            copy.start()
        copies.append((k, pair))
    whole = pltpu.make_async_copy(momentum, held, sem.at[2 * groups])
    whole.start()
    listed.wait()
    name_places(same.shape[1], own, *named)
    for k, pair in copies:
        for copy in pair:
            copy.wait()
        outs[k][...] = far[k] - near[k]
        if k == 0:
            quarter[...] = far[0]
    whole.wait()

    def take(to, carry):
        for o, out in enumerate((same, other)):
            piece = 2 * to + (core ^ o)
            out[to] = held[:, column(piece * groups + rep, part)]
        return carry

    lax.fori_loop(0, same.shape[0], take, 0, unroll=same.shape[0] <= 8)


def mean_body(groups, block_of, *refs):
    parts, (mean, same, other) = refs[:groups], refs[groups:]
    _, _, core = place()
    total = parts[0][...]
    for ref in parts[1:]:
        total = total + ref[...]
    mean[...] = total / groups
    chips, slots, _ = same.shape

    def fill(chip, carry):
        for o, out in enumerate((same, other)):
            for s in range(slots):
                block = block_of[(2 * chip + (core ^ o)) * slots + s]
                out[chip, pl.ds(s, 1), :] = mean[pl.ds(block, 1), :]
        return carry

    lax.fori_loop(0, chips, fill, 0, unroll=chips <= 8)


def pack_body(direct, same, other, *outs):
    _, chip, _ = place()
    if direct:
        for k, out in enumerate(outs):
            out[0] = same[chip ^ k]
            out[1] = other[chip ^ k]
    else:
        outs[0][:, 0] = same[...]
        outs[0][:, 1] = other[...]


def join_body(direct, half, *refs):
    *received, first, second, out1, out2, out3 = refs
    chips = received[0].shape[0] if not direct else len(received)
    part = received[0].shape[-1]

    def fill(k, carry):
        for o in range(2):
            rows = received[k][o] if direct else received[0][k, o]
            for out in (out1, out2, out3):
                out[:, column(2 * k + o, part)] = rows
        return carry

    if direct:
        for k in range(chips):
            fill(k, 0)
    else:
        lax.fori_loop(0, chips, fill, 0)
    skip = 2 * chips * part
    for out, ref, start in ((out2, first, 0), (out1, second, half)):
        for t in range((out.shape[1] - skip) // 128):
            out[:, skip + 128 * t : skip + 128 * (t + 1)] = ref[start + 4 * t : start + 4 * t + 4, :]


def unfold(half, extra, messages):
    first, second = messages[1], messages[0]
    skip = first.shape[1] - 32 * half
    for t in range(extra.shape[0] // 8):
        ref, at = (first, 8 * t) if 8 * t < half else (second, 8 * t - half)
        for h in range(2):
            lane = skip + 32 * (at + 4 * h)
            extra[8 * t + 4 * h : 8 * t + 4 * h + 4, :] = ref[:, lane : lane + 128]


def tiles(rows, columns):
    return [
        (i, min(8, rows - i), j, min(128, columns - j))
        for i in range(0, rows, 8)
        for j in range(0, columns, 128)
    ]


def dense_body(direct, row_of, quarter, mean, factor, *refs):
    *received, out, rows, work = refs
    _, here, core = place()
    slots = received[0].shape[-2]
    blocks, part = mean.shape
    if direct:
        for k, ref in enumerate(received):
            rows[k] = ref[...]
        table = rows
    else:
        table = received[0]

    def update(block, carry):
        row = row_of[block]
        owner = row // slots
        chip = (owner // 2) ^ here if direct else owner // 2
        momentum = table[chip, (owner % 2) ^ core, pl.ds(row % slots, 1), :]
        mean_row = mean[pl.ds(block, 1), :]
        new_momentum = momentum_decay * momentum + mean_row
        work[pl.ds(block, 1), :] = quarter[pl.ds(block, 1), :] - outer_rate * (
            mean_row + momentum_decay * new_momentum
        )
        return carry

    lax.fori_loop(0, blocks, update, 0, unroll=blocks <= 16)
    at = 0
    for ref in (work, factor):
        for i, height, j, width in tiles(*ref.shape):
            out[at : at + height, :width] = ref[i : i + height, j : j + width]
            at += 8


def two_parts(x):
    high = x.astype(jnp.bfloat16)
    return high, (x - high.astype(f32)).astype(jnp.bfloat16)


def dot(a, b, contract):
    return lax.dot_general(a, b, (contract, ((), ())), preferred_element_type=f32)


def factor_body(anchor, inner, basis_t, out):
    rank = out.shape[0]
    high, low = two_parts(anchor[...] - inner[0])
    basis_high, basis_low = two_parts(basis_t[...])
    both = dot(jnp.concatenate([basis_high, basis_low], axis=0), high, ((1,), (1,)))
    out[...] = both[:rank] + (both[rank:] + dot(basis_high, low, ((1,), (1,))))


def finish_body(
    part, half, direct, owned, anchor, momentum_t, basis_t, momentum, *refs
):
    dense, gradient, results, (extra, mean, sem, *made) = (
        refs[:3],
        refs[3:7],
        refs[7:11],
        refs[11:],
    )
    new_dense, new_momentum, new_emb, new_momentum_t = made
    copies = [
        pltpu.make_async_copy(ref, result, sem.at[i])
        for i, (ref, result) in enumerate(zip(made, results))
    ]
    rep, here, core = place()
    slots, groups = momentum.shape[0], 4
    pieces = momentum.shape[1] // part // groups
    live = lax.broadcasted_iota(jnp.int32, (slots, part), 0) < owned[here * 2 + core]

    def fill(i, carry):
        k, o = (i >> 1, i & 1)
        piece = 2 * (here ^ k if direct else k) + (core ^ o)
        for g, ref in enumerate(gradient):
            at = column(piece * groups + (rep ^ g), part)
            rows = momentum_decay * momentum[:, at] + ref[:, column(i, part)]
            new_momentum[:, at] = jnp.where(live, rows, 0.0)
        return carry

    lax.fori_loop(0, pieces, fill, 0, unroll=pieces <= 16)
    copies[1].start()

    unfold(half, extra, (gradient[1], gradient[2]))
    parts = (*dense, extra)
    blocks = new_dense.shape[0]
    dense_tiles = tiles(blocks, part)
    for k, ref in enumerate(parts):
        for t, (i, height, j, width) in enumerate(dense_tiles):
            at = pl.multiple_of((rep ^ k) * part + j, 128)
            new_dense[i : i + height, pl.ds(at, width)] = ref[8 * t : 8 * t + height, :width]
    copies[0].start()

    for t, (i, height, j, width) in enumerate(tiles(*mean.shape)):
        at = slice(8 * (len(dense_tiles) + t), 8 * (len(dense_tiles) + t) + height)
        sums = [ref[at, :width] for ref in parts]
        while len(sums) > 1:
            sums = [a + b for a, b in zip(sums[::2], sums[1::2])]
        mean[i : i + height, j : j + width] = sums[0] / groups
    moved = momentum_decay * momentum_t[...] + mean[...]
    new_momentum_t[...] = moved
    copies[3].start()
    high, low = two_parts(mean[...] + momentum_decay * moved)
    basis_high, basis_low = two_parts(basis_t[...])
    back = dot(
        jnp.concatenate([high, low, high], axis=0),
        jnp.concatenate([basis_high, basis_high, basis_low], axis=0),
        ((0,), (0,)),
    )
    new_emb[...] = anchor[...] - outer_rate * back
    copies[2].start()
    for copy in copies:
        copy.wait()


def over_chips(same, other, chips, owner_count, name):
    other = swap(other, "own", owner_count, 1)
    shape = (2,) + same.shape[1:]
    if chips <= most_direct_chips:
        outs = run(
            functools.partial(pack_body, True),
            [kept(shape)] * chips,
            [on_chip(same), on_chip(other)],
            name=name,
        )
        moved = [outs[0]] + [swap(outs[k], "own", owner_count, 2 * k) for k in range(1, chips)]
        return moved, outs
    (packed,) = run(
        functools.partial(pack_body, False),
        [stored((chips,) + shape)],
        [same, other],
        name=name,
    )
    groups = [list(range(core, owner_count, 2)) for core in range(2)]
    moved = lax.all_to_all(
        packed, "own", split_axis=0, concat_axis=0, axis_index_groups=groups, tiled=True
    )
    return [moved], []


def per_device(
    owners, inner_dense, anchor_dense, momentum_dense, inner_emb, anchor_emb, momentum_emb, basis
):
    owner_count = lax.axis_size("own")
    groups = lax.axis_size("rep")
    chips = owner_count // 2
    direct = chips <= most_direct_chips
    slot_count = momentum_dense.shape[0]
    blocks, piece_len = anchor_dense.shape
    part = piece_len // groups
    rows, rank = momentum_emb.shape
    chunk = (chips, slot_count, part)
    table = (chips, 2, slot_count, part)

    *parts, quarter, same, other, momentum, row_of, block_of, owned = run(
        functools.partial(start_body, groups, part),
        [kept((blocks, part))] * (groups + 1)
        + [kept(chunk)] * 2
        + [kept(momentum_dense.shape)]
        + [pltpu.SMEM((n,), jnp.int32) for n in (blocks, owner_count * slot_count, owner_count)],
        [],
        far=[owners[:, 0], anchor_dense, inner_dense, momentum_dense],
        out_specs=[vmem] * (groups + 4) + [smem] * 3,
        scratch=[
            pltpu.SMEM((blocks,), jnp.int32),
            pltpu.VMEM((groups, blocks, part), f32),
            pltpu.VMEM((groups, blocks, part), f32),
            pltpu.SemaphoreType.DMA((2 * groups + 2,)),
        ],
        name="start",
    )
    parts = [parts[0]] + [swap(parts[k], "rep", groups, k) for k in range(1, groups)]
    momentum_rows, packed_momentum = over_chips(same, other, chips, owner_count, "pack_momentum")

    basis_t = basis.T
    (factor,) = run(
        factor_body, [kept((rank, rows))], [anchor_emb, inner_emb, basis_t], name="factor"
    )

    mean, same, other = run(
        functools.partial(mean_body, groups),
        [kept((blocks, part)), kept(chunk), kept(chunk)],
        [on_chip(x) for x in parts],
        [block_of],
        name="mean",
    )
    gradient_rows, packed_mean = over_chips(same, other, chips, owner_count, "pack_mean")

    skip = 8 * len(tiles(blocks, part))
    (dense,) = run(
        functools.partial(dense_body, direct),
        [kept((skip + 8 * len(tiles(rank, rows)), 128))],
        [on_chip(x) for x in (quarter, mean, factor, *momentum_rows)],
        [row_of],
        [
            pltpu.VMEM(table if direct else (8, 128), f32),
            pltpu.VMEM((blocks, part), f32),
        ],
        name="dense",
    )
    half = dense.shape[0] // 2
    dense = [dense] + [swap(dense, "rep", groups, k) for k in (1, 2)]

    length = 2 * chips * part
    messages = run(
        functools.partial(join_body, direct, half),
        [kept((slot_count, length + 32 * half))] * 2 + [kept((slot_count, length))],
        [on_chip(x) for x in (*gradient_rows, dense[1], dense[2])],
        name="join",
    )
    gradient = [messages[2]] + [swap(m, "rep", groups, k + 1) for k, m in enumerate(messages)]

    shapes = [anchor_dense.shape, momentum_dense.shape, anchor_emb.shape, (rank, rows)]
    new_dense, new_momentum_dense, new_emb, new_momentum_t = run(
        functools.partial(finish_body, part, half, direct),
        [stored(shape) for shape in shapes],
        [
            on_chip(x)
            for x in (anchor_emb, momentum_emb.T, basis_t, momentum, *dense, *gradient)
        ],
        [owned],
        out_specs=[anywhere] * 4,
        scratch=[
            pltpu.VMEM(dense[0].shape, f32),
            pltpu.VMEM((rank, rows), f32),
            pltpu.SemaphoreType.DMA((4,)),
        ]
        + [pltpu.VMEM(shape, f32) for shape in shapes],
        name="finish",
    )
    return (new_dense, new_momentum_dense, new_emb, new_momentum_t.T)


def solution(mesh):
    placed = (
        P(),
        P("rep", None, "own"),
        P(None, "own"),
        P("own", None),
        P("rep", "own", None),
        P("own", None),
        P("own", None),
        P(),
    )
    return jax.shard_map(
        per_device,
        mesh=mesh,
        in_specs=placed,
        out_specs=(P(None, "own"), P("own", None), P("own", None), P("own", None)),
        check_vma=False,
    )
```

```python
import functools

import jax
import jax.numpy as jnp
from jax import lax
from jax.experimental import pallas as pl
from jax.experimental.pallas import tpu as pltpu
from jax.sharding import PartitionSpec as P

outer_rate = 0.7
momentum_decay = 0.9
most_direct_chips = 8
f32 = jnp.float32
vmem_limit = 48 * 1024 * 1024

vmem = pl.BlockSpec(memory_space=pltpu.VMEM)
smem = pl.BlockSpec(memory_space=pltpu.SMEM)
anywhere = pl.BlockSpec(memory_space=pl.ANY)


def on_chip(x):
    return pltpu.with_memory_space_constraint(x, pltpu.VMEM)


def in_scalars(x):
    return pltpu.with_memory_space_constraint(x, pltpu.SMEM)


def in_hbm(x):
    return pltpu.with_memory_space_constraint(x, pltpu.HBM)


def kept(shape):
    return pltpu.VMEM(shape, f32)


def stored(shape):
    return jax.ShapeDtypeStruct(shape, f32)


def run(
    body, outs, operands, scalars=(), scratch=(), far=(), after=(), out_specs=None, name=None
):
    skip = len(after)

    def whole(*refs):
        body(*refs[skip:])

    return pl.pallas_call(
        whole,
        out_shape=list(outs),
        in_specs=[anywhere] * skip
        + [smem] * len(scalars)
        + [anywhere] * len(far)
        + [vmem] * len(operands),
        out_specs=out_specs or [vmem] * len(outs),
        scratch_shapes=list(scratch),
        compiler_params=pltpu.CompilerParams(vmem_limit_bytes=vmem_limit),
        name=name,
    )(
        *[on_chip(x) for x in after],
        *[in_scalars(x) for x in scalars],
        *[in_hbm(x) for x in far],
        *[on_chip(x) for x in operands],
    )


def swap(x, axis, count, mask):
    return lax.ppermute(x, axis, [(i, i ^ mask) for i in range(count)])


def place():
    position = lax.axis_index("own")
    return lax.axis_index("rep"), lax.shift_right_logical(position, 1), position & 1


def column(index, part):
    return pl.ds(pl.multiple_of(index * part, 128), part)


def tiles(rows, columns):
    return [
        (i, min(8, rows - i), j, min(128, columns - j))
        for i in range(0, rows, 8)
        for j in range(0, columns, 128)
    ]


def two_parts(x):
    high = x.astype(jnp.bfloat16)
    return high, (x - high.astype(f32)).astype(jnp.bfloat16)


def dot(a, b, contract):
    return lax.dot_general(a, b, (contract, ((), ())), preferred_element_type=f32)


def name_places(slots, owners, row_of, block_of, owned):
    blocks, owner_count = row_of.shape[0], owned.shape[0]

    def clear(i, carry):
        block_of[i] = 0
        return carry

    def clear_count(i, carry):
        owned[i] = 0
        return carry

    def name(u, carry):
        owner = owners[u]
        slot = owned[owner]
        row = owner * slots + slot
        row_of[u] = row
        block_of[row] = u
        owned[owner] = slot + 1
        return carry

    short = blocks <= 16
    lax.fori_loop(0, block_of.shape[0], clear, 0, unroll=short)
    lax.fori_loop(0, owner_count, clear_count, 0, unroll=short)
    lax.fori_loop(0, blocks, name, 0, unroll=short)


def start_body(groups, part, owners, anchor, inner, momentum, emb, inner_emb, basis_t, *refs):
    outs, (quarter, same, other, held), named, scratch = (
        refs[:groups],
        refs[groups : groups + 4],
        refs[groups + 4 : groups + 7],
        refs[groups + 7 :],
    )
    own, far, near, emb_far, emb_near, basis, factor, sem = scratch
    rep, chip, core = place()
    blocks, rank = quarter.shape[0], basis.shape[0]
    share = rank // groups
    moves = [pltpu.make_async_copy(owners, own, sem.at[2 * groups])]
    for k in range(groups):
        at = column(rep ^ k, part)
        moves.append(pltpu.make_async_copy(anchor.at[:, at], far.at[k], sem.at[k]))
        moves.append(pltpu.make_async_copy(inner.at[0, :, at], near.at[k], sem.at[groups + k]))
    for i, (a, b) in enumerate(
        ((emb, emb_far), (inner_emb.at[0], emb_near), (basis_t, basis), (momentum, held))
    ):
        moves.append(pltpu.make_async_copy(a, b, sem.at[2 * groups + 1 + i]))
    for move in moves:
        move.start()
    moves[0].wait()
    name_places(same.shape[1], own, *named)

    for k in range(groups):
        moves[2 * k + 1].wait()
        moves[2 * k + 2].wait()
        for t, (i, height, j, width) in enumerate(tiles(blocks, part)):
            rows, columns = slice(i, i + height), slice(j, j + width)
            outs[k][8 * t : 8 * t + height, :width] = far[k, rows, columns] - near[k, rows, columns]
        if k == 0:
            quarter[...] = far[0]
    for move in moves[2 * groups + 1 : 2 * groups + 4]:
        move.wait()
    high, low = two_parts(emb_far[...] - emb_near[...])
    basis_high, basis_low = two_parts(basis[...])
    both = dot(jnp.concatenate([basis_high, basis_low], axis=0), high, ((1,), (1,)))
    factor[...] = both[:rank] + (both[rank:] + dot(basis_high, low, ((1,), (1,))))
    skip = 8 * len(tiles(blocks, part))
    for k in range(groups):
        for t, (i, height, j, width) in enumerate(tiles(share, factor.shape[1])):
            rows = pl.ds(pl.multiple_of((rep ^ k) * share + i, 8), height)
            outs[k][skip + 8 * t : skip + 8 * t + height, :width] = factor[rows, j : j + width]

    moves[2 * groups + 4].wait()

    def take(to, carry):
        for o, out in enumerate((same, other)):
            piece = 2 * to + (core ^ o)
            out[to] = held[:, column(piece * groups + rep, part)]
        return carry

    lax.fori_loop(0, same.shape[0], take, 0, unroll=same.shape[0] <= 8)


def mean_body(groups, direct, block_of, *refs):
    parts, (mean, shared, *outs) = refs[:groups], refs[groups:]
    _, here, core = place()
    dense_tiles = tiles(*mean.shape)
    for t, (i, height, j, width) in enumerate(dense_tiles):
        at = slice(8 * t, 8 * t + height)
        total = parts[0][at, :width]
        for ref in parts[1:]:
            total = total + ref[at, :width]
        mean[i : i + height, j : j + width] = total / groups
    at = slice(8 * len(dense_tiles), parts[0].shape[0])
    total = parts[0][at, :]
    for ref in parts[1:]:
        total = total + ref[at, :]
    shared[...] = total / groups
    slots = outs[0].shape[-2]

    def fill(k, carry):
        for o in range(2):
            owner = 2 * (here ^ k if direct else k) + (core ^ o)
            for s in range(slots):
                row = mean[pl.ds(block_of[owner * slots + s], 1), :]
                if direct:
                    outs[k][o, pl.ds(s, 1), :] = row
                else:
                    outs[0][k, o, pl.ds(s, 1), :] = row
        return carry

    if direct:
        for k in range(len(outs)):
            fill(k, 0)
    else:
        lax.fori_loop(0, outs[0].shape[0], fill, 0)


def pack_body(direct, same, other, *outs):
    _, chip, _ = place()
    if direct:
        for k, out in enumerate(outs):
            out[0] = same[chip ^ k]
            out[1] = other[chip ^ k]
    else:
        outs[0][:, 0] = same[...]
        outs[0][:, 1] = other[...]


def other_body(direct, *refs):
    *received, out = refs
    if direct:
        for k, ref in enumerate(received):
            out[k] = ref[1]
    else:
        out[...] = received[0][:, 1]


def join_body(direct, *refs):
    *received, crossed, out = refs
    chips, _, part = crossed.shape

    def fill(k, carry):
        out[:, column(2 * k, part)] = received[k][0] if direct else received[0][k, 0]
        out[:, column(2 * k + 1, part)] = crossed[k]
        return carry

    if direct:
        for k in range(chips):
            fill(k, 0)
    else:
        lax.fori_loop(0, chips, fill, 0)


def dense_body(direct, row_of, quarter, mean, shared, *refs):
    *received, out, rows, work = refs
    _, here, core = place()
    slots = received[0].shape[-2]
    blocks = mean.shape[0]
    if direct:
        for k, ref in enumerate(received):
            rows[k] = ref[...]
        table = rows
    else:
        table = received[0]

    def update(block, carry):
        row = row_of[block]
        owner = row // slots
        chip = (owner // 2) ^ here if direct else owner // 2
        momentum = table[chip, (owner % 2) ^ core, pl.ds(row % slots, 1), :]
        mean_row = mean[pl.ds(block, 1), :]
        new_momentum = momentum_decay * momentum + mean_row
        work[pl.ds(block, 1), :] = quarter[pl.ds(block, 1), :] - outer_rate * (
            mean_row + momentum_decay * new_momentum
        )
        return carry

    lax.fori_loop(0, blocks, update, 0, unroll=blocks <= 16)
    dense_tiles = tiles(*work.shape)
    for t, (i, height, j, width) in enumerate(dense_tiles):
        out[8 * t : 8 * t + height, :width] = work[i : i + height, j : j + width]
    out[8 * len(dense_tiles) :, :] = shared[...]


def finish_body(part, anchor, momentum_t, basis_t, *refs):
    *parts, result0, result1, result2, mean, sem, new_dense, new_emb, new_momentum_t = refs
    copies = [
        pltpu.make_async_copy(ref, result, sem.at[i])
        for i, (ref, result) in enumerate(
            ((new_dense, result0), (new_emb, result1), (new_momentum_t, result2))
        )
    ]
    rep, _, _ = place()
    blocks, (rank, rows) = new_dense.shape[0], mean.shape
    share = rank // len(parts)
    dense_tiles = tiles(blocks, part)
    for k, ref in enumerate(parts):
        for t, (i, height, j, width) in enumerate(dense_tiles):
            at = pl.multiple_of((rep ^ k) * part + j, 128)
            new_dense[i : i + height, pl.ds(at, width)] = ref[8 * t : 8 * t + height, :width]
        for t, (i, height, j, width) in enumerate(tiles(share, rows)):
            at = 8 * (len(dense_tiles) + t)
            mean[pl.ds(pl.multiple_of((rep ^ k) * share + i, 8), height), j : j + width] = ref[
                at : at + height, :width
            ]
    copies[0].start()

    moved = momentum_decay * momentum_t[...] + mean[...]
    new_momentum_t[...] = moved
    copies[2].start()
    high, low = two_parts(mean[...] + momentum_decay * moved)
    basis_high, basis_low = two_parts(basis_t[...])
    back = dot(
        jnp.concatenate([high, low, high], axis=0),
        jnp.concatenate([basis_high, basis_high, basis_low], axis=0),
        ((0,), (0,)),
    )
    new_emb[...] = anchor[...] - outer_rate * back
    copies[1].start()
    for copy in copies:
        copy.wait()


def finish_momentum_body(part, direct, owned, momentum, *refs):
    *gradient, result, made, sem = refs
    rep, here, core = place()
    slots, groups = momentum.shape[0], len(gradient)
    pieces = momentum.shape[1] // part // groups
    live = lax.broadcasted_iota(jnp.int32, (slots, part), 0) < owned[here * 2 + core]

    def fill(i, carry):
        k, o = (i >> 1, i & 1)
        piece = 2 * (here ^ k if direct else k) + (core ^ o)
        for g, ref in enumerate(gradient):
            at = column(piece * groups + (rep ^ g), part)
            rows = momentum_decay * momentum[:, at] + ref[:, column(i, part)]
            made[:, at] = jnp.where(live, rows, 0.0)
        return carry

    lax.fori_loop(0, pieces, fill, 0, unroll=pieces <= 16)
    copy = pltpu.make_async_copy(made, result, sem)
    copy.start()
    copy.wait()


def over_chips(outs, direct, owner_count):
    if direct:
        return [outs[0]] + [swap(outs[k], "own", owner_count, 2 * k) for k in range(1, len(outs))]
    groups = [list(range(core, owner_count, 2)) for core in range(2)]
    return [
        lax.all_to_all(
            outs[0], "own", split_axis=0, concat_axis=0, axis_index_groups=groups, tiled=True
        )
    ]


def per_device(
    owners, inner_dense, anchor_dense, momentum_dense, inner_emb, anchor_emb, momentum_emb, basis
):
    owner_count = lax.axis_size("own")
    groups = lax.axis_size("rep")
    chips = owner_count // 2
    direct = chips <= most_direct_chips
    slot_count = momentum_dense.shape[0]
    blocks, piece_len = anchor_dense.shape
    part = piece_len // groups
    rows, rank = momentum_emb.shape
    basis_t = basis.T
    chunk = (chips, slot_count, part)
    table = (chips, 2, slot_count, part)
    message = (8 * (len(tiles(blocks, part)) + len(tiles(rank // groups, rows))), 128)
    parted = [kept(table[1:])] * chips if direct else [kept(table)]

    *parts, quarter, same, other, momentum, row_of, block_of, owned = run(
        functools.partial(start_body, groups, part),
        [kept(message)] * groups
        + [kept((blocks, part))]
        + [kept(chunk)] * 2
        + [kept(momentum_dense.shape)]
        + [pltpu.SMEM((n,), jnp.int32) for n in (blocks, owner_count * slot_count, owner_count)],
        [],
        far=[
            owners[:, 0],
            anchor_dense,
            inner_dense,
            momentum_dense,
            anchor_emb,
            inner_emb,
            basis_t,
        ],
        out_specs=[vmem] * (groups + 4) + [smem] * 3,
        scratch=[
            pltpu.SMEM((blocks,), jnp.int32),
            pltpu.VMEM((groups, blocks, part), f32),
            pltpu.VMEM((groups, blocks, part), f32),
            pltpu.VMEM(anchor_emb.shape, f32),
            pltpu.VMEM(anchor_emb.shape, f32),
            pltpu.VMEM(basis_t.shape, f32),
            pltpu.VMEM((rank, rows), f32),
            pltpu.SemaphoreType.DMA((2 * groups + 5,)),
        ],
        name="start",
    )
    parts = [parts[0]] + [swap(parts[k], "rep", groups, k) for k in range(1, groups)]

    other = swap(other, "own", owner_count, 1)
    packed = run(functools.partial(pack_body, direct), parted, [same, other], name="pack")
    momentum_rows = over_chips(packed, direct, owner_count)

    mean, shared, *sent = run(
        functools.partial(mean_body, groups, direct),
        [kept((blocks, part)), kept((8 * len(tiles(rank // groups, rows)), 128))] + parted,
        parts,
        [block_of],
        name="mean",
    )
    gradient_rows = over_chips(sent, direct, owner_count)
    (other,) = run(
        functools.partial(other_body, direct),
        [kept(chunk)],
        gradient_rows,
        name="other",
    )
    crossed = swap(other, "own", owner_count, 1)

    (dense,) = run(
        functools.partial(dense_body, direct),
        [kept(message)],
        [quarter, mean, shared, *momentum_rows],
        [row_of],
        [
            pltpu.VMEM(table if direct else (8, 128), f32),
            pltpu.VMEM((blocks, part), f32),
        ],
        name="dense",
    )
    dense = [dense] + [swap(dense, "rep", groups, k) for k in range(1, groups)]

    (gradient,) = run(
        functools.partial(join_body, direct),
        [kept((slot_count, 2 * chips * part))],
        [*gradient_rows, crossed],
        after=dense[1:],
        name="join",
    )
    gradient = [gradient] + [swap(gradient, "rep", groups, k) for k in range(1, groups)]

    shapes = [anchor_dense.shape, anchor_emb.shape, (rank, rows)]
    new_dense, new_emb, new_momentum_t = run(
        functools.partial(finish_body, part),
        [stored(shape) for shape in shapes],
        [anchor_emb, momentum_emb.T, basis_t, *dense],
        out_specs=[anywhere] * 3,
        scratch=[pltpu.VMEM((rank, rows), f32), pltpu.SemaphoreType.DMA((3,))]
        + [pltpu.VMEM(shape, f32) for shape in shapes],
        name="finish",
    )
    (new_momentum_dense,) = run(
        functools.partial(finish_momentum_body, part, direct),
        [stored(momentum_dense.shape)],
        [momentum, *gradient],
        [owned],
        out_specs=[anywhere],
        scratch=[pltpu.VMEM(momentum_dense.shape, f32), pltpu.SemaphoreType.DMA],
        name="finish_momentum",
    )
    return (new_dense, new_momentum_dense, new_emb, new_momentum_t.T)


def solution(mesh):
    placed = (
        P(),
        P("rep", None, "own"),
        P(None, "own"),
        P("own", None),
        P("rep", "own", None),
        P("own", None),
        P("own", None),
        P(),
    )
    return jax.shard_map(
        per_device,
        mesh=mesh,
        in_specs=placed,
        out_specs=(P(None, "own"), P("own", None), P("own", None), P("own", None)),
        check_vma=False,
    )
```

```python
import functools

import jax
import jax.numpy as jnp
from jax import lax
from jax.experimental import pallas as pl
from jax.experimental.pallas import tpu as pltpu
from jax.sharding import PartitionSpec as P

outer_rate = 0.7
momentum_decay = 0.9
most_direct_chips = 8
f32 = jnp.float32
vmem_limit = 48 * 1024 * 1024

vmem = pl.BlockSpec(memory_space=pltpu.VMEM)
smem = pl.BlockSpec(memory_space=pltpu.SMEM)
anywhere = pl.BlockSpec(memory_space=pl.ANY)


def on_chip(x):
    return pltpu.with_memory_space_constraint(x, pltpu.VMEM)


def in_scalars(x):
    return pltpu.with_memory_space_constraint(x, pltpu.SMEM)


def in_hbm(x):
    return pltpu.with_memory_space_constraint(x, pltpu.HBM)


def kept(shape):
    return pltpu.VMEM(shape, f32)


def stored(shape):
    return jax.ShapeDtypeStruct(shape, f32)


def run(
    body, outs, operands, scalars=(), scratch=(), far=(), after=(), out_specs=None, name=None
):
    skip = len(after)

    def whole(*refs):
        body(*refs[skip:])

    return pl.pallas_call(
        whole,
        out_shape=list(outs),
        in_specs=[anywhere] * skip
        + [smem] * len(scalars)
        + [anywhere] * len(far)
        + [vmem] * len(operands),
        out_specs=out_specs or [vmem] * len(outs),
        scratch_shapes=list(scratch),
        compiler_params=pltpu.CompilerParams(vmem_limit_bytes=vmem_limit),
        name=name,
    )(
        *[on_chip(x) for x in after],
        *[in_scalars(x) for x in scalars],
        *[in_hbm(x) for x in far],
        *[on_chip(x) for x in operands],
    )


def swap(x, axis, count, mask):
    return lax.ppermute(x, axis, [(i, i ^ mask) for i in range(count)])


def place():
    position = lax.axis_index("own")
    return lax.axis_index("rep"), lax.shift_right_logical(position, 1), position & 1


def column(index, part):
    return pl.ds(pl.multiple_of(index * part, 128), part)


def tiles(rows, columns):
    return [
        (i, min(8, rows - i), j, min(128, columns - j))
        for i in range(0, rows, 8)
        for j in range(0, columns, 128)
    ]


def two_parts(x):
    high = x.astype(jnp.bfloat16)
    return high, (x - high.astype(f32)).astype(jnp.bfloat16)


def dot(a, b, contract):
    return lax.dot_general(a, b, (contract, ((), ())), preferred_element_type=f32)


def name_places(slots, owners, row_of, block_of, owned):
    blocks, owner_count = row_of.shape[0], owned.shape[0]

    def clear(i, carry):
        block_of[i] = 0
        return carry

    def clear_count(i, carry):
        owned[i] = 0
        return carry

    def name(u, carry):
        owner = owners[u]
        slot = owned[owner]
        row = owner * slots + slot
        row_of[u] = row
        block_of[row] = u
        owned[owner] = slot + 1
        return carry

    short = blocks <= 16
    lax.fori_loop(0, block_of.shape[0], clear, 0, unroll=short)
    lax.fori_loop(0, owner_count, clear_count, 0, unroll=short)
    lax.fori_loop(0, blocks, name, 0, unroll=short)


def start_body(groups, part, owners, anchor, inner, momentum, emb, inner_emb, basis_t, *refs):
    outs, (quarter, same, other), named, scratch = (
        refs[:groups],
        refs[groups : groups + 3],
        refs[groups + 3 : groups + 6],
        refs[groups + 6 :],
    )
    own, far, near, emb_far, emb_near, basis, factor, sem, piece_sem = scratch
    rep, chip, core = place()
    blocks, rank = quarter.shape[0], basis.shape[0]
    share = rank // groups
    chips = same.shape[0]
    listed = pltpu.make_async_copy(owners, own, sem.at[2 * groups])
    listed.start()
    moves = {}
    for k in (*range(groups - 1, 0, -1), 0):
        at = column(rep ^ k, part)
        moves[k] = (
            pltpu.make_async_copy(anchor.at[:, at], far.at[k], sem.at[k]),
            pltpu.make_async_copy(inner.at[0, :, at], near.at[k], sem.at[groups + k]),
        )
        for move in moves[k]:
            move.start()
    emb_moves = [
        pltpu.make_async_copy(a, b, sem.at[2 * groups + 1 + i])
        for i, (a, b) in enumerate(
            ((basis_t, basis), (emb, emb_far), (inner_emb.at[0], emb_near))
        )
    ]
    for move in emb_moves:
        move.start()
    pieces = [
        pltpu.make_async_copy(
            momentum.at[:, column((2 * to + (core ^ o)) * groups + rep, part)],
            out.at[to],
            piece_sem.at[2 * to + o],
        )
        for to in range(chips)
        for o, out in enumerate((same, other))
    ]
    for piece in pieces:
        piece.start()
    listed.wait()
    name_places(same.shape[1], own, *named)

    dense_tiles = tiles(blocks, part)
    for k in moves:
        for move in moves[k]:
            move.wait()
        for t, (i, height, j, width) in enumerate(dense_tiles):
            rows, columns = slice(i, i + height), slice(j, j + width)
            outs[k][8 * t : 8 * t + height, :width] = far[k, rows, columns] - near[k, rows, columns]
    quarter[...] = far[0]
    for move in emb_moves:
        move.wait()
    high, low = two_parts(emb_far[...] - emb_near[...])
    basis_high, basis_low = two_parts(basis[...])
    products = dot(jnp.concatenate([basis_high, basis_low], axis=0), high, ((1,), (1,)))
    factor[...] = products[:rank] + (products[rank:] + dot(basis_high, low, ((1,), (1,))))
    skip = 8 * len(dense_tiles)
    for k in range(groups):
        for t, (i, height, j, width) in enumerate(tiles(share, factor.shape[1])):
            rows = pl.ds(pl.multiple_of((rep ^ k) * share + i, 8), height)
            outs[k][skip + 8 * t : skip + 8 * t + height, :width] = factor[rows, j : j + width]
    for piece in pieces:
        piece.wait()


def mean_body(groups, direct, block_of, *refs):
    parts, (mean, shared, *outs) = refs[:groups], refs[groups:]
    _, here, core = place()
    dense_tiles = tiles(*mean.shape)
    for t, (i, height, j, width) in enumerate(dense_tiles):
        at = slice(8 * t, 8 * t + height)
        total = parts[0][at, :width]
        for ref in parts[1:]:
            total = total + ref[at, :width]
        mean[i : i + height, j : j + width] = total / groups
    at = slice(8 * len(dense_tiles), parts[0].shape[0])
    total = parts[0][at, :]
    for ref in parts[1:]:
        total = total + ref[at, :]
    shared[...] = total / groups
    slots = outs[0].shape[-2]

    def fill(k, carry):
        for o in range(2):
            owner = 2 * (here ^ k if direct else k) + (core ^ o)
            for s in range(slots):
                row = mean[pl.ds(block_of[owner * slots + s], 1), :]
                if direct:
                    outs[k][o, pl.ds(s, 1), :] = row
                else:
                    outs[0][k, o, pl.ds(s, 1), :] = row
        return carry

    if direct:
        for k in range(len(outs)):
            fill(k, 0)
    else:
        lax.fori_loop(0, outs[0].shape[0], fill, 0)


def pack_body(direct, same, other, *outs):
    _, chip, _ = place()
    if direct:
        for k, out in enumerate(outs):
            out[0] = same[chip ^ k]
            out[1] = other[chip ^ k]
    else:
        outs[0][:, 0] = same[...]
        outs[0][:, 1] = other[...]


def other_body(direct, *refs):
    *received, out = refs
    if direct:
        for k, ref in enumerate(received):
            out[k] = ref[1]
    else:
        out[...] = received[0][:, 1]


def join_body(direct, *refs):
    *received, crossed, first, second = refs
    chips, _, part = crossed.shape
    half = chips // 2

    def fill(k, carry):
        for out, chip in ((first, k), (second, k + half)):
            mine = received[chip][0] if direct else received[0][chip, 0]
            out[:, column(2 * k, part)] = mine
            out[:, column(2 * k + 1, part)] = crossed[chip]
        return carry

    if direct:
        for k in range(half):
            fill(k, 0)
    else:
        lax.fori_loop(0, half, fill, 0)


def cut_body(ref, out):
    out[...] = ref[: out.shape[0], :]


def copies_body(*refs):
    count = len(refs) // 2
    for ref, out in zip(refs[:count], refs[count:]):
        out[:, : ref.shape[1]] = ref[...]
        if out.shape[1] > ref.shape[1]:
            out[:, ref.shape[1] :] = jnp.zeros((out.shape[0], out.shape[1] - ref.shape[1]), f32)


def dense_body(direct, row_of, quarter, mean, shared, *refs):
    *received, out, rows, work = refs
    _, here, core = place()
    slots = received[0].shape[-2]
    blocks = mean.shape[0]
    if direct:
        for k, ref in enumerate(received):
            rows[k] = ref[...]
        table = rows
    else:
        table = received[0]

    def update(block, carry):
        row = row_of[block]
        owner = row // slots
        chip = (owner // 2) ^ here if direct else owner // 2
        momentum = table[chip, (owner % 2) ^ core, pl.ds(row % slots, 1), :]
        mean_row = mean[pl.ds(block, 1), :]
        new_momentum = momentum_decay * momentum + mean_row
        work[pl.ds(block, 1), :] = quarter[pl.ds(block, 1), :] - outer_rate * (
            mean_row + momentum_decay * new_momentum
        )
        return carry

    lax.fori_loop(0, blocks, update, 0, unroll=blocks <= 16)
    dense_tiles = tiles(*work.shape)
    for t, (i, height, j, width) in enumerate(dense_tiles):
        out[8 * t : 8 * t + height, :width] = work[i : i + height, j : j + width]
    out[8 * len(dense_tiles) :, :] = shared[...]


def finish_body(part, anchor, momentum_t, basis_t, *refs):
    *parts, result0, result1, result2, mean, sem, new_dense, new_emb, new_momentum_t = refs
    copies = [
        pltpu.make_async_copy(ref, result, sem.at[i])
        for i, (ref, result) in enumerate(
            ((new_dense, result0), (new_emb, result1), (new_momentum_t, result2))
        )
    ]
    rep, _, _ = place()
    blocks, (rank, rows) = new_dense.shape[0], mean.shape
    share = rank // len(parts)
    dense_tiles = tiles(blocks, part)
    for k, ref in enumerate(parts):
        for t, (i, height, j, width) in enumerate(dense_tiles):
            at = pl.multiple_of((rep ^ k) * part + j, 128)
            new_dense[i : i + height, pl.ds(at, width)] = ref[8 * t : 8 * t + height, :width]
        for t, (i, height, j, width) in enumerate(tiles(share, rows)):
            at = 8 * (len(dense_tiles) + t)
            mean[pl.ds(pl.multiple_of((rep ^ k) * share + i, 8), height), j : j + width] = ref[
                at : at + height, :width
            ]
    copies[0].start()

    moved = momentum_decay * momentum_t[...] + mean[...]
    new_momentum_t[...] = moved
    copies[2].start()
    high, low = two_parts(mean[...] + momentum_decay * moved)
    basis_high, basis_low = two_parts(basis_t[...])
    back = dot(
        jnp.concatenate([high, low, high], axis=0),
        jnp.concatenate([basis_high, basis_high, basis_low], axis=0),
        ((0,), (0,)),
    )
    new_emb[...] = anchor[...] - outer_rate * back
    copies[1].start()
    for copy in copies:
        copy.wait()


def finish_momentum_body(part, direct, members, owned, _, momentum, *refs):
    *gradient, result, made, sem = refs
    rep, here, core = place()
    slots, pieces = momentum.shape[0], made.shape[1]
    groups = momentum.shape[1] // part // pieces
    half = pieces // 2
    live = lax.broadcasted_iota(jnp.int32, (slots, part), 0) < owned[here * 2 + core]

    def move(n, g, i):
        k, o = (i >> 1, i & 1)
        piece = 2 * (here ^ k if direct else k) + (core ^ o)
        at = column(piece * groups + (rep ^ g), part)
        return at, pltpu.make_async_copy(made.at[n, i], result.at[:, at], sem.at[n, i])

    def fill(h, i, carry):
        for n, g in enumerate(members):
            at, copy = move(n, g, i + h * half)
            rows = momentum_decay * momentum[:, at] + gradient[2 * n + h][:, column(i, part)]
            made[n, i + h * half] = jnp.where(live, rows, 0.0)
            copy.start()
        return carry

    def finish(i, carry):
        for n, g in enumerate(members):
            move(n, g, i)[1].wait()
        return carry

    short = pieces <= 16
    for h in range(2):
        lax.fori_loop(0, half, functools.partial(fill, h), 0, unroll=short)
    lax.fori_loop(0, pieces, finish, 0, unroll=short)


def over_chips(outs, direct, owner_count):
    if direct:
        return [outs[0]] + [swap(outs[k], "own", owner_count, 2 * k) for k in range(1, len(outs))]
    groups = [list(range(core, owner_count, 2)) for core in range(2)]
    return [
        lax.all_to_all(
            outs[0], "own", split_axis=0, concat_axis=0, axis_index_groups=groups, tiled=True
        )
    ]


def per_device(
    owners, inner_dense, anchor_dense, momentum_dense, inner_emb, anchor_emb, momentum_emb, basis
):
    owner_count = lax.axis_size("own")
    groups = lax.axis_size("rep")
    chips = owner_count // 2
    direct = chips <= most_direct_chips
    slot_count = momentum_dense.shape[0]
    blocks, piece_len = anchor_dense.shape
    part = piece_len // groups
    rows, rank = momentum_emb.shape
    basis_t = basis.T
    chunk = (chips, slot_count, part)
    table = (chips, 2, slot_count, part)
    message = (8 * (len(tiles(blocks, part)) + len(tiles(rank // groups, rows))), 128)
    parted = [kept(table[1:])] * chips if direct else [kept(table)]

    *parts, quarter, same, other, row_of, block_of, owned = run(
        functools.partial(start_body, groups, part),
        [kept(message)] * groups
        + [kept((blocks, part))]
        + [kept(chunk)] * 2
        + [pltpu.SMEM((n,), jnp.int32) for n in (blocks, owner_count * slot_count, owner_count)],
        [],
        far=[
            owners[:, 0],
            anchor_dense,
            inner_dense,
            momentum_dense,
            anchor_emb,
            inner_emb,
            basis_t,
        ],
        out_specs=[vmem] * (groups + 3) + [smem] * 3,
        scratch=[
            pltpu.SMEM((blocks,), jnp.int32),
            pltpu.VMEM((groups, blocks, part), f32),
            pltpu.VMEM((groups, blocks, part), f32),
            pltpu.VMEM(anchor_emb.shape, f32),
            pltpu.VMEM(anchor_emb.shape, f32),
            pltpu.VMEM(basis_t.shape, f32),
            pltpu.VMEM((rank, rows), f32),
            pltpu.SemaphoreType.DMA((2 * groups + 4,)),
            pltpu.SemaphoreType.DMA((owner_count,)),
        ],
        name="start",
    )
    parts = [parts[0]] + [swap(parts[k], "rep", groups, k) for k in range(1, groups)]

    other = swap(other, "own", owner_count, 1)
    packed = run(functools.partial(pack_body, direct), parted, [same, other], name="pack")
    momentum_rows = over_chips(packed, direct, owner_count)

    mean, shared, *sent = run(
        functools.partial(mean_body, groups, direct),
        [kept((blocks, part)), kept((8 * len(tiles(rank // groups, rows)), 128))] + parted,
        parts,
        [block_of],
        name="mean",
    )
    gradient_rows = over_chips(sent, direct, owner_count)
    (other,) = run(
        functools.partial(other_body, direct),
        [kept(chunk)],
        gradient_rows,
        name="other",
    )
    crossed = swap(other, "own", owner_count, 1)

    (dense,) = run(
        functools.partial(dense_body, direct),
        [kept(message)],
        [quarter, mean, shared, *momentum_rows],
        [row_of],
        [
            pltpu.VMEM(table if direct else (8, 128), f32),
            pltpu.VMEM((blocks, part), f32),
        ],
        name="dense",
    )
    dense = [dense] + [swap(dense, "rep", groups, k) for k in range(1, groups)]

    length = chips * part
    halves = run(
        functools.partial(join_body, direct),
        [kept((slot_count, length))] * 2,
        [*gradient_rows, crossed],
        after=gradient_rows[:0:-1],
        name="join",
    )
    again = run(
        copies_body,
        [kept((slot_count, length + 128))] * 2,
        halves,
        name="again",
    )
    (sign,) = run(
        cut_body, [kept((248, 128))], [dense[0]], after=dense[1:], name="gathered"
    )
    sign = swap(sign, "own", owner_count, 1)
    near1 = swap(halves[0], "rep", groups, 1)
    near2 = swap(halves[1], "rep", groups, 2)
    passed = run(
        copies_body,
        [kept((slot_count, length))] * 2,
        [near1, near2],
        after=[sign],
        name="pass_on",
    )
    gradient = [
        *halves,
        near1,
        swap(again[1], "rep", groups, 1),
        swap(again[0], "rep", groups, 2),
        near2,
        swap(passed[0], "rep", groups, 2),
        swap(passed[1], "rep", groups, 1),
    ]

    shapes = [anchor_dense.shape, anchor_emb.shape, (rank, rows)]
    new_dense, new_emb, new_momentum_t = run(
        functools.partial(finish_body, part),
        [stored(shape) for shape in shapes],
        [anchor_emb, momentum_emb.T, basis_t, *dense],
        out_specs=[anywhere] * 3,
        scratch=[pltpu.VMEM((rank, rows), f32), pltpu.SemaphoreType.DMA((3,))]
        + [pltpu.VMEM(shape, f32) for shape in shapes],
        name="finish",
    )
    new_momentum_dense = new_momentum_t
    for members in (tuple(range(groups - 1)), (groups - 1,)):
        (new_momentum_dense,) = pl.pallas_call(
            functools.partial(finish_momentum_body, part, direct, members),
            out_shape=[stored(momentum_dense.shape)],
            in_specs=[smem, anywhere] + [vmem] * (1 + 2 * len(members)),
            out_specs=[anywhere],
            scratch_shapes=[
                pltpu.VMEM((len(members), owner_count, slot_count, part), f32),
                pltpu.SemaphoreType.DMA((len(members), owner_count)),
            ],
            input_output_aliases={1: 0} if members[0] else {},
            compiler_params=pltpu.CompilerParams(vmem_limit_bytes=vmem_limit),
            name="finish_momentum",
        )(
            in_scalars(owned),
            new_momentum_dense,
            on_chip(momentum_dense),
            *[on_chip(gradient[2 * g + h]) for g in members for h in range(2)],
        )
    return (new_dense, new_momentum_dense, new_emb, new_momentum_t.T)


def solution(mesh):
    placed = (
        P(),
        P("rep", None, "own"),
        P(None, "own"),
        P("own", None),
        P("rep", "own", None),
        P("own", None),
        P("own", None),
        P(),
    )
    return jax.shard_map(
        per_device,
        mesh=mesh,
        in_specs=placed,
        out_specs=(P(None, "own"), P("own", None), P("own", None), P("own", None)),
        check_vma=False,
    )
```

```python
import functools

import jax
import jax.numpy as jnp
from jax import lax
from jax.experimental import pallas as pl
from jax.experimental.pallas import tpu as pltpu
from jax.sharding import PartitionSpec as P

outer_rate = 0.7
momentum_decay = 0.9
most_direct_chips = 8
f32 = jnp.float32
vmem_limit = 48 * 1024 * 1024

vmem = pl.BlockSpec(memory_space=pltpu.VMEM)
smem = pl.BlockSpec(memory_space=pltpu.SMEM)
anywhere = pl.BlockSpec(memory_space=pl.ANY)


def on_chip(x):
    return pltpu.with_memory_space_constraint(x, pltpu.VMEM)


def in_scalars(x):
    return pltpu.with_memory_space_constraint(x, pltpu.SMEM)


def in_hbm(x):
    return pltpu.with_memory_space_constraint(x, pltpu.HBM)


def kept(shape):
    return pltpu.VMEM(shape, f32)


def stored(shape):
    return jax.ShapeDtypeStruct(shape, f32)


def run(
    body, outs, operands, scalars=(), scratch=(), far=(), after=(), out_specs=None, name=None
):
    skip = len(after)

    def whole(*refs):
        body(*refs[skip:])

    return pl.pallas_call(
        whole,
        out_shape=list(outs),
        in_specs=[anywhere] * skip
        + [smem] * len(scalars)
        + [anywhere] * len(far)
        + [vmem] * len(operands),
        out_specs=out_specs or [vmem] * len(outs),
        scratch_shapes=list(scratch),
        compiler_params=pltpu.CompilerParams(vmem_limit_bytes=vmem_limit),
        name=name,
    )(
        *[on_chip(x) for x in after],
        *[in_scalars(x) for x in scalars],
        *[in_hbm(x) for x in far],
        *[on_chip(x) for x in operands],
    )


def swap(x, axis, count, mask):
    return lax.ppermute(x, axis, [(i, i ^ mask) for i in range(count)])


def place():
    position = lax.axis_index("own")
    return lax.axis_index("rep"), lax.shift_right_logical(position, 1), position & 1


def column(index, part):
    return pl.ds(pl.multiple_of(index * part, 128), part)


def tiles(rows, columns):
    return [
        (i, min(8, rows - i), j, min(128, columns - j))
        for i in range(0, rows, 8)
        for j in range(0, columns, 128)
    ]


def two_parts(x):
    high = x.astype(jnp.bfloat16)
    return high, (x - high.astype(f32)).astype(jnp.bfloat16)


def dot(a, b, contract):
    return lax.dot_general(a, b, (contract, ((), ())), preferred_element_type=f32)


def name_places(slots, owners, row_of, block_of, owned):
    blocks, owner_count = row_of.shape[0], owned.shape[0]

    def clear(i, carry):
        block_of[i] = 0
        return carry

    def clear_count(i, carry):
        owned[i] = 0
        return carry

    def name(u, carry):
        owner = owners[u]
        slot = owned[owner]
        row = owner * slots + slot
        row_of[u] = row
        block_of[row] = u
        owned[owner] = slot + 1
        return carry

    short = blocks <= 16
    lax.fori_loop(0, block_of.shape[0], clear, 0, unroll=short)
    lax.fori_loop(0, owner_count, clear_count, 0, unroll=short)
    lax.fori_loop(0, blocks, name, 0, unroll=short)


def start_body(groups, part, owners, anchor, inner, momentum, *refs):
    outs, (quarter, same, other), named, scratch = (
        refs[:groups],
        refs[groups : groups + 3],
        refs[groups + 3 : groups + 6],
        refs[groups + 6 :],
    )
    own, far, near, sem, piece_sem = scratch
    rep, chip, core = place()
    blocks = quarter.shape[0]
    chips = same.shape[0]
    listed = pltpu.make_async_copy(owners, own, sem.at[2])
    listed.start()
    dense_moves = [
        pltpu.make_async_copy(anchor, far, sem.at[0]),
        pltpu.make_async_copy(inner.at[0], near, sem.at[1]),
    ]
    for move in dense_moves:
        move.start()
    pieces = [
        pltpu.make_async_copy(
            momentum.at[:, column((2 * to + (core ^ o)) * groups + rep, part)],
            out.at[to],
            piece_sem.at[2 * to + o],
        )
        for to in range(chips)
        for o, out in enumerate((same, other))
    ]
    for piece in pieces:
        piece.start()
    listed.wait()
    name_places(same.shape[1], own, *named)
    dense_tiles = tiles(blocks, part)
    for move in dense_moves:
        move.wait()
    for k in range(groups):
        for t, (i, height, j, width) in enumerate(dense_tiles):
            columns = pl.ds(pl.multiple_of((rep ^ k) * part + j, 128), width)
            rows = slice(i, i + height)
            outs[k][8 * t : 8 * t + height, :width] = far[rows, columns] - near[rows, columns]
            if k == 0:
                quarter[rows, j : j + width] = far[rows, columns]
    for piece in pieces:
        piece.wait()


def factor_body(anchor, inner, basis_t, out):
    rank = out.shape[0]
    high, low = two_parts(anchor[...] - inner[0])
    basis_high, basis_low = two_parts(basis_t[...])
    both = dot(jnp.concatenate([basis_high, basis_low], axis=0), high, ((1,), (1,)))
    out[...] = both[:rank] + (both[rank:] + dot(basis_high, low, ((1,), (1,))))


def mean_body(groups, direct, block_of, *refs):
    parts, (mean, *outs) = refs[:groups], refs[groups:]
    _, here, core = place()
    dense_tiles = tiles(*mean.shape)
    for t, (i, height, j, width) in enumerate(dense_tiles):
        at = slice(8 * t, 8 * t + height)
        total = parts[0][at, :width]
        for ref in parts[1:]:
            total = total + ref[at, :width]
        mean[i : i + height, j : j + width] = total / groups
    slots = outs[0].shape[-2]

    def fill(k, carry):
        for o in range(2):
            owner = 2 * (here ^ k if direct else k) + (core ^ o)
            for s in range(slots):
                row = mean[pl.ds(block_of[owner * slots + s], 1), :]
                if direct:
                    outs[k][o, pl.ds(s, 1), :] = row
                else:
                    outs[0][k, o, pl.ds(s, 1), :] = row
        return carry

    if direct:
        for k in range(len(outs)):
            fill(k, 0)
    else:
        lax.fori_loop(0, outs[0].shape[0], fill, 0)


def pack_body(direct, same, other, *outs):
    _, chip, _ = place()
    if direct:
        for k, out in enumerate(outs):
            out[0] = same[chip ^ k]
            out[1] = other[chip ^ k]
    else:
        outs[0][:, 0] = same[...]
        outs[0][:, 1] = other[...]


def rows_body(direct, core, *refs):
    *received, out = refs
    chips = len(received) if direct else received[0].shape[0]
    part = received[0].shape[-1]

    def fill(k, carry):
        out[:, column(k, part)] = received[k][core] if direct else received[0][k, core]
        return carry

    if direct:
        for k in range(chips):
            fill(k, 0)
    else:
        lax.fori_loop(0, chips, fill, 0)
    spare = out.shape[1] - chips * part
    out[:, chips * part :] = jnp.zeros((out.shape[0], spare), f32)


def cut_body(ref, out):
    out[...] = ref[: out.shape[0], :]


def fold(tile, out, lane):
    for h in range(0, tile.shape[0], 4):
        out[:, lane + 32 * h : lane + 32 * h + tile.shape[1]] = tile[h : h + 4, :]


def unfold(ref, lane, height, width):
    runs = [ref[:, lane + 32 * h : lane + 32 * h + width] for h in range(0, height, 4)]
    return jnp.concatenate(runs, axis=0)


def again_body(skip, first, second, factor, received1, received2, out1, out2, pair):
    out1[:, :skip] = first[:, :skip]
    out2[:, :skip] = second[:, :skip]
    factor_tiles = tiles(*factor.shape)
    at = received2.shape[0] - 8 * len(factor_tiles)
    count = at // 16
    for t in range(count):
        fold(received1[8 * t : 8 * t + 8, :], out1, skip + 256 * t)
        fold(received2[8 * (count + t) : 8 * (count + t) + 8, :], out2, skip + 256 * t)
    skip += 256 * count
    for t, (i, height, j, width) in enumerate(factor_tiles):
        total = factor[i : i + height, j : j + width] + received2[at : at + height, :width]
        pair[i : i + height, j : j + width] = total
        fold(total, out2, skip + 256 * t)
        at += 8


def copies_body(*refs):
    count = len(refs) // 2
    for ref, out in zip(refs[:count], refs[count:]):
        out[...] = ref[:, : out.shape[1]]


def dense_body(direct, row_of, quarter, mean, factor, *refs):
    *received, plain, with_factor, rows, work = refs
    _, here, core = place()
    slots = received[0].shape[-2]
    blocks = mean.shape[0]
    if direct:
        for k, ref in enumerate(received):
            rows[k] = ref[...]
        table = rows
    else:
        table = received[0]

    def update(block, carry):
        row = row_of[block]
        owner = row // slots
        chip = (owner // 2) ^ here if direct else owner // 2
        momentum = table[chip, (owner % 2) ^ core, pl.ds(row % slots, 1), :]
        mean_row = mean[pl.ds(block, 1), :]
        new_momentum = momentum_decay * momentum + mean_row
        work[pl.ds(block, 1), :] = quarter[pl.ds(block, 1), :] - outer_rate * (
            mean_row + momentum_decay * new_momentum
        )
        return carry

    lax.fori_loop(0, blocks, update, 0, unroll=blocks <= 16)
    dense_tiles = tiles(*work.shape)
    for t, (i, height, j, width) in enumerate(dense_tiles):
        tile = work[i : i + height, j : j + width]
        plain[8 * t : 8 * t + height, :width] = tile
        with_factor[8 * t : 8 * t + height, :width] = tile
    skip = 8 * len(dense_tiles)
    plain[skip:, :] = jnp.zeros((plain.shape[0] - skip, 128), f32)
    for t, (i, height, j, width) in enumerate(tiles(*factor.shape)):
        at = slice(skip + 8 * t, skip + 8 * t + height)
        with_factor[at, :width] = factor[i : i + height, j : j + width]


class Pieces:
    def __init__(self, part, direct, members, owned, momentum, gradient, result, made, sem):
        self.part, self.direct, self.members = part, direct, members
        self.momentum, self.gradient, self.result = momentum, gradient, result
        self.made, self.sem = made, sem
        self.pieces = made.shape[1]
        self.groups = momentum.shape[1] // part // self.pieces
        self.rep, self.here, self.core = place()
        rows = lax.broadcasted_iota(jnp.int32, (momentum.shape[0], part), 0)
        self.live = rows < owned[self.here * 2 + self.core]
        self.short = self.pieces <= 16

    def move(self, n, g, i):
        half = self.pieces // 2
        k, o = i % half, i // half
        piece = 2 * (self.here ^ k if self.direct else k) + (self.core ^ o)
        at = column(piece * self.groups + (self.rep ^ g), self.part)
        target = self.result.at[:, at]
        return at, pltpu.make_async_copy(self.made.at[n, i], target, self.sem.at[n, i])

    def fill(self, h, i, carry):
        half = self.pieces // 2
        for n, g in enumerate(self.members):
            at, copy = self.move(n, g, i + h * half)
            received = self.gradient[2 * n + h][:, column(i, self.part)]
            rows = momentum_decay * self.momentum[:, at] + received
            self.made[n, i + h * half] = jnp.where(self.live, rows, 0.0)
            copy.start()
        return carry

    def wait(self, i, carry):
        for n, g in enumerate(self.members):
            self.move(n, g, i)[1].wait()
        return carry

    def make(self):
        for h in range(2):
            body = functools.partial(self.fill, h)
            lax.fori_loop(0, self.pieces // 2, body, 0, unroll=self.short)

    def finish(self):
        lax.fori_loop(0, self.pieces, self.wait, 0, unroll=self.short)


def finish_body(part, direct, groups, owned, anchor, momentum_t, basis_t, momentum, *refs):
    parts, pair, gradient = refs[: groups - 1], refs[groups - 1], refs[groups : 3 * groups - 2]
    refs = refs[3 * groups - 2 :]
    result0, result1, result2, result3, mean, sem, made, made_sem, *whole = refs
    new_dense, new_emb, new_momentum_t = whole
    copies = [
        pltpu.make_async_copy(ref, result, sem.at[i])
        for i, (ref, result) in enumerate(
            ((new_dense, result0), (new_emb, result1), (new_momentum_t, result2))
        )
    ]
    rep, _, _ = place()
    blocks, (rank, rows) = new_dense.shape[0], mean.shape
    dense_tiles = tiles(blocks, part)
    skip = gradient[3].shape[1] - 256 * len(tiles(rank, rows))
    for t, (i, height, j, width) in enumerate(tiles(rank, rows)):
        here = (slice(i, i + height), slice(j, j + width))
        mean[here] = (pair[here] + unfold(gradient[3], skip + 256 * t, height, width)) / groups
    moved = momentum_decay * momentum_t[...] + mean[...]
    new_momentum_t[...] = moved
    copies[2].start()
    high, low = two_parts(mean[...] + momentum_decay * moved)
    basis_high, basis_low = two_parts(basis_t[...])
    back = dot(
        jnp.concatenate([high, low, high], axis=0),
        jnp.concatenate([basis_high, basis_high, basis_low], axis=0),
        ((0,), (0,)),
    )
    new_emb[...] = anchor[...] - outer_rate * back
    copies[1].start()

    count = len(dense_tiles) // 2
    skip = gradient[4].shape[1] - 256 * count
    for k in range(groups):
        for t, (i, height, j, width) in enumerate(dense_tiles):
            at = pl.multiple_of((rep ^ k) * part + j, 128)
            if k < len(parts):
                tile = parts[k][8 * t : 8 * t + height, :width]
            else:
                ref = gradient[4] if t < count else gradient[3]
                tile = unfold(ref, skip + 256 * (t % count), height, width)
            new_dense[i : i + height, pl.ds(at, width)] = tile
    copies[0].start()

    members = tuple(range(groups - 1))
    pieces = Pieces(part, direct, members, owned, momentum, gradient, result3, made, made_sem)
    pieces.make()
    pieces.finish()
    for copy in copies:
        copy.wait()


def finish_momentum_body(part, direct, members, owned, _, momentum, *refs):
    *gradient, result, made, sem = refs
    pieces = Pieces(part, direct, members, owned, momentum, gradient, result, made, sem)
    pieces.make()
    pieces.finish()


def over_chips(outs, direct, owner_count):
    if direct:
        return [outs[0]] + [swap(outs[k], "own", owner_count, 2 * k) for k in range(1, len(outs))]
    groups = [list(range(core, owner_count, 2)) for core in range(2)]
    return [
        lax.all_to_all(
            outs[0], "own", split_axis=0, concat_axis=0, axis_index_groups=groups, tiled=True
        )
    ]


def per_device(
    owners, inner_dense, anchor_dense, momentum_dense, inner_emb, anchor_emb, momentum_emb, basis
):
    owner_count = lax.axis_size("own")
    groups = lax.axis_size("rep")
    chips = owner_count // 2
    direct = chips <= most_direct_chips
    slot_count = momentum_dense.shape[0]
    blocks, piece_len = anchor_dense.shape
    part = piece_len // groups
    rows, rank = momentum_emb.shape
    basis_t = basis.T
    chunk = (chips, slot_count, part)
    table = (chips, 2, slot_count, part)
    parted = [kept(table[1:])] * chips if direct else [kept(table)]

    *parts, quarter, same, other, row_of, block_of, owned = run(
        functools.partial(start_body, groups, part),
        [kept((8 * len(tiles(blocks, part)), 128))] * groups
        + [kept((blocks, part))]
        + [kept(chunk)] * 2
        + [pltpu.SMEM((n,), jnp.int32) for n in (blocks, owner_count * slot_count, owner_count)],
        [],
        far=[
            owners[:, 0],
            anchor_dense,
            inner_dense,
            momentum_dense,
        ],
        out_specs=[vmem] * (groups + 3) + [smem] * 3,
        scratch=[
            pltpu.SMEM((blocks,), jnp.int32),
            pltpu.VMEM(anchor_dense.shape, f32),
            pltpu.VMEM(anchor_dense.shape, f32),
            pltpu.SemaphoreType.DMA((3,)),
            pltpu.SemaphoreType.DMA((owner_count,)),
        ],
        name="start",
    )
    parts = [parts[0]] + [swap(parts[k], "rep", groups, k) for k in range(1, groups)]

    other = swap(other, "own", owner_count, 1)
    packed = run(functools.partial(pack_body, direct), parted, [same, other], name="pack")
    momentum_rows = over_chips(packed, direct, owner_count)

    (factor,) = run(
        factor_body, [kept((rank, rows))], [anchor_emb, inner_emb, basis_t], name="factor"
    )
    mean, *sent = run(
        functools.partial(mean_body, groups, direct),
        [kept((blocks, part))] + parted,
        parts,
        [block_of],
        after=[factor],
        name="mean",
    )
    gradient_rows = over_chips(sent, direct, owner_count)
    length = chips * part
    (other,) = run(
        functools.partial(rows_body, direct, 1),
        [kept((slot_count, length + 256))],
        gradient_rows,
        after=[gradient_rows[k] for k in (3, 2, 1)] if direct else (),
        name="other",
    )
    (mine,) = run(
        functools.partial(rows_body, direct, 0),
        [kept((slot_count, length + 512))],
        gradient_rows,
        after=[gradient_rows[k] for k in (3, 2, 1)] if direct else (),
        name="mine",
    )
    halves = [mine, swap(other, "own", owner_count, 1)]

    momentum = on_chip(momentum_dense)
    dense_rows = 8 * len(tiles(blocks, part))
    plain, with_factor = run(
        functools.partial(dense_body, direct),
        [kept((dense_rows + 16, 128)), kept((dense_rows + 8 * len(tiles(rank, rows)), 128))],
        [quarter, mean, factor, *momentum_rows],
        [row_of],
        [
            pltpu.VMEM(table if direct else (8, 128), f32),
            pltpu.VMEM((blocks, part), f32),
        ],
        after=[*momentum_rows[:0:-1], momentum],
        name="dense",
    )
    dense = [plain, swap(plain, "rep", groups, 1), swap(with_factor, "rep", groups, 2)]

    passed_on = 16 * dense_rows
    *again, pair = run(
        functools.partial(again_body, length),
        [
            kept((slot_count, length + passed_on)),
            kept((slot_count, length + passed_on + 256 * len(tiles(rank, rows)))),
            kept((rank, rows)),
        ],
        [*halves, factor, dense[1], dense[2]],
        name="again",
    )
    (sign,) = run(
        cut_body, [kept((260, 128))], [plain], after=[dense[k] for k in (2, 1)], name="gathered"
    )
    sign = swap(sign, "own", owner_count, 1)
    near1 = swap(halves[0], "rep", groups, 1)
    near2 = swap(halves[1], "rep", groups, 2)
    passed = run(
        copies_body,
        [kept((slot_count, length))] * 2,
        [near1, near2],
        after=[sign],
        name="pass_on",
    )
    gradient = [
        *halves,
        near1,
        swap(again[1], "rep", groups, 1),
        swap(again[0], "rep", groups, 2),
        near2,
        swap(passed[0], "rep", groups, 2),
        swap(passed[1], "rep", groups, 1),
    ]

    made = [
        pltpu.VMEM((n, owner_count, slot_count, part), f32) for n in (groups - 1, 1)
    ]
    made_sems = [pltpu.SemaphoreType.DMA((n, owner_count)) for n in (groups - 1, 1)]
    shapes = [anchor_dense.shape, anchor_emb.shape, (rank, rows)]
    new_dense, new_emb, new_momentum_t, first_columns = run(
        functools.partial(finish_body, part, direct, groups),
        [stored(shape) for shape in (*shapes, momentum_dense.shape)],
        [
            anchor_emb,
            momentum_emb.T,
            basis_t,
            momentum,
            *dense,
            pair,
            *gradient[: 2 * groups - 2],
        ],
        [owned],
        out_specs=[anywhere] * 4,
        scratch=[
            pltpu.VMEM((rank, rows), f32),
            pltpu.SemaphoreType.DMA((3,)),
            made[0],
            made_sems[0],
        ]
        + [pltpu.VMEM(shape, f32) for shape in shapes],
        name="finish",
    )
    (new_momentum_dense,) = pl.pallas_call(
        functools.partial(finish_momentum_body, part, direct, (groups - 1,)),
        out_shape=[stored(momentum_dense.shape)],
        in_specs=[smem, anywhere] + [vmem] * 3,
        out_specs=[anywhere],
        scratch_shapes=[made[1], made_sems[1]],
        input_output_aliases={1: 0},
        compiler_params=pltpu.CompilerParams(vmem_limit_bytes=vmem_limit),
        name="finish_momentum",
    )(
        in_scalars(owned),
        first_columns,
        on_chip(momentum),
        *[on_chip(x) for x in gradient[2 * groups - 2 :]],
    )
    return (new_dense, new_momentum_dense, new_emb, new_momentum_t.T)


def solution(mesh):
    placed = (
        P(),
        P("rep", None, "own"),
        P(None, "own"),
        P("own", None),
        P("rep", "own", None),
        P("own", None),
        P("own", None),
        P(),
    )
    return jax.shard_map(
        per_device,
        mesh=mesh,
        in_specs=placed,
        out_specs=(P(None, "own"), P("own", None), P("own", None), P("own", None)),
        check_vma=False,
    )
```

```python
import functools

import jax
import jax.numpy as jnp
from jax import lax
from jax.experimental import pallas as pl
from jax.experimental.pallas import tpu as pltpu
from jax.sharding import PartitionSpec as P

outer_rate = 0.7
momentum_decay = 0.9
most_direct_chips = 8
f32 = jnp.float32
vmem_limit = 48 * 1024 * 1024

vmem = pl.BlockSpec(memory_space=pltpu.VMEM)
smem = pl.BlockSpec(memory_space=pltpu.SMEM)
anywhere = pl.BlockSpec(memory_space=pl.ANY)


def on_chip(x):
    return pltpu.with_memory_space_constraint(x, pltpu.VMEM)


def in_scalars(x):
    return pltpu.with_memory_space_constraint(x, pltpu.SMEM)


def in_hbm(x):
    return pltpu.with_memory_space_constraint(x, pltpu.HBM)


def kept(shape):
    return pltpu.VMEM(shape, f32)


def stored(shape):
    return jax.ShapeDtypeStruct(shape, f32)


def run(
    body, outs, operands, scalars=(), scratch=(), far=(), after=(), out_specs=None, name=None
):
    skip = len(after)

    def whole(*refs):
        body(*refs[skip:])

    return pl.pallas_call(
        whole,
        out_shape=list(outs),
        in_specs=[anywhere] * skip
        + [smem] * len(scalars)
        + [anywhere] * len(far)
        + [vmem] * len(operands),
        out_specs=out_specs or [vmem] * len(outs),
        scratch_shapes=list(scratch),
        compiler_params=pltpu.CompilerParams(vmem_limit_bytes=vmem_limit),
        name=name,
    )(
        *[on_chip(x) for x in after],
        *[in_scalars(x) for x in scalars],
        *[in_hbm(x) for x in far],
        *[on_chip(x) for x in operands],
    )


def swap(x, axis, count, mask):
    return lax.ppermute(x, axis, [(i, i ^ mask) for i in range(count)])


def turn(step, core):
    return 1 + ((step + core) & 1)


def swap_in_turn(x, step):
    groups, owner_count = lax.axis_size("rep"), lax.axis_size("own")
    pairs = [
        (rep * owner_count + own, (rep ^ turn(step, own & 1)) * owner_count + own)
        for rep in range(groups)
        for own in range(owner_count)
    ]
    return lax.ppermute(x, ("rep", "own"), pairs)


def member(rep, core, k):
    return rep ^ (k if k in (0, 3) else turn(k - 1, core))


def place():
    position = lax.axis_index("own")
    return lax.axis_index("rep"), lax.shift_right_logical(position, 1), position & 1


def column(index, part):
    return pl.ds(pl.multiple_of(index * part, 128), part)


def tiles(rows, columns):
    return [
        (i, min(8, rows - i), j, min(128, columns - j))
        for i in range(0, rows, 8)
        for j in range(0, columns, 128)
    ]


def two_parts(x):
    high = x.astype(jnp.bfloat16)
    return high, (x - high.astype(f32)).astype(jnp.bfloat16)


def dot(a, b, contract):
    return lax.dot_general(a, b, (contract, ((), ())), preferred_element_type=f32)


def name_places(slots, owners, row_of, block_of, owned):
    blocks, owner_count = row_of.shape[0], owned.shape[0]

    def clear(i, carry):
        block_of[i] = 0
        return carry

    def clear_count(i, carry):
        owned[i] = 0
        return carry

    def name(u, carry):
        owner = owners[u]
        slot = owned[owner]
        row = owner * slots + slot
        row_of[u] = row
        block_of[row] = u
        owned[owner] = slot + 1
        return carry

    short = blocks <= 16
    lax.fori_loop(0, block_of.shape[0], clear, 0, unroll=short)
    lax.fori_loop(0, owner_count, clear_count, 0, unroll=short)
    lax.fori_loop(0, blocks, name, 0, unroll=short)


def start_body(groups, part, owners, anchor, inner, momentum, *refs):
    outs, (quarter, same, other), named, scratch = (
        refs[:groups],
        refs[groups : groups + 3],
        refs[groups + 3 : groups + 6],
        refs[groups + 6 :],
    )
    own, far, near, sem, piece_sem = scratch
    rep, chip, core = place()
    blocks = quarter.shape[0]
    chips = same.shape[0]
    listed = pltpu.make_async_copy(owners, own, sem.at[2])
    listed.start()
    dense_moves = [
        pltpu.make_async_copy(anchor, far, sem.at[0]),
        pltpu.make_async_copy(inner.at[0], near, sem.at[1]),
    ]
    for move in dense_moves:
        move.start()
    pieces = [
        pltpu.make_async_copy(
            momentum.at[:, column((2 * to + (core ^ o)) * groups + rep, part)],
            out.at[to],
            piece_sem.at[2 * to + o],
        )
        for to in range(chips)
        for o, out in enumerate((same, other))
    ]
    for piece in pieces:
        piece.start()
    listed.wait()
    name_places(same.shape[1], own, *named)
    dense_tiles = tiles(blocks, part)
    for move in dense_moves:
        move.wait()
    for k in range(groups):
        for t, (i, height, j, width) in enumerate(dense_tiles):
            columns = pl.ds(pl.multiple_of((rep ^ k) * part + j, 128), width)
            rows = slice(i, i + height)
            outs[k][8 * t : 8 * t + height, :width] = far[rows, columns] - near[rows, columns]
            if k == 0:
                quarter[rows, j : j + width] = far[rows, columns]
    for piece in pieces:
        piece.wait()


def factor_body(anchor, inner, basis_t, out):
    rank = out.shape[0]
    high, low = two_parts(anchor[...] - inner[0])
    basis_high, basis_low = two_parts(basis_t[...])
    both = dot(jnp.concatenate([basis_high, basis_low], axis=0), high, ((1,), (1,)))
    out[...] = both[:rank] + (both[rank:] + dot(basis_high, low, ((1,), (1,))))


def mean_body(groups, direct, block_of, *refs):
    parts, (mean, *outs) = refs[:groups], refs[groups:]
    _, here, core = place()
    dense_tiles = tiles(*mean.shape)
    for t, (i, height, j, width) in enumerate(dense_tiles):
        at = slice(8 * t, 8 * t + height)
        total = parts[0][at, :width]
        for ref in parts[1:]:
            total = total + ref[at, :width]
        mean[i : i + height, j : j + width] = total / groups
    slots = outs[0].shape[-2]

    def fill(k, carry):
        for o in range(2):
            owner = 2 * (here ^ k if direct else k) + (core ^ o)
            for s in range(slots):
                row = mean[pl.ds(block_of[owner * slots + s], 1), :]
                if direct:
                    outs[k][o, pl.ds(s, 1), :] = row
                else:
                    outs[0][k, o, pl.ds(s, 1), :] = row
        return carry

    if direct:
        for k in range(len(outs)):
            fill(k, 0)
    else:
        lax.fori_loop(0, outs[0].shape[0], fill, 0)


def pack_body(direct, same, other, *outs):
    _, chip, _ = place()
    if direct:
        for k, out in enumerate(outs):
            out[0] = same[chip ^ k]
            out[1] = other[chip ^ k]
    else:
        outs[0][:, 0] = same[...]
        outs[0][:, 1] = other[...]


def rows_body(direct, core, *refs):
    *received, out = refs
    chips = len(received) if direct else received[0].shape[0]
    part = received[0].shape[-1]

    def fill(k, carry):
        out[:, column(k, part)] = received[k][core] if direct else received[0][k, core]
        return carry

    if direct:
        for k in range(chips):
            fill(k, 0)
    else:
        lax.fori_loop(0, chips, fill, 0)
    spare = out.shape[1] - chips * part
    out[:, chips * part :] = jnp.zeros((out.shape[0], spare), f32)


def cut_body(ref, out):
    out[...] = ref[: out.shape[0], :]


def fold(tile, out, lane):
    for h in range(0, tile.shape[0], 4):
        out[:, lane + 32 * h : lane + 32 * h + tile.shape[1]] = tile[h : h + 4, :]


def unfold(ref, lane, height, width):
    runs = [ref[:, lane + 32 * h : lane + 32 * h + width] for h in range(0, height, 4)]
    return jnp.concatenate(runs, axis=0)


def again_body(skip, first, second, factor, received1, received2, out1, out2, pair):
    out1[:, :skip] = first[:, :skip]
    out2[:, :skip] = second[:, :skip]
    factor_tiles = tiles(*factor.shape)
    at = received2.shape[0] - 8 * len(factor_tiles)
    count = at // 16
    for t in range(count):
        fold(received1[8 * t : 8 * t + 8, :], out1, skip + 256 * t)
        fold(received2[8 * (count + t) : 8 * (count + t) + 8, :], out2, skip + 256 * t)
    skip += 256 * count
    for t, (i, height, j, width) in enumerate(factor_tiles):
        total = factor[i : i + height, j : j + width] + received2[at : at + height, :width]
        pair[i : i + height, j : j + width] = total
        fold(total, out2, skip + 256 * t)
        at += 8


def copies_body(*refs):
    count = len(refs) // 2
    for ref, out in zip(refs[:count], refs[count:]):
        out[...] = ref[:, : out.shape[1]]


def dense_body(direct, row_of, quarter, mean, factor, *refs):
    *received, plain, with_factor, rows, work = refs
    _, here, core = place()
    slots = received[0].shape[-2]
    blocks = mean.shape[0]
    if direct:
        for k, ref in enumerate(received):
            rows[k] = ref[...]
        table = rows
    else:
        table = received[0]

    def update(block, carry):
        row = row_of[block]
        owner = row // slots
        chip = (owner // 2) ^ here if direct else owner // 2
        momentum = table[chip, (owner % 2) ^ core, pl.ds(row % slots, 1), :]
        mean_row = mean[pl.ds(block, 1), :]
        new_momentum = momentum_decay * momentum + mean_row
        work[pl.ds(block, 1), :] = quarter[pl.ds(block, 1), :] - outer_rate * (
            mean_row + momentum_decay * new_momentum
        )
        return carry

    lax.fori_loop(0, blocks, update, 0, unroll=blocks <= 16)
    dense_tiles = tiles(*work.shape)
    for t, (i, height, j, width) in enumerate(dense_tiles):
        tile = work[i : i + height, j : j + width]
        plain[8 * t : 8 * t + height, :width] = tile
        with_factor[8 * t : 8 * t + height, :width] = tile
    skip = 8 * len(dense_tiles)
    plain[skip:, :] = jnp.zeros((plain.shape[0] - skip, 128), f32)
    for t, (i, height, j, width) in enumerate(tiles(*factor.shape)):
        at = slice(skip + 8 * t, skip + 8 * t + height)
        with_factor[at, :width] = factor[i : i + height, j : j + width]


class Pieces:
    def __init__(self, part, direct, halves, owned, momentum, gradient, result, made, sem):
        self.part, self.direct, self.halves = part, direct, halves
        self.momentum, self.gradient, self.result = momentum, gradient, result
        self.made, self.sem = made, sem
        self.chips = made.shape[1]
        self.groups = momentum.shape[1] // part // (2 * self.chips)
        self.rep, self.here, self.core = place()
        rows = lax.broadcasted_iota(jnp.int32, (momentum.shape[0], part), 0)
        self.live = rows < owned[self.here * 2 + self.core]
        self.short = self.chips <= 8

    def move(self, n, k):
        g, o = self.halves[n]
        piece = 2 * (self.here ^ k if self.direct else k) + (self.core ^ o)
        at = column(piece * self.groups + member(self.rep, self.core, g), self.part)
        target = self.result.at[:, at]
        return at, pltpu.make_async_copy(self.made.at[n, k], target, self.sem.at[n, k])

    def fill(self, k, carry):
        for n, received in enumerate(self.gradient):
            at, copy = self.move(n, k)
            rows = momentum_decay * self.momentum[:, at] + received[:, column(k, self.part)]
            self.made[n, k] = jnp.where(self.live, rows, 0.0)
            copy.start()
        return carry

    def wait(self, k, carry):
        for n in range(len(self.halves)):
            self.move(n, k)[1].wait()
        return carry

    def make(self):
        lax.fori_loop(0, self.chips, self.fill, 0, unroll=self.short)

    def finish(self):
        lax.fori_loop(0, self.chips, self.wait, 0, unroll=self.short)


def early_body(part, direct, halves, owned, momentum, *refs):
    *refs, result0, result1, made, made_sem, new_dense, sem = refs
    parts, gradient = refs[: -len(halves)], refs[-len(halves) :]
    rep, _, core = place()
    blocks = new_dense.shape[1]
    copies = []
    for k, ref in enumerate(parts):
        for t, (i, height, j, width) in enumerate(tiles(blocks, part)):
            new_dense[k, i : i + height, j : j + width] = ref[8 * t : 8 * t + height, :width]
        target = result0.at[:, column(member(rep, core, k), part)]
        copies.append(pltpu.make_async_copy(new_dense.at[k], target, sem.at[k]))
        copies[-1].start()
    pieces = Pieces(part, direct, halves, owned, momentum, gradient, result1, made, made_sem)
    pieces.make()
    pieces.finish()
    for copy in copies:
        copy.wait()


def late_body(part, direct, halves, owned, _, __, anchor, momentum_t, basis_t, momentum, *refs):
    pair, first, second, *refs = refs
    result0, result1, result2, result3, mean, sem, made, made_sem, *whole = refs
    new_dense, new_emb, new_momentum_t = whole
    rep, _, core = place()
    groups = momentum.shape[1] // part // (2 * made.shape[1])
    target = result0.at[:, column(member(rep, core, groups - 1), part)]
    copies = [
        pltpu.make_async_copy(ref, result, sem.at[i])
        for i, (ref, result) in enumerate(
            ((new_dense, target), (new_emb, result1), (new_momentum_t, result2))
        )
    ]
    rank, rows = mean.shape
    skip = second.shape[1] - 256 * len(tiles(rank, rows))
    for t, (i, height, j, width) in enumerate(tiles(rank, rows)):
        here = (slice(i, i + height), slice(j, j + width))
        mean[here] = (pair[here] + unfold(second, skip + 256 * t, height, width)) / groups
    moved = momentum_decay * momentum_t[...] + mean[...]
    new_momentum_t[...] = moved
    copies[2].start()
    high, low = two_parts(mean[...] + momentum_decay * moved)
    basis_high, basis_low = two_parts(basis_t[...])
    back = dot(
        jnp.concatenate([high, low, high], axis=0),
        jnp.concatenate([basis_high, basis_high, basis_low], axis=0),
        ((0,), (0,)),
    )
    new_emb[...] = anchor[...] - outer_rate * back
    copies[1].start()

    dense_tiles = tiles(*new_dense.shape)
    count = len(dense_tiles) // 2
    skip = first.shape[1] - 256 * count
    for t, (i, height, j, width) in enumerate(dense_tiles):
        ref = first if t < count else second
        tile = unfold(ref, skip + 256 * (t % count), height, width)
        new_dense[i : i + height, j : j + width] = tile
    copies[0].start()
    gradient = (second, first)
    pieces = Pieces(part, direct, halves, owned, momentum, gradient, result3, made, made_sem)
    pieces.make()
    pieces.finish()
    for copy in copies:
        copy.wait()


def last_body(part, direct, halves, owned, _, momentum, *refs):
    *gradient, result, made, sem = refs
    pieces = Pieces(part, direct, halves, owned, momentum, gradient, result, made, sem)
    pieces.make()
    pieces.finish()


def over_chips(outs, direct, owner_count):
    if direct:
        return [outs[0]] + [swap(outs[k], "own", owner_count, 2 * k) for k in range(1, len(outs))]
    groups = [list(range(core, owner_count, 2)) for core in range(2)]
    return [
        lax.all_to_all(
            outs[0], "own", split_axis=0, concat_axis=0, axis_index_groups=groups, tiled=True
        )
    ]


def per_device(
    owners, inner_dense, anchor_dense, momentum_dense, inner_emb, anchor_emb, momentum_emb, basis
):
    owner_count = lax.axis_size("own")
    groups = lax.axis_size("rep")
    chips = owner_count // 2
    direct = chips <= most_direct_chips
    slot_count = momentum_dense.shape[0]
    blocks, piece_len = anchor_dense.shape
    part = piece_len // groups
    rows, rank = momentum_emb.shape
    basis_t = basis.T
    chunk = (chips, slot_count, part)
    table = (chips, 2, slot_count, part)
    parted = [kept(table[1:])] * chips if direct else [kept(table)]

    *parts, quarter, same, other, row_of, block_of, owned = run(
        functools.partial(start_body, groups, part),
        [kept((8 * len(tiles(blocks, part)), 128))] * groups
        + [kept((blocks, part))]
        + [kept(chunk)] * 2
        + [pltpu.SMEM((n,), jnp.int32) for n in (blocks, owner_count * slot_count, owner_count)],
        [],
        far=[
            owners[:, 0],
            anchor_dense,
            inner_dense,
            momentum_dense,
        ],
        out_specs=[vmem] * (groups + 3) + [smem] * 3,
        scratch=[
            pltpu.SMEM((blocks,), jnp.int32),
            pltpu.VMEM(anchor_dense.shape, f32),
            pltpu.VMEM(anchor_dense.shape, f32),
            pltpu.SemaphoreType.DMA((3,)),
            pltpu.SemaphoreType.DMA((owner_count,)),
        ],
        name="start",
    )
    parts = [parts[0]] + [swap(parts[k], "rep", groups, k) for k in range(1, groups)]

    other = swap(other, "own", owner_count, 1)
    packed = run(functools.partial(pack_body, direct), parted, [same, other], name="pack")
    momentum_rows = over_chips(packed, direct, owner_count)

    (factor,) = run(
        factor_body, [kept((rank, rows))], [anchor_emb, inner_emb, basis_t], name="factor"
    )
    mean, *sent = run(
        functools.partial(mean_body, groups, direct),
        [kept((blocks, part))] + parted,
        parts,
        [block_of],
        after=[factor],
        name="mean",
    )
    gradient_rows = over_chips(sent, direct, owner_count)
    length = chips * part
    (other,) = run(
        functools.partial(rows_body, direct, 1),
        [kept((slot_count, length + 256))],
        gradient_rows,
        after=[gradient_rows[k] for k in (3, 2, 1)] if direct else (),
        name="other",
    )
    (mine,) = run(
        functools.partial(rows_body, direct, 0),
        [kept((slot_count, length + 512))],
        gradient_rows,
        after=[gradient_rows[k] for k in (3, 2, 1)] if direct else (),
        name="mine",
    )
    halves = [mine, swap(other, "own", owner_count, 1)]

    momentum = on_chip(momentum_dense)
    dense_rows = 8 * len(tiles(blocks, part))
    plain, with_factor = run(
        functools.partial(dense_body, direct),
        [kept((dense_rows + 16, 128)), kept((dense_rows + 8 * len(tiles(rank, rows)), 128))],
        [quarter, mean, factor, *momentum_rows],
        [row_of],
        [
            pltpu.VMEM(table if direct else (8, 128), f32),
            pltpu.VMEM((blocks, part), f32),
        ],
        after=[*momentum_rows[:0:-1], momentum],
        name="dense",
    )
    dense = [plain, swap_in_turn(plain, 0), swap_in_turn(with_factor, 1)]

    passed_on = 16 * dense_rows
    *again, pair = run(
        functools.partial(again_body, length),
        [
            kept((slot_count, length + passed_on)),
            kept((slot_count, length + passed_on + 256 * len(tiles(rank, rows)))),
            kept((rank, rows)),
        ],
        [*halves, factor, dense[1], dense[2]],
        name="again",
    )
    (sign,) = run(
        cut_body, [kept((260, 128))], [plain], after=[dense[k] for k in (2, 1)], name="gathered"
    )
    sign = swap(sign, "own", owner_count, 1)
    near1 = swap_in_turn(halves[0], 0)
    near2 = swap_in_turn(halves[1], 1)
    passed = run(
        copies_body,
        [kept((slot_count, length))] * 2,
        [near1, near2],
        after=[sign],
        name="pass_on",
    )
    gradient = [
        *halves,
        near1,
        swap_in_turn(again[1], 0),
        swap_in_turn(again[0], 1),
        near2,
        swap_in_turn(passed[0], 1),
        swap_in_turn(passed[1], 0),
    ]

    own_rows, own_crossed, near1, late2, late1, near2, last1, last2 = gradient

    def finishing(body, halves, outs, operands, aliased=(), scratch=(), name=None):
        made = (len(halves), chips, slot_count, part)
        return pl.pallas_call(
            functools.partial(body, part, direct, halves),
            out_shape=[stored(shape) for shape in outs],
            in_specs=[smem] + [anywhere] * len(aliased) + [vmem] * len(operands),
            out_specs=[anywhere] * len(outs),
            scratch_shapes=[
                *scratch[:2],
                pltpu.VMEM(made, f32),
                pltpu.SemaphoreType.DMA(made[:2]),
                *scratch[2:],
            ],
            input_output_aliases={1 + i: out for i, (_, out) in enumerate(aliased)},
            compiler_params=pltpu.CompilerParams(vmem_limit_bytes=vmem_limit),
            name=name,
        )(in_scalars(owned), *[x for x, _ in aliased], *[on_chip(x) for x in operands])

    held = momentum_dense.shape
    new_dense, new_momentum_dense = pl.pallas_call(
        functools.partial(early_body, part, direct, ((0, 0), (0, 1), (1, 0), (2, 1))),
        out_shape=[stored(anchor_dense.shape), stored(held)],
        in_specs=[smem] + [vmem] * (5 + len(dense)),
        out_specs=[anywhere] * 2,
        scratch_shapes=[
            pltpu.VMEM((4, chips, slot_count, part), f32),
            pltpu.SemaphoreType.DMA((4, chips)),
            pltpu.VMEM((groups - 1, blocks, part), f32),
            pltpu.SemaphoreType.DMA((groups - 1,)),
        ],
        compiler_params=pltpu.CompilerParams(vmem_limit_bytes=vmem_limit),
        name="early",
    )(
        in_scalars(owned),
        *[on_chip(x) for x in (momentum, *dense, own_rows, own_crossed, near1, near2)],
    )
    new_dense, new_emb, new_momentum_t, new_momentum_dense = finishing(
        late_body,
        ((1, 1), (2, 0)),
        [anchor_dense.shape, anchor_emb.shape, (rank, rows), held],
        [anchor_emb, momentum_emb.T, basis_t, momentum, pair, late1, late2],
        aliased=[(new_dense, 0), (new_momentum_dense, 3)],
        scratch=[
            pltpu.VMEM((rank, rows), f32),
            pltpu.SemaphoreType.DMA((3,)),
            pltpu.VMEM((blocks, part), f32),
            pltpu.VMEM(anchor_emb.shape, f32),
            pltpu.VMEM((rank, rows), f32),
        ],
        name="late",
    )
    (new_momentum_dense,) = finishing(
        last_body,
        ((3, 0), (3, 1)),
        [held],
        [momentum, last1, last2],
        aliased=[(new_momentum_dense, 0)],
        name="last",
    )
    return (new_dense, new_momentum_dense, new_emb, new_momentum_t.T)


def solution(mesh):
    placed = (
        P(),
        P("rep", None, "own"),
        P(None, "own"),
        P("own", None),
        P("rep", "own", None),
        P("own", None),
        P("own", None),
        P(),
    )
    return jax.shard_map(
        per_device,
        mesh=mesh,
        in_specs=placed,
        out_specs=(P(None, "own"), P("own", None), P("own", None), P("own", None)),
        check_vma=False,
    )
```

```python
import functools

import jax
import jax.numpy as jnp
from jax import lax
from jax.experimental import pallas as pl
from jax.experimental.pallas import tpu as pltpu
from jax.sharding import PartitionSpec as P

outer_rate = 0.7
momentum_decay = 0.9
most_direct_chips = 8
f32 = jnp.float32
vmem_limit = 48 * 1024 * 1024

vmem = pl.BlockSpec(memory_space=pltpu.VMEM)
smem = pl.BlockSpec(memory_space=pltpu.SMEM)
anywhere = pl.BlockSpec(memory_space=pl.ANY)


def on_chip(x):
    return pltpu.with_memory_space_constraint(x, pltpu.VMEM)


def in_scalars(x):
    return pltpu.with_memory_space_constraint(x, pltpu.SMEM)


def in_hbm(x):
    return pltpu.with_memory_space_constraint(x, pltpu.HBM)


def kept(shape):
    return pltpu.VMEM(shape, f32)


def stored(shape):
    return jax.ShapeDtypeStruct(shape, f32)


def run(
    body, outs, operands, scalars=(), scratch=(), far=(), after=(), out_specs=None, name=None
):
    skip = len(after)

    def whole(*refs):
        body(*refs[skip:])

    return pl.pallas_call(
        whole,
        out_shape=list(outs),
        in_specs=[anywhere] * skip
        + [smem] * len(scalars)
        + [anywhere] * len(far)
        + [vmem] * len(operands),
        out_specs=out_specs or [vmem] * len(outs),
        scratch_shapes=list(scratch),
        compiler_params=pltpu.CompilerParams(vmem_limit_bytes=vmem_limit),
        name=name,
    )(
        *[on_chip(x) for x in after],
        *[in_scalars(x) for x in scalars],
        *[in_hbm(x) for x in far],
        *[on_chip(x) for x in operands],
    )


def swap(x, axis, count, mask):
    return lax.ppermute(x, axis, [(i, i ^ mask) for i in range(count)])


def turn(step, core):
    return 1 + ((step + core) & 1)


def swap_in_turn(x, step):
    groups, owner_count = lax.axis_size("rep"), lax.axis_size("own")
    pairs = [
        (rep * owner_count + own, (rep ^ turn(step, own & 1)) * owner_count + own)
        for rep in range(groups)
        for own in range(owner_count)
    ]
    return lax.ppermute(x, ("rep", "own"), pairs)


def member(rep, core, k):
    return rep ^ (k if k in (0, 3) else turn(k - 1, core))


def place():
    position = lax.axis_index("own")
    return lax.axis_index("rep"), lax.shift_right_logical(position, 1), position & 1


def column(index, part):
    return pl.ds(pl.multiple_of(index * part, 128), part)


def tiles(rows, columns):
    return [
        (i, min(8, rows - i), j, min(128, columns - j))
        for i in range(0, rows, 8)
        for j in range(0, columns, 128)
    ]


def two_parts(x):
    high = x.astype(jnp.bfloat16)
    return high, (x - high.astype(f32)).astype(jnp.bfloat16)


def dot(a, b, contract):
    return lax.dot_general(a, b, (contract, ((), ())), preferred_element_type=f32)


def name_places(slots, owners, row_of, block_of, owned):
    blocks, owner_count = row_of.shape[0], owned.shape[0]

    def clear(i, carry):
        block_of[i] = 0
        return carry

    def clear_count(i, carry):
        owned[i] = 0
        return carry

    def name(u, carry):
        owner = owners[u]
        slot = owned[owner]
        row = owner * slots + slot
        row_of[u] = row
        block_of[row] = u
        owned[owner] = slot + 1
        return carry

    short = blocks <= 16
    lax.fori_loop(0, block_of.shape[0], clear, 0, unroll=short)
    lax.fori_loop(0, owner_count, clear_count, 0, unroll=short)
    lax.fori_loop(0, blocks, name, 0, unroll=short)


def start_body(groups, part, owners, anchor, inner, momentum, *refs):
    outs, (quarter, same, other), named, scratch = (
        refs[:groups],
        refs[groups : groups + 3],
        refs[groups + 3 : groups + 6],
        refs[groups + 6 :],
    )
    own, far, near, sem, piece_sem = scratch
    rep, chip, core = place()
    blocks = quarter.shape[0]
    chips = same.shape[0]
    listed = pltpu.make_async_copy(owners, own, sem.at[2])
    listed.start()
    dense_moves = [
        pltpu.make_async_copy(anchor, far, sem.at[0]),
        pltpu.make_async_copy(inner.at[0], near, sem.at[1]),
    ]
    for move in dense_moves:
        move.start()
    pieces = [
        pltpu.make_async_copy(
            momentum.at[:, column((2 * to + (core ^ o)) * groups + rep, part)],
            out.at[to],
            piece_sem.at[2 * to + o],
        )
        for to in range(chips)
        for o, out in enumerate((same, other))
    ]
    for piece in pieces:
        piece.start()
    listed.wait()
    name_places(same.shape[1], own, *named)
    dense_tiles = tiles(blocks, part)
    for move in dense_moves:
        move.wait()
    for k in range(groups):
        for t, (i, height, j, width) in enumerate(dense_tiles):
            columns = pl.ds(pl.multiple_of((rep ^ k) * part + j, 128), width)
            rows = slice(i, i + height)
            outs[k][8 * t : 8 * t + height, :width] = far[rows, columns] - near[rows, columns]
            if k == 0:
                quarter[rows, j : j + width] = far[rows, columns]
    for piece in pieces:
        piece.wait()


def factor_body(anchor, inner, basis_t, out):
    rank = out.shape[0]
    high, low = two_parts(anchor[...] - inner[0])
    basis_high, basis_low = two_parts(basis_t[...])
    both = dot(jnp.concatenate([basis_high, basis_low], axis=0), high, ((1,), (1,)))
    out[...] = both[:rank] + (both[rank:] + dot(basis_high, low, ((1,), (1,))))


def mean_body(groups, direct, block_of, *refs):
    parts, (mean, *outs) = refs[:groups], refs[groups:]
    _, here, core = place()
    dense_tiles = tiles(*mean.shape)
    for t, (i, height, j, width) in enumerate(dense_tiles):
        at = slice(8 * t, 8 * t + height)
        total = parts[0][at, :width]
        for ref in parts[1:]:
            total = total + ref[at, :width]
        mean[i : i + height, j : j + width] = total / groups
    slots = outs[0].shape[-2]

    def fill(k, carry):
        for o in range(2):
            owner = 2 * (here ^ k if direct else k) + (core ^ o)
            for s in range(slots):
                row = mean[pl.ds(block_of[owner * slots + s], 1), :]
                if direct:
                    outs[k][o, pl.ds(s, 1), :] = row
                else:
                    outs[0][k, o, pl.ds(s, 1), :] = row
        return carry

    if direct:
        for k in range(len(outs)):
            fill(k, 0)
    else:
        lax.fori_loop(0, outs[0].shape[0], fill, 0)


def pack_body(direct, same, other, *outs):
    _, chip, _ = place()
    if direct:
        for k, out in enumerate(outs):
            out[0] = same[chip ^ k]
            out[1] = other[chip ^ k]
    else:
        outs[0][:, 0] = same[...]
        outs[0][:, 1] = other[...]


def rows_body(direct, core, *refs):
    *received, out = refs
    chips = len(received) if direct else received[0].shape[0]
    part = received[0].shape[-1]

    def fill(k, carry):
        out[:, column(k, part)] = received[k][core] if direct else received[0][k, core]
        return carry

    if direct:
        for k in range(chips):
            fill(k, 0)
    else:
        lax.fori_loop(0, chips, fill, 0)
    spare = out.shape[1] - chips * part
    out[:, chips * part :] = jnp.zeros((out.shape[0], spare), f32)


def cut_body(ref, out):
    out[...] = ref[: out.shape[0], :]


def fold(tile, out, lane):
    for h in range(0, tile.shape[0], 4):
        out[:, lane + 32 * h : lane + 32 * h + tile.shape[1]] = tile[h : h + 4, :]


def unfold(ref, lane, height, width):
    runs = [ref[:, lane + 32 * h : lane + 32 * h + width] for h in range(0, height, 4)]
    return jnp.concatenate(runs, axis=0)


def again_body(skip, first, second, factor, received1, received2, out1, out2, pair):
    out1[:, :skip] = first[:, :skip]
    out2[:, :skip] = second[:, :skip]
    factor_tiles = tiles(*factor.shape)
    at = received2.shape[0] - 8 * len(factor_tiles)
    count = at // 16
    for t in range(count):
        fold(received1[8 * t : 8 * t + 8, :], out1, skip + 256 * t)
        fold(received2[8 * (count + t) : 8 * (count + t) + 8, :], out2, skip + 256 * t)
    skip += 256 * count
    for t, (i, height, j, width) in enumerate(factor_tiles):
        total = factor[i : i + height, j : j + width] + received2[at : at + height, :width]
        pair[i : i + height, j : j + width] = total
        fold(total, out2, skip + 256 * t)
        at += 8


def copies_body(*refs):
    count = len(refs) // 2
    for ref, out in zip(refs[:count], refs[count:]):
        out[...] = ref[:, : out.shape[1]]


def dense_body(direct, row_of, quarter, mean, factor, *refs):
    *received, plain, with_factor, rows, work = refs
    _, here, core = place()
    slots = received[0].shape[-2]
    blocks = mean.shape[0]
    if direct:
        for k, ref in enumerate(received):
            rows[k] = ref[...]
        table = rows
    else:
        table = received[0]

    def update(block, carry):
        row = row_of[block]
        owner = row // slots
        chip = (owner // 2) ^ here if direct else owner // 2
        momentum = table[chip, (owner % 2) ^ core, pl.ds(row % slots, 1), :]
        mean_row = mean[pl.ds(block, 1), :]
        new_momentum = momentum_decay * momentum + mean_row
        work[pl.ds(block, 1), :] = quarter[pl.ds(block, 1), :] - outer_rate * (
            mean_row + momentum_decay * new_momentum
        )
        return carry

    lax.fori_loop(0, blocks, update, 0, unroll=blocks <= 16)
    dense_tiles = tiles(*work.shape)
    for t, (i, height, j, width) in enumerate(dense_tiles):
        tile = work[i : i + height, j : j + width]
        plain[8 * t : 8 * t + height, :width] = tile
        with_factor[8 * t : 8 * t + height, :width] = tile
    skip = 8 * len(dense_tiles)
    plain[skip:, :] = jnp.zeros((plain.shape[0] - skip, 128), f32)
    for t, (i, height, j, width) in enumerate(tiles(*factor.shape)):
        at = slice(skip + 8 * t, skip + 8 * t + height)
        with_factor[at, :width] = factor[i : i + height, j : j + width]


class Pieces:
    def __init__(self, part, direct, halves, owned, momentum, gradient, result, made, sem):
        self.part, self.direct, self.halves = part, direct, halves
        self.momentum, self.gradient, self.result = momentum, gradient, result
        self.made, self.sem = made, sem
        self.chips = made.shape[1]
        self.groups = momentum.shape[1] // part // (2 * self.chips)
        self.rep, self.here, self.core = place()
        rows = lax.broadcasted_iota(jnp.int32, (momentum.shape[0], part), 0)
        self.live = rows < owned[self.here * 2 + self.core]
        self.short = self.chips <= 8

    def move(self, n, k):
        g, o = self.halves[n]
        piece = 2 * (self.here ^ k if self.direct else k) + (self.core ^ o)
        at = column(piece * self.groups + member(self.rep, self.core, g), self.part)
        target = self.result.at[:, at]
        return at, pltpu.make_async_copy(self.made.at[n, k], target, self.sem.at[n, k])

    def fill(self, k, carry):
        for n, received in enumerate(self.gradient):
            at, copy = self.move(n, k)
            rows = momentum_decay * self.momentum[:, at] + received[:, column(k, self.part)]
            self.made[n, k] = jnp.where(self.live, rows, 0.0)
            copy.start()
        return carry

    def wait(self, k, carry):
        for n in range(len(self.halves)):
            self.move(n, k)[1].wait()
        return carry

    def make(self):
        lax.fori_loop(0, self.chips, self.fill, 0, unroll=self.short)

    def finish(self):
        lax.fori_loop(0, self.chips, self.wait, 0, unroll=self.short)


def early_body(part, direct, halves, owned, momentum, *refs):
    *refs, result0, result1, made, made_sem, new_dense, sem = refs
    parts, gradient = refs[: -len(halves)], refs[-len(halves) :]
    rep, _, core = place()
    blocks = new_dense.shape[1]
    copies = []
    for k, ref in enumerate(parts):
        for t, (i, height, j, width) in enumerate(tiles(blocks, part)):
            new_dense[k, i : i + height, j : j + width] = ref[8 * t : 8 * t + height, :width]
        target = result0.at[:, column(member(rep, core, k), part)]
        copies.append(pltpu.make_async_copy(new_dense.at[k], target, sem.at[k]))
        copies[-1].start()
    pieces = Pieces(part, direct, halves, owned, momentum, gradient, result1, made, made_sem)
    pieces.make()
    pieces.finish()
    for copy in copies:
        copy.wait()


def late_body(part, direct, halves, owned, _, __, anchor, momentum_t, basis_t, momentum, *refs):
    pair, first, second, *refs = refs
    result0, result1, result2, result3, mean, sem, made, made_sem, *whole = refs
    new_dense, new_emb, new_momentum_t = whole
    rep, _, core = place()
    groups = momentum.shape[1] // part // (2 * made.shape[1])
    target = result0.at[:, column(member(rep, core, groups - 1), part)]
    copies = [
        pltpu.make_async_copy(ref, result, sem.at[i])
        for i, (ref, result) in enumerate(
            ((new_dense, target), (new_emb, result1), (new_momentum_t, result2))
        )
    ]
    rank, rows = mean.shape
    skip = second.shape[1] - 256 * len(tiles(rank, rows))
    for t, (i, height, j, width) in enumerate(tiles(rank, rows)):
        here = (slice(i, i + height), slice(j, j + width))
        mean[here] = (pair[here] + unfold(second, skip + 256 * t, height, width)) / groups
    moved = momentum_decay * momentum_t[...] + mean[...]
    new_momentum_t[...] = moved
    copies[2].start()
    high, low = two_parts(mean[...] + momentum_decay * moved)
    basis_high, basis_low = two_parts(basis_t[...])
    back = dot(
        jnp.concatenate([high, low, high], axis=0),
        jnp.concatenate([basis_high, basis_high, basis_low], axis=0),
        ((0,), (0,)),
    )
    new_emb[...] = anchor[...] - outer_rate * back
    copies[1].start()

    dense_tiles = tiles(*new_dense.shape)
    count = len(dense_tiles) // 2
    skip = first.shape[1] - 256 * count
    for t, (i, height, j, width) in enumerate(dense_tiles):
        ref = first if t < count else second
        tile = unfold(ref, skip + 256 * (t % count), height, width)
        new_dense[i : i + height, j : j + width] = tile
    copies[0].start()
    gradient = (second, first)
    pieces = Pieces(part, direct, halves, owned, momentum, gradient, result3, made, made_sem)
    pieces.make()
    pieces.finish()
    for copy in copies:
        copy.wait()


def last_body(part, direct, halves, owned, _, momentum, *refs):
    *gradient, result, made, sem = refs
    pieces = Pieces(part, direct, halves, owned, momentum, gradient, result, made, sem)
    pieces.make()
    pieces.finish()


def over_chips(outs, direct, owner_count):
    if direct:
        return [outs[0]] + [swap(outs[k], "own", owner_count, 2 * k) for k in range(1, len(outs))]
    groups = [list(range(core, owner_count, 2)) for core in range(2)]
    return [
        lax.all_to_all(
            outs[0], "own", split_axis=0, concat_axis=0, axis_index_groups=groups, tiled=True
        )
    ]


def per_device(
    owners, inner_dense, anchor_dense, momentum_dense, inner_emb, anchor_emb, momentum_emb, basis
):
    owner_count = lax.axis_size("own")
    groups = lax.axis_size("rep")
    chips = owner_count // 2
    direct = chips <= most_direct_chips
    slot_count = momentum_dense.shape[0]
    blocks, piece_len = anchor_dense.shape
    part = piece_len // groups
    rows, rank = momentum_emb.shape
    basis_t = basis.T
    chunk = (chips, slot_count, part)
    table = (chips, 2, slot_count, part)
    parted = [kept(table[1:])] * chips if direct else [kept(table)]

    *parts, quarter, same, other, row_of, block_of, owned = run(
        functools.partial(start_body, groups, part),
        [kept((8 * len(tiles(blocks, part)), 128))] * groups
        + [kept((blocks, part))]
        + [kept(chunk)] * 2
        + [pltpu.SMEM((n,), jnp.int32) for n in (blocks, owner_count * slot_count, owner_count)],
        [],
        far=[
            owners[:, 0],
            anchor_dense,
            inner_dense,
            momentum_dense,
        ],
        out_specs=[vmem] * (groups + 3) + [smem] * 3,
        scratch=[
            pltpu.SMEM((blocks,), jnp.int32),
            pltpu.VMEM(anchor_dense.shape, f32),
            pltpu.VMEM(anchor_dense.shape, f32),
            pltpu.SemaphoreType.DMA((3,)),
            pltpu.SemaphoreType.DMA((owner_count,)),
        ],
        name="start",
    )
    parts = [parts[0]] + [swap(parts[k], "rep", groups, k) for k in range(1, groups)]

    other = swap(other, "own", owner_count, 1)
    packed = run(functools.partial(pack_body, direct), parted, [same, other], name="pack")
    momentum_rows = over_chips(packed, direct, owner_count)

    (factor,) = run(
        factor_body, [kept((rank, rows))], [anchor_emb, inner_emb, basis_t], name="factor"
    )
    mean, *sent = run(
        functools.partial(mean_body, groups, direct),
        [kept((blocks, part))] + parted,
        parts,
        [block_of],
        after=[factor],
        name="mean",
    )
    gradient_rows = over_chips(sent, direct, owner_count)
    length = chips * part
    (other,) = run(
        functools.partial(rows_body, direct, 1),
        [kept((slot_count, length + 256))],
        gradient_rows,
        after=[gradient_rows[k] for k in (3, 2, 1)] if direct else (),
        name="other",
    )
    (mine,) = run(
        functools.partial(rows_body, direct, 0),
        [kept((slot_count, length + 512))],
        gradient_rows,
        after=[gradient_rows[k] for k in (3, 2, 1)] if direct else (),
        name="mine",
    )
    halves = [mine, swap(other, "own", owner_count, 1)]

    momentum = on_chip(momentum_dense)
    dense_rows = 8 * len(tiles(blocks, part))
    plain, with_factor = run(
        functools.partial(dense_body, direct),
        [kept((dense_rows + 16, 128)), kept((dense_rows + 8 * len(tiles(rank, rows)), 128))],
        [quarter, mean, factor, *momentum_rows],
        [row_of],
        [
            pltpu.VMEM(table if direct else (8, 128), f32),
            pltpu.VMEM((blocks, part), f32),
        ],
        after=[*momentum_rows[:0:-1], momentum],
        name="dense",
    )
    dense = [plain, swap_in_turn(plain, 0), swap_in_turn(with_factor, 1)]

    passed_on = 16 * dense_rows
    *again, pair = run(
        functools.partial(again_body, length),
        [
            kept((slot_count, length + passed_on)),
            kept((slot_count, length + passed_on + 256 * len(tiles(rank, rows)))),
            kept((rank, rows)),
        ],
        [*halves, factor, dense[1], dense[2]],
        name="again",
    )
    (sign,) = run(
        cut_body, [kept((dense_rows + 4, 128))], [plain], after=dense[1:], name="gathered"
    )
    sign = swap(sign, "own", owner_count, 1)
    near1 = swap_in_turn(halves[0], 0)
    near2 = swap_in_turn(halves[1], 1)
    passed = run(
        copies_body,
        [kept((slot_count, length))] * 2,
        [near1, near2],
        after=[sign],
        name="pass_on",
    )
    late2, late1 = swap_in_turn(again[1], 0), swap_in_turn(again[0], 1)
    last1, last2 = swap_in_turn(passed[0], 1), swap_in_turn(passed[1], 0)

    def finishing(body, halves, outs, operands, aliased=(), before=(), after=(), name=None):
        made = (len(halves), chips, slot_count, part)
        return pl.pallas_call(
            functools.partial(body, part, direct, halves),
            out_shape=[stored(shape) for shape in outs],
            in_specs=[smem] + [anywhere] * len(aliased) + [vmem] * len(operands),
            out_specs=[anywhere] * len(outs),
            scratch_shapes=[
                *before,
                pltpu.VMEM(made, f32),
                pltpu.SemaphoreType.DMA(made[:2]),
                *after,
            ],
            input_output_aliases={1 + i: out for i, (_, out) in enumerate(aliased)},
            compiler_params=pltpu.CompilerParams(vmem_limit_bytes=vmem_limit),
            name=name,
        )(in_scalars(owned), *[x for x, _ in aliased], *[on_chip(x) for x in operands])

    held = momentum_dense.shape
    new_dense, new_momentum_dense = finishing(
        early_body,
        ((0, 0), (0, 1), (1, 0), (2, 1)),
        [anchor_dense.shape, held],
        [momentum, *dense, *halves, near1, near2],
        after=[
            pltpu.VMEM((groups - 1, blocks, part), f32),
            pltpu.SemaphoreType.DMA((groups - 1,)),
        ],
        name="early",
    )
    new_dense, new_emb, new_momentum_t, new_momentum_dense = finishing(
        late_body,
        ((1, 1), (2, 0)),
        [anchor_dense.shape, anchor_emb.shape, (rank, rows), held],
        [anchor_emb, momentum_emb.T, basis_t, momentum, pair, late1, late2],
        aliased=[(new_dense, 0), (new_momentum_dense, 3)],
        before=[pltpu.VMEM((rank, rows), f32), pltpu.SemaphoreType.DMA((3,))],
        after=[
            pltpu.VMEM((blocks, part), f32),
            pltpu.VMEM(anchor_emb.shape, f32),
            pltpu.VMEM((rank, rows), f32),
        ],
        name="late",
    )
    (new_momentum_dense,) = finishing(
        last_body,
        ((3, 0), (3, 1)),
        [held],
        [momentum, last1, last2],
        aliased=[(new_momentum_dense, 0)],
        name="last",
    )
    return (new_dense, new_momentum_dense, new_emb, new_momentum_t.T)


def solution(mesh):
    placed = (
        P(),
        P("rep", None, "own"),
        P(None, "own"),
        P("own", None),
        P("rep", "own", None),
        P("own", None),
        P("own", None),
        P(),
    )
    return jax.shard_map(
        per_device,
        mesh=mesh,
        in_specs=placed,
        out_specs=(P(None, "own"), P("own", None), P("own", None), P("own", None)),
        check_vma=False,
    )
```

```python
import functools

import jax
import jax.numpy as jnp
from jax import lax
from jax.experimental import pallas as pl
from jax.experimental.pallas import tpu as pltpu
from jax.sharding import PartitionSpec as P

outer_rate = 0.7
momentum_decay = 0.9
most_direct_chips = 8
f32 = jnp.float32
vmem_limit = 48 * 1024 * 1024

vmem = pl.BlockSpec(memory_space=pltpu.VMEM)
smem = pl.BlockSpec(memory_space=pltpu.SMEM)
anywhere = pl.BlockSpec(memory_space=pl.ANY)


def on_chip(x):
    return pltpu.with_memory_space_constraint(x, pltpu.VMEM)


def in_scalars(x):
    return pltpu.with_memory_space_constraint(x, pltpu.SMEM)


def in_hbm(x):
    return pltpu.with_memory_space_constraint(x, pltpu.HBM)


def kept(shape):
    return pltpu.VMEM(shape, f32)


def stored(shape):
    return jax.ShapeDtypeStruct(shape, f32)


def run(
    body, outs, operands, scalars=(), scratch=(), far=(), after=(), out_specs=None, name=None
):
    skip = len(after)

    def whole(*refs):
        body(*refs[skip:])

    return pl.pallas_call(
        whole,
        out_shape=list(outs),
        in_specs=[anywhere] * skip
        + [smem] * len(scalars)
        + [anywhere] * len(far)
        + [vmem] * len(operands),
        out_specs=out_specs or [vmem] * len(outs),
        scratch_shapes=list(scratch),
        compiler_params=pltpu.CompilerParams(vmem_limit_bytes=vmem_limit),
        name=name,
    )(
        *[on_chip(x) for x in after],
        *[in_scalars(x) for x in scalars],
        *[in_hbm(x) for x in far],
        *[on_chip(x) for x in operands],
    )


def swap(x, axis, count, mask):
    return lax.ppermute(x, axis, [(i, i ^ mask) for i in range(count)])


def turn(step, core):
    return 1 + ((step + core) & 1)


def swap_in_turn(x, step):
    groups, owner_count = lax.axis_size("rep"), lax.axis_size("own")
    pairs = [
        (rep * owner_count + own, (rep ^ turn(step, own & 1)) * owner_count + own)
        for rep in range(groups)
        for own in range(owner_count)
    ]
    return lax.ppermute(x, ("rep", "own"), pairs)


def member(rep, core, k):
    return rep ^ (k if k in (0, 3) else turn(k - 1, core))


def place():
    position = lax.axis_index("own")
    return lax.axis_index("rep"), lax.shift_right_logical(position, 1), position & 1


def column(index, part):
    return pl.ds(pl.multiple_of(index * part, 128), part)


def tiles(rows, columns):
    return [
        (i, min(8, rows - i), j, min(128, columns - j))
        for i in range(0, rows, 8)
        for j in range(0, columns, 128)
    ]


def two_parts(x):
    high = x.astype(jnp.bfloat16)
    return high, (x - high.astype(f32)).astype(jnp.bfloat16)


def dot(a, b, contract):
    return lax.dot_general(a, b, (contract, ((), ())), preferred_element_type=f32)


def name_places(slots, owners, row_of, block_of, owned):
    blocks, owner_count = row_of.shape[0], owned.shape[0]

    def clear(i, carry):
        block_of[i] = 0
        return carry

    def clear_count(i, carry):
        owned[i] = 0
        return carry

    def name(u, carry):
        owner = owners[u]
        slot = owned[owner]
        row = owner * slots + slot
        row_of[u] = row
        block_of[row] = u
        owned[owner] = slot + 1
        return carry

    short = blocks <= 16
    lax.fori_loop(0, block_of.shape[0], clear, 0, unroll=short)
    lax.fori_loop(0, owner_count, clear_count, 0, unroll=short)
    lax.fori_loop(0, blocks, name, 0, unroll=short)


def start_body(groups, part, owners, anchor, inner, momentum, *refs):
    outs, (quarter, same, other), named, scratch = (
        refs[:groups],
        refs[groups : groups + 3],
        refs[groups + 3 : groups + 6],
        refs[groups + 6 :],
    )
    own, far, near, sem, piece_sem = scratch
    rep, chip, core = place()
    blocks = quarter.shape[0]
    chips = same.shape[0]
    listed = pltpu.make_async_copy(owners, own, sem.at[2])
    listed.start()
    dense_moves = [
        pltpu.make_async_copy(anchor, far, sem.at[0]),
        pltpu.make_async_copy(inner.at[0], near, sem.at[1]),
    ]
    for move in dense_moves:
        move.start()
    pieces = [
        pltpu.make_async_copy(
            momentum.at[:, column((2 * to + (core ^ o)) * groups + rep, part)],
            out.at[to],
            piece_sem.at[2 * to + o],
        )
        for to in range(chips)
        for o, out in enumerate((same, other))
    ]
    for piece in pieces:
        piece.start()
    listed.wait()
    name_places(same.shape[1], own, *named)
    dense_tiles = tiles(blocks, part)
    for move in dense_moves:
        move.wait()
    for k in range(groups):
        for t, (i, height, j, width) in enumerate(dense_tiles):
            columns = pl.ds(pl.multiple_of((rep ^ k) * part + j, 128), width)
            rows = slice(i, i + height)
            outs[k][8 * t : 8 * t + height, :width] = far[rows, columns] - near[rows, columns]
            if k == 0:
                quarter[rows, j : j + width] = far[rows, columns]
    for piece in pieces:
        piece.wait()


def factor_body(anchor, inner, basis_t, out):
    rank = out.shape[0]
    high, low = two_parts(anchor[...] - inner[0])
    basis_high, basis_low = two_parts(basis_t[...])
    both = dot(jnp.concatenate([basis_high, basis_low], axis=0), high, ((1,), (1,)))
    out[...] = both[:rank] + (both[rank:] + dot(basis_high, low, ((1,), (1,))))


def mean_body(groups, direct, block_of, *refs):
    parts, (mean, *outs) = refs[:groups], refs[groups:]
    _, here, core = place()
    dense_tiles = tiles(*mean.shape)
    for t, (i, height, j, width) in enumerate(dense_tiles):
        at = slice(8 * t, 8 * t + height)
        total = parts[0][at, :width]
        for ref in parts[1:]:
            total = total + ref[at, :width]
        mean[i : i + height, j : j + width] = total / groups
    slots = outs[0].shape[-2]

    def fill(k, carry):
        for o in range(2):
            owner = 2 * (here ^ k if direct else k) + (core ^ o)
            for s in range(slots):
                row = mean[pl.ds(block_of[owner * slots + s], 1), :]
                if direct:
                    outs[k][o, pl.ds(s, 1), :] = row
                else:
                    outs[0][k, o, pl.ds(s, 1), :] = row
        return carry

    if direct:
        for k in range(len(outs)):
            fill(k, 0)
    else:
        lax.fori_loop(0, outs[0].shape[0], fill, 0)


def pack_body(direct, same, other, *outs):
    _, chip, _ = place()
    if direct:
        for k, out in enumerate(outs):
            out[0] = same[chip ^ k]
            out[1] = other[chip ^ k]
    else:
        outs[0][:, 0] = same[...]
        outs[0][:, 1] = other[...]


def rows_body(direct, *refs):
    *received, out = refs
    chips = len(received) if direct else received[0].shape[0]
    part = received[0].shape[-1]

    def fill(k, carry):
        out[:, column(k, part)] = received[k][1] if direct else received[0][k, 1]
        return carry

    if direct:
        for k in range(chips):
            fill(k, 0)
    else:
        lax.fori_loop(0, chips, fill, 0)
    spare = out.shape[1] - chips * part
    out[:, chips * part :] = jnp.zeros((out.shape[0], spare), f32)


def new_momentum_body(direct, o, owned, momentum, *refs):
    *received, out = refs
    rep, here, core = place()
    slots, groups = momentum.shape[0], lax.axis_size("rep")
    chips = lax.axis_size("own") // 2
    part = momentum.shape[1] // (2 * chips * groups)
    live = lax.broadcasted_iota(jnp.int32, (slots, part), 0) < owned[here * 2 + core]

    def fill(k, carry):
        piece = 2 * (here ^ k if direct else k) + (core ^ o)
        if o == 1:
            rows = received[0][:, column(k, part)]
        else:
            rows = received[k][0] if direct else received[0][k, 0]
        rows = momentum_decay * momentum[:, column(piece * groups + rep, part)] + rows
        out[:, column(k, part)] = jnp.where(live, rows, 0.0)
        return carry

    if direct:
        for k in range(chips):
            fill(k, 0)
    else:
        lax.fori_loop(0, chips, fill, 0)
    spare = out.shape[1] - chips * part
    out[:, chips * part :] = jnp.zeros((slots, spare), f32)


def cut_body(ref, out):
    out[...] = ref[: out.shape[0], :]


def fold(tile, out, lane):
    for h in range(0, tile.shape[0], 4):
        out[:, lane + 32 * h : lane + 32 * h + tile.shape[1]] = tile[h : h + 4, :]


def unfold(ref, lane, height, width):
    runs = [ref[:, lane + 32 * h : lane + 32 * h + width] for h in range(0, height, 4)]
    return jnp.concatenate(runs, axis=0)


def again_body(skip, first, second, factor, received1, received2, out1, out2, pair):
    out1[:, :skip] = first[:, :skip]
    out2[:, :skip] = second[:, :skip]
    factor_tiles = tiles(*factor.shape)
    at = received2.shape[0] - 8 * len(factor_tiles)
    count = at // 16
    for t in range(count):
        fold(received1[8 * t : 8 * t + 8, :], out1, skip + 256 * t)
        fold(received2[8 * (count + t) : 8 * (count + t) + 8, :], out2, skip + 256 * t)
    skip += 256 * count
    for t, (i, height, j, width) in enumerate(factor_tiles):
        total = factor[i : i + height, j : j + width] + received2[at : at + height, :width]
        pair[i : i + height, j : j + width] = total
        fold(total, out2, skip + 256 * t)
        at += 8


def copies_body(*refs):
    count = len(refs) // 2
    for ref, out in zip(refs[:count], refs[count:]):
        out[...] = ref[:, : out.shape[1]]


def dense_body(direct, row_of, quarter, mean, factor, *refs):
    *received, plain, with_factor, rows, work = refs
    _, here, core = place()
    slots = received[0].shape[-2]
    blocks = mean.shape[0]
    if direct:
        for k, ref in enumerate(received):
            rows[k] = ref[...]
        table = rows
    else:
        table = received[0]

    def update(block, carry):
        row = row_of[block]
        owner = row // slots
        chip = (owner // 2) ^ here if direct else owner // 2
        momentum = table[chip, (owner % 2) ^ core, pl.ds(row % slots, 1), :]
        mean_row = mean[pl.ds(block, 1), :]
        new_momentum = momentum_decay * momentum + mean_row
        work[pl.ds(block, 1), :] = quarter[pl.ds(block, 1), :] - outer_rate * (
            mean_row + momentum_decay * new_momentum
        )
        return carry

    lax.fori_loop(0, blocks, update, 0, unroll=blocks <= 16)
    dense_tiles = tiles(*work.shape)
    for t, (i, height, j, width) in enumerate(dense_tiles):
        tile = work[i : i + height, j : j + width]
        plain[8 * t : 8 * t + height, :width] = tile
        with_factor[8 * t : 8 * t + height, :width] = tile
    skip = 8 * len(dense_tiles)
    plain[skip:, :] = jnp.zeros((plain.shape[0] - skip, 128), f32)
    for t, (i, height, j, width) in enumerate(tiles(*factor.shape)):
        at = slice(skip + 8 * t, skip + 8 * t + height)
        with_factor[at, :width] = factor[i : i + height, j : j + width]


class Pieces:
    def __init__(self, part, direct, halves, gradient, result, sem):
        self.part, self.direct, self.halves = part, direct, halves
        self.gradient, self.result, self.sem = gradient, result, sem
        self.chips = sem.shape[1]
        self.groups = result.shape[1] // part // (2 * self.chips)
        self.rep, self.here, self.core = place()

    def each(self, act):
        def body(k, carry):
            for n, (g, o) in enumerate(self.halves):
                piece = 2 * (self.here ^ k if self.direct else k) + (self.core ^ o)
                at = column(piece * self.groups + member(self.rep, self.core, g), self.part)
                source = self.gradient[n].at[:, column(k, self.part)]
                act(pltpu.make_async_copy(source, self.result.at[:, at], self.sem.at[n, k]))
            return carry

        lax.fori_loop(0, self.chips, body, 0, unroll=self.chips <= 8)

    def start(self):
        self.each(lambda copy: copy.start())

    def finish(self):
        self.each(lambda copy: copy.wait())


def early_body(part, direct, halves, *refs):
    *refs, result0, result1, piece_sem, new_dense, sem = refs
    parts, gradient = refs[: -len(halves)], refs[-len(halves) :]
    pieces = Pieces(part, direct, halves, gradient, result1, piece_sem)
    pieces.start()
    rep, _, core = place()
    blocks = new_dense.shape[1]
    copies = []
    for k, ref in enumerate(parts):
        for t, (i, height, j, width) in enumerate(tiles(blocks, part)):
            new_dense[k, i : i + height, j : j + width] = ref[8 * t : 8 * t + height, :width]
        target = result0.at[:, column(member(rep, core, k), part)]
        copies.append(pltpu.make_async_copy(new_dense.at[k], target, sem.at[k]))
        copies[-1].start()
    pieces.finish()
    for copy in copies:
        copy.wait()


def late_body(part, direct, halves, _, __, anchor, momentum_t, basis_t, *refs):
    pair, first, second, *refs = refs
    result0, result1, result2, result3, mean, sem, piece_sem, *whole = refs
    new_dense, new_emb, new_momentum_t = whole
    pieces = Pieces(part, direct, halves, (second, first), result3, piece_sem)
    pieces.start()
    rep, _, core = place()
    groups = pieces.groups
    target = result0.at[:, column(member(rep, core, groups - 1), part)]
    copies = [
        pltpu.make_async_copy(ref, result, sem.at[i])
        for i, (ref, result) in enumerate(
            ((new_dense, target), (new_emb, result1), (new_momentum_t, result2))
        )
    ]
    rank, rows = mean.shape
    skip = second.shape[1] - 256 * len(tiles(rank, rows))
    for t, (i, height, j, width) in enumerate(tiles(rank, rows)):
        here = (slice(i, i + height), slice(j, j + width))
        mean[here] = (pair[here] + unfold(second, skip + 256 * t, height, width)) / groups
    moved = momentum_decay * momentum_t[...] + mean[...]
    new_momentum_t[...] = moved
    copies[2].start()
    high, low = two_parts(mean[...] + momentum_decay * moved)
    basis_high, basis_low = two_parts(basis_t[...])
    back = dot(
        jnp.concatenate([high, low, high], axis=0),
        jnp.concatenate([basis_high, basis_high, basis_low], axis=0),
        ((0,), (0,)),
    )
    new_emb[...] = anchor[...] - outer_rate * back
    copies[1].start()

    dense_tiles = tiles(*new_dense.shape)
    count = len(dense_tiles) // 2
    skip = first.shape[1] - 256 * count
    for t, (i, height, j, width) in enumerate(dense_tiles):
        ref = first if t < count else second
        tile = unfold(ref, skip + 256 * (t % count), height, width)
        new_dense[i : i + height, j : j + width] = tile
    copies[0].start()
    pieces.finish()
    for copy in copies:
        copy.wait()


def last_body(part, direct, halves, _, *refs):
    *gradient, result, sem = refs
    pieces = Pieces(part, direct, halves, gradient, result, sem)
    pieces.start()
    pieces.finish()


def over_chips(outs, direct, owner_count):
    if direct:
        return [outs[0]] + [swap(outs[k], "own", owner_count, 2 * k) for k in range(1, len(outs))]
    groups = [list(range(core, owner_count, 2)) for core in range(2)]
    return [
        lax.all_to_all(
            outs[0], "own", split_axis=0, concat_axis=0, axis_index_groups=groups, tiled=True
        )
    ]


def per_device(
    owners, inner_dense, anchor_dense, momentum_dense, inner_emb, anchor_emb, momentum_emb, basis
):
    owner_count = lax.axis_size("own")
    groups = lax.axis_size("rep")
    chips = owner_count // 2
    direct = chips <= most_direct_chips
    slot_count = momentum_dense.shape[0]
    blocks, piece_len = anchor_dense.shape
    part = piece_len // groups
    rows, rank = momentum_emb.shape
    basis_t = basis.T
    chunk = (chips, slot_count, part)
    table = (chips, 2, slot_count, part)
    parted = [kept(table[1:])] * chips if direct else [kept(table)]

    *parts, quarter, same, other, row_of, block_of, owned = run(
        functools.partial(start_body, groups, part),
        [kept((8 * len(tiles(blocks, part)), 128))] * groups
        + [kept((blocks, part))]
        + [kept(chunk)] * 2
        + [pltpu.SMEM((n,), jnp.int32) for n in (blocks, owner_count * slot_count, owner_count)],
        [],
        far=[
            owners[:, 0],
            anchor_dense,
            inner_dense,
            momentum_dense,
        ],
        out_specs=[vmem] * (groups + 3) + [smem] * 3,
        scratch=[
            pltpu.SMEM((blocks,), jnp.int32),
            pltpu.VMEM(anchor_dense.shape, f32),
            pltpu.VMEM(anchor_dense.shape, f32),
            pltpu.SemaphoreType.DMA((3,)),
            pltpu.SemaphoreType.DMA((owner_count,)),
        ],
        name="start",
    )
    parts = [parts[0]] + [swap(parts[k], "rep", groups, k) for k in range(1, groups)]

    other = swap(other, "own", owner_count, 1)
    packed = run(functools.partial(pack_body, direct), parted, [same, other], name="pack")
    momentum_rows = over_chips(packed, direct, owner_count)

    (factor,) = run(
        factor_body, [kept((rank, rows))], [anchor_emb, inner_emb, basis_t], name="factor"
    )
    mean, *sent = run(
        functools.partial(mean_body, groups, direct),
        [kept((blocks, part))] + parted,
        parts,
        [block_of],
        after=[factor],
        name="mean",
    )
    gradient_rows = over_chips(sent, direct, owner_count)
    length = chips * part
    (other,) = run(
        functools.partial(rows_body, direct),
        [kept((slot_count, length + 256))],
        gradient_rows,
        after=[gradient_rows[k] for k in (3, 2, 1)] if direct else (),
        name="other",
    )
    momentum = on_chip(momentum_dense)
    (mine,) = run(
        functools.partial(new_momentum_body, direct, 0),
        [kept((slot_count, length + 512))],
        [momentum, *gradient_rows],
        [owned],
        after=[gradient_rows[k] for k in (3, 2, 1)] if direct else (),
        name="mine",
    )
    (crossed,) = run(
        functools.partial(new_momentum_body, direct, 1),
        [kept((slot_count, length + 256))],
        [momentum, swap(other, "own", owner_count, 1)],
        [owned],
        name="crossed",
    )
    halves = [mine, crossed]

    dense_rows = 8 * len(tiles(blocks, part))
    plain, with_factor = run(
        functools.partial(dense_body, direct),
        [kept((dense_rows + 16, 128)), kept((dense_rows + 8 * len(tiles(rank, rows)), 128))],
        [quarter, mean, factor, *momentum_rows],
        [row_of],
        [
            pltpu.VMEM(table if direct else (8, 128), f32),
            pltpu.VMEM((blocks, part), f32),
        ],
        after=[*momentum_rows[:0:-1], momentum],
        name="dense",
    )
    dense = [plain, swap_in_turn(plain, 0), swap_in_turn(with_factor, 1)]

    passed_on = 16 * dense_rows
    *again, pair = run(
        functools.partial(again_body, length),
        [
            kept((slot_count, length + passed_on)),
            kept((slot_count, length + passed_on + 256 * len(tiles(rank, rows)))),
            kept((rank, rows)),
        ],
        [*halves, factor, dense[1], dense[2]],
        name="again",
    )
    (sign,) = run(
        cut_body, [kept((dense_rows + 4, 128))], [plain], after=dense[1:], name="gathered"
    )
    sign = swap(sign, "own", owner_count, 1)
    near1 = swap_in_turn(halves[0], 0)
    near2 = swap_in_turn(halves[1], 1)
    passed = run(
        copies_body,
        [kept((slot_count, length))] * 2,
        [near1, near2],
        after=[sign],
        name="pass_on",
    )
    late2, late1 = swap_in_turn(again[1], 0), swap_in_turn(again[0], 1)
    last1, last2 = swap_in_turn(passed[0], 1), swap_in_turn(passed[1], 0)

    def finishing(body, halves, outs, operands, aliased=(), before=(), after=(), name=None):
        return pl.pallas_call(
            functools.partial(body, part, direct, halves),
            out_shape=[stored(shape) for shape in outs],
            in_specs=[anywhere] * len(aliased) + [vmem] * len(operands),
            out_specs=[anywhere] * len(outs),
            scratch_shapes=[
                *before,
                pltpu.SemaphoreType.DMA((len(halves), chips)),
                *after,
            ],
            input_output_aliases={i: out for i, (_, out) in enumerate(aliased)},
            compiler_params=pltpu.CompilerParams(vmem_limit_bytes=vmem_limit),
            name=name,
        )(*[x for x, _ in aliased], *[on_chip(x) for x in operands])

    held = momentum_dense.shape
    new_dense, new_momentum_dense = finishing(
        early_body,
        ((0, 0), (0, 1), (1, 0), (2, 1)),
        [anchor_dense.shape, held],
        [*dense, *halves, near1, near2],
        after=[
            pltpu.VMEM((groups - 1, blocks, part), f32),
            pltpu.SemaphoreType.DMA((groups - 1,)),
        ],
        name="early",
    )
    new_dense, new_emb, new_momentum_t, new_momentum_dense = finishing(
        late_body,
        ((1, 1), (2, 0)),
        [anchor_dense.shape, anchor_emb.shape, (rank, rows), held],
        [anchor_emb, momentum_emb.T, basis_t, pair, late1, late2],
        aliased=[(new_dense, 0), (new_momentum_dense, 3)],
        before=[pltpu.VMEM((rank, rows), f32), pltpu.SemaphoreType.DMA((3,))],
        after=[
            pltpu.VMEM((blocks, part), f32),
            pltpu.VMEM(anchor_emb.shape, f32),
            pltpu.VMEM((rank, rows), f32),
        ],
        name="late",
    )
    (new_momentum_dense,) = finishing(
        last_body,
        ((3, 0), (3, 1)),
        [held],
        [last1, last2],
        aliased=[(new_momentum_dense, 0)],
        name="last",
    )
    return (new_dense, new_momentum_dense, new_emb, new_momentum_t.T)


def solution(mesh):
    placed = (
        P(),
        P("rep", None, "own"),
        P(None, "own"),
        P("own", None),
        P("rep", "own", None),
        P("own", None),
        P("own", None),
        P(),
    )
    return jax.shard_map(
        per_device,
        mesh=mesh,
        in_specs=placed,
        out_specs=(P(None, "own"), P("own", None), P("own", None), P("own", None)),
        check_vma=False,
    )
```

```python
import functools

import jax
import jax.numpy as jnp
from jax import lax
from jax.experimental import pallas as pl
from jax.experimental.pallas import tpu as pltpu
from jax.sharding import PartitionSpec as P

outer_rate = 0.7
momentum_decay = 0.9
most_direct_chips = 8
f32 = jnp.float32
vmem_limit = 48 * 1024 * 1024

vmem = pl.BlockSpec(memory_space=pltpu.VMEM)
smem = pl.BlockSpec(memory_space=pltpu.SMEM)
anywhere = pl.BlockSpec(memory_space=pl.ANY)


def on_chip(x):
    return pltpu.with_memory_space_constraint(x, pltpu.VMEM)


def in_scalars(x):
    return pltpu.with_memory_space_constraint(x, pltpu.SMEM)


def in_hbm(x):
    return pltpu.with_memory_space_constraint(x, pltpu.HBM)


def kept(shape):
    return pltpu.VMEM(shape, f32)


def stored(shape):
    return jax.ShapeDtypeStruct(shape, f32)


def run(
    body, outs, operands, scalars=(), scratch=(), far=(), after=(), out_specs=None, name=None
):
    skip = len(after)

    def whole(*refs):
        body(*refs[skip:])

    return pl.pallas_call(
        whole,
        out_shape=list(outs),
        in_specs=[anywhere] * skip
        + [smem] * len(scalars)
        + [anywhere] * len(far)
        + [vmem] * len(operands),
        out_specs=out_specs or [vmem] * len(outs),
        scratch_shapes=list(scratch),
        compiler_params=pltpu.CompilerParams(vmem_limit_bytes=vmem_limit),
        name=name,
    )(
        *[on_chip(x) for x in after],
        *[in_scalars(x) for x in scalars],
        *[in_hbm(x) for x in far],
        *[on_chip(x) for x in operands],
    )


def swap(x, axis, count, mask):
    return lax.ppermute(x, axis, [(i, i ^ mask) for i in range(count)])


def turn(step, core):
    return 1 + ((step + core) & 1)


def swap_in_turn(x, step):
    groups, owner_count = lax.axis_size("rep"), lax.axis_size("own")
    pairs = [
        (rep * owner_count + own, (rep ^ turn(step, own & 1)) * owner_count + own)
        for rep in range(groups)
        for own in range(owner_count)
    ]
    return lax.ppermute(x, ("rep", "own"), pairs)


def member(rep, core, k):
    return rep ^ (k if k in (0, 3) else turn(k - 1, core))


def place():
    position = lax.axis_index("own")
    return lax.axis_index("rep"), lax.shift_right_logical(position, 1), position & 1


def column(index, part):
    return pl.ds(pl.multiple_of(index * part, 128), part)


def tiles(rows, columns):
    return [
        (i, min(8, rows - i), j, min(128, columns - j))
        for i in range(0, rows, 8)
        for j in range(0, columns, 128)
    ]


def two_parts(x):
    high = x.astype(jnp.bfloat16)
    return high, (x - high.astype(f32)).astype(jnp.bfloat16)


def dot(a, b, contract):
    return lax.dot_general(a, b, (contract, ((), ())), preferred_element_type=f32)


def name_places(slots, owners, row_of, block_of, owned):
    blocks, owner_count = row_of.shape[0], owned.shape[0]

    def clear(i, carry):
        block_of[i] = 0
        return carry

    def clear_count(i, carry):
        owned[i] = 0
        return carry

    def name(u, carry):
        owner = owners[u]
        slot = owned[owner]
        row = owner * slots + slot
        row_of[u] = row
        block_of[row] = u
        owned[owner] = slot + 1
        return carry

    short = blocks <= 16
    lax.fori_loop(0, block_of.shape[0], clear, 0, unroll=short)
    lax.fori_loop(0, owner_count, clear_count, 0, unroll=short)
    lax.fori_loop(0, blocks, name, 0, unroll=short)


def start_body(groups, part, owners, anchor, inner, momentum, *refs):
    outs, (quarter, same, other), named, scratch = (
        refs[:groups],
        refs[groups : groups + 3],
        refs[groups + 3 : groups + 6],
        refs[groups + 6 :],
    )
    own, far, near, sem, piece_sem = scratch
    rep, chip, core = place()
    blocks = quarter.shape[0]
    chips = same.shape[0]
    listed = pltpu.make_async_copy(owners, own, sem.at[2])
    listed.start()
    dense_moves = [
        pltpu.make_async_copy(anchor, far, sem.at[0]),
        pltpu.make_async_copy(inner.at[0], near, sem.at[1]),
    ]
    for move in dense_moves:
        move.start()
    pieces = [
        pltpu.make_async_copy(
            momentum.at[:, column((2 * to + (core ^ o)) * groups + rep, part)],
            out.at[to],
            piece_sem.at[2 * to + o],
        )
        for to in range(chips)
        for o, out in enumerate((same, other))
    ]
    for piece in pieces:
        piece.start()
    listed.wait()
    name_places(same.shape[1], own, *named)
    dense_tiles = tiles(blocks, part)
    for move in dense_moves:
        move.wait()
    for k in range(groups):
        for t, (i, height, j, width) in enumerate(dense_tiles):
            columns = pl.ds(pl.multiple_of((rep ^ k) * part + j, 128), width)
            rows = slice(i, i + height)
            outs[k][8 * t : 8 * t + height, :width] = far[rows, columns] - near[rows, columns]
            if k == 0:
                quarter[rows, j : j + width] = far[rows, columns]
    for piece in pieces:
        piece.wait()


def factor_body(anchor, inner, basis_t, out):
    rank = out.shape[0]
    high, low = two_parts(anchor[...] - inner[0])
    basis_high, basis_low = two_parts(basis_t[...])
    both = dot(jnp.concatenate([basis_high, basis_low], axis=0), high, ((1,), (1,)))
    out[...] = both[:rank] + (both[rank:] + dot(basis_high, low, ((1,), (1,))))


def mean_body(groups, direct, block_of, *refs):
    parts, (mean, *outs) = refs[:groups], refs[groups:]
    _, here, core = place()
    dense_tiles = tiles(*mean.shape)
    for t, (i, height, j, width) in enumerate(dense_tiles):
        at = slice(8 * t, 8 * t + height)
        total = parts[0][at, :width]
        for ref in parts[1:]:
            total = total + ref[at, :width]
        mean[i : i + height, j : j + width] = total / groups
    slots = outs[0].shape[-2]

    def fill(k, carry):
        for o in range(2):
            owner = 2 * (here ^ k if direct else k) + (core ^ o)
            for s in range(slots):
                row = mean[pl.ds(block_of[owner * slots + s], 1), :]
                if direct:
                    outs[k][o, pl.ds(s, 1), :] = row
                else:
                    outs[0][k, o, pl.ds(s, 1), :] = row
        return carry

    if direct:
        for k in range(len(outs)):
            fill(k, 0)
    else:
        lax.fori_loop(0, outs[0].shape[0], fill, 0)


def pack_body(direct, same, other, *outs):
    _, chip, _ = place()
    if direct:
        for k, out in enumerate(outs):
            out[0] = same[chip ^ k]
            out[1] = other[chip ^ k]
    else:
        outs[0][:, 0] = same[...]
        outs[0][:, 1] = other[...]


def rows_body(direct, *refs):
    *received, out = refs
    chips = len(received) if direct else received[0].shape[0]
    part = received[0].shape[-1]

    def fill(k, carry):
        out[:, column(k, part)] = received[k][1] if direct else received[0][k, 1]
        return carry

    if direct:
        for k in range(chips):
            fill(k, 0)
    else:
        lax.fori_loop(0, chips, fill, 0)


def new_momentum_body(direct, o, owned, momentum, *refs):
    *received, out = refs
    rep, here, core = place()
    slots, groups = momentum.shape[0], lax.axis_size("rep")
    chips = lax.axis_size("own") // 2
    part = momentum.shape[1] // (2 * chips * groups)
    live = lax.broadcasted_iota(jnp.int32, (slots, part), 0) < owned[here * 2 + core]

    def fill(k, carry):
        piece = 2 * (here ^ k if direct else k) + (core ^ o)
        if o == 1:
            rows = received[0][:, column(k, part)]
        else:
            rows = received[k][0] if direct else received[0][k, 0]
        rows = momentum_decay * momentum[:, column(piece * groups + rep, part)] + rows
        out[:, column(k, part)] = jnp.where(live, rows, 0.0)
        return carry

    if direct:
        for k in range(chips):
            fill(k, 0)
    else:
        lax.fori_loop(0, chips, fill, 0)
    spare = out.shape[1] - chips * part
    out[:, chips * part :] = jnp.zeros((slots, spare), f32)


def cut_body(ref, out):
    out[...] = ref[: out.shape[0], :]


def fold(tile, out, lane):
    for h in range(0, tile.shape[0], 4):
        out[:, lane + 32 * h : lane + 32 * h + tile.shape[1]] = tile[h : h + 4, :]


def unfold(ref, lane, height, width):
    runs = [ref[:, lane + 32 * h : lane + 32 * h + width] for h in range(0, height, 4)]
    return jnp.concatenate(runs, axis=0)


def again_body(skip, first, second, factor, received1, received2, out1, out2, pair):
    out1[:, :skip] = first[:, :skip]
    out2[:, :skip] = second[:, :skip]
    factor_tiles = tiles(*factor.shape)
    at = received2.shape[0] - 8 * len(factor_tiles)
    count = at // 16
    for t in range(count):
        fold(received1[8 * t : 8 * t + 8, :], out1, skip + 256 * t)
        fold(received2[8 * (count + t) : 8 * (count + t) + 8, :], out2, skip + 256 * t)
    skip += 256 * count
    for t, (i, height, j, width) in enumerate(factor_tiles):
        total = factor[i : i + height, j : j + width] + received2[at : at + height, :width]
        pair[i : i + height, j : j + width] = total
        fold(total, out2, skip + 256 * t)
        at += 8


def copies_body(*refs):
    count = len(refs) // 2
    for ref, out in zip(refs[:count], refs[count:]):
        out[...] = ref[:, : out.shape[1]]


def dense_body(direct, row_of, quarter, mean, factor, *refs):
    *received, plain, with_factor, rows, work = refs
    _, here, core = place()
    slots = received[0].shape[-2]
    blocks = mean.shape[0]
    if direct:
        for k, ref in enumerate(received):
            rows[k] = ref[...]
        table = rows
    else:
        table = received[0]

    def update(block, carry):
        row = row_of[block]
        owner = row // slots
        chip = (owner // 2) ^ here if direct else owner // 2
        momentum = table[chip, (owner % 2) ^ core, pl.ds(row % slots, 1), :]
        mean_row = mean[pl.ds(block, 1), :]
        new_momentum = momentum_decay * momentum + mean_row
        work[pl.ds(block, 1), :] = quarter[pl.ds(block, 1), :] - outer_rate * (
            mean_row + momentum_decay * new_momentum
        )
        return carry

    lax.fori_loop(0, blocks, update, 0, unroll=blocks <= 16)
    dense_tiles = tiles(*work.shape)
    for t, (i, height, j, width) in enumerate(dense_tiles):
        tile = work[i : i + height, j : j + width]
        plain[8 * t : 8 * t + height, :width] = tile
        with_factor[8 * t : 8 * t + height, :width] = tile
    skip = 8 * len(dense_tiles)
    plain[skip:, :] = jnp.zeros((plain.shape[0] - skip, 128), f32)
    for t, (i, height, j, width) in enumerate(tiles(*factor.shape)):
        at = slice(skip + 8 * t, skip + 8 * t + height)
        with_factor[at, :width] = factor[i : i + height, j : j + width]


class Pieces:
    def __init__(self, part, direct, halves, gradient, result, sem):
        self.part, self.direct, self.halves = part, direct, halves
        self.gradient, self.result, self.sem = gradient, result, sem
        self.chips = sem.shape[1]
        self.groups = result.shape[1] // part // (2 * self.chips)
        self.rep, self.here, self.core = place()

    def each(self, act):
        def body(k, carry):
            for n, (g, o) in enumerate(self.halves):
                piece = 2 * (self.here ^ k if self.direct else k) + (self.core ^ o)
                at = column(piece * self.groups + member(self.rep, self.core, g), self.part)
                source = self.gradient[n].at[:, column(k, self.part)]
                act(pltpu.make_async_copy(source, self.result.at[:, at], self.sem.at[n, k]))
            return carry

        lax.fori_loop(0, self.chips, body, 0, unroll=self.chips <= 8)

    def start(self):
        self.each(lambda copy: copy.start())

    def finish(self):
        self.each(lambda copy: copy.wait())


def early_body(part, direct, halves, *refs):
    *refs, result0, result1, piece_sem, new_dense, sem = refs
    parts, gradient = refs[: -len(halves)], refs[-len(halves) :]
    pieces = Pieces(part, direct, halves, gradient, result1, piece_sem)
    pieces.start()
    rep, _, core = place()
    blocks = new_dense.shape[1]
    copies = []
    for k, ref in enumerate(parts):
        for t, (i, height, j, width) in enumerate(tiles(blocks, part)):
            new_dense[k, i : i + height, j : j + width] = ref[8 * t : 8 * t + height, :width]
        target = result0.at[:, column(member(rep, core, k), part)]
        copies.append(pltpu.make_async_copy(new_dense.at[k], target, sem.at[k]))
        copies[-1].start()
    pieces.finish()
    for copy in copies:
        copy.wait()


def late_body(part, direct, halves, _, __, anchor, momentum_t, basis_t, *refs):
    pair, first, second, *refs = refs
    result0, result1, result2, result3, mean, sem, piece_sem, *whole = refs
    new_dense, new_emb, new_momentum_t = whole
    pieces = Pieces(part, direct, halves, (second, first), result3, piece_sem)
    pieces.start()
    rep, _, core = place()
    groups = pieces.groups
    target = result0.at[:, column(member(rep, core, groups - 1), part)]
    copies = [
        pltpu.make_async_copy(ref, result, sem.at[i])
        for i, (ref, result) in enumerate(
            ((new_dense, target), (new_emb, result1), (new_momentum_t, result2))
        )
    ]
    rank, rows = mean.shape
    skip = second.shape[1] - 256 * len(tiles(rank, rows))
    for t, (i, height, j, width) in enumerate(tiles(rank, rows)):
        here = (slice(i, i + height), slice(j, j + width))
        mean[here] = (pair[here] + unfold(second, skip + 256 * t, height, width)) / groups
    moved = momentum_decay * momentum_t[...] + mean[...]
    new_momentum_t[...] = moved
    copies[2].start()
    high, low = two_parts(mean[...] + momentum_decay * moved)
    basis_high, basis_low = two_parts(basis_t[...])
    back = dot(
        jnp.concatenate([high, low, high], axis=0),
        jnp.concatenate([basis_high, basis_high, basis_low], axis=0),
        ((0,), (0,)),
    )
    new_emb[...] = anchor[...] - outer_rate * back
    copies[1].start()

    dense_tiles = tiles(*new_dense.shape)
    count = len(dense_tiles) // 2
    skip = first.shape[1] - 256 * count
    for t, (i, height, j, width) in enumerate(dense_tiles):
        ref = first if t < count else second
        tile = unfold(ref, skip + 256 * (t % count), height, width)
        new_dense[i : i + height, j : j + width] = tile
    copies[0].start()
    pieces.finish()
    for copy in copies:
        copy.wait()


def last_body(part, direct, halves, _, *refs):
    *gradient, result, sem = refs
    pieces = Pieces(part, direct, halves, gradient, result, sem)
    pieces.start()
    pieces.finish()


def over_chips(outs, direct, owner_count):
    if direct:
        return [outs[0]] + [swap(outs[k], "own", owner_count, 2 * k) for k in range(1, len(outs))]
    groups = [list(range(core, owner_count, 2)) for core in range(2)]
    return [
        lax.all_to_all(
            outs[0], "own", split_axis=0, concat_axis=0, axis_index_groups=groups, tiled=True
        )
    ]


def per_device(
    owners, inner_dense, anchor_dense, momentum_dense, inner_emb, anchor_emb, momentum_emb, basis
):
    owner_count = lax.axis_size("own")
    groups = lax.axis_size("rep")
    chips = owner_count // 2
    direct = chips <= most_direct_chips
    slot_count = momentum_dense.shape[0]
    blocks, piece_len = anchor_dense.shape
    part = piece_len // groups
    rows, rank = momentum_emb.shape
    basis_t = basis.T
    chunk = (chips, slot_count, part)
    table = (chips, 2, slot_count, part)
    parted = [kept(table[1:])] * chips if direct else [kept(table)]

    *parts, quarter, same, other, row_of, block_of, owned = run(
        functools.partial(start_body, groups, part),
        [kept((8 * len(tiles(blocks, part)), 128))] * groups
        + [kept((blocks, part))]
        + [kept(chunk)] * 2
        + [pltpu.SMEM((n,), jnp.int32) for n in (blocks, owner_count * slot_count, owner_count)],
        [],
        far=[
            owners[:, 0],
            anchor_dense,
            inner_dense,
            momentum_dense,
        ],
        out_specs=[vmem] * (groups + 3) + [smem] * 3,
        scratch=[
            pltpu.SMEM((blocks,), jnp.int32),
            pltpu.VMEM(anchor_dense.shape, f32),
            pltpu.VMEM(anchor_dense.shape, f32),
            pltpu.SemaphoreType.DMA((3,)),
            pltpu.SemaphoreType.DMA((owner_count,)),
        ],
        name="start",
    )
    parts = [parts[0]] + [swap(parts[k], "rep", groups, k) for k in range(1, groups)]

    other = swap(other, "own", owner_count, 1)
    packed = run(functools.partial(pack_body, direct), parted, [same, other], name="pack")
    momentum_rows = over_chips(packed, direct, owner_count)

    (factor,) = run(
        factor_body, [kept((rank, rows))], [anchor_emb, inner_emb, basis_t], name="factor"
    )
    mean, *sent = run(
        functools.partial(mean_body, groups, direct),
        [kept((blocks, part))] + parted,
        parts,
        [block_of],
        after=[factor],
        name="mean",
    )
    gradient_rows = over_chips(sent, direct, owner_count)
    length = chips * part
    (other,) = run(
        functools.partial(rows_body, direct),
        [kept((slot_count, length))],
        gradient_rows,
        after=[gradient_rows[k] for k in (3, 2, 1)] if direct else (),
        name="other",
    )
    momentum = on_chip(momentum_dense)
    (mine,) = run(
        functools.partial(new_momentum_body, direct, 0),
        [kept((slot_count, length + 256))],
        [momentum, *gradient_rows],
        [owned],
        after=[gradient_rows[k] for k in (3, 2, 1)] if direct else (),
        name="mine",
    )
    (crossed,) = run(
        functools.partial(new_momentum_body, direct, 1),
        [kept((slot_count, length + 128))],
        [momentum, swap(other, "own", owner_count, 1)],
        [owned],
        name="crossed",
    )
    halves = [mine, crossed]

    dense_rows = 8 * len(tiles(blocks, part))
    plain, with_factor = run(
        functools.partial(dense_body, direct),
        [kept((dense_rows + 8, 128)), kept((dense_rows + 8 * len(tiles(rank, rows)), 128))],
        [quarter, mean, factor, *momentum_rows],
        [row_of],
        [
            pltpu.VMEM(table if direct else (8, 128), f32),
            pltpu.VMEM((blocks, part), f32),
        ],
        after=[*momentum_rows[:0:-1], momentum],
        name="dense",
    )
    dense = [plain, swap_in_turn(plain, 0), swap_in_turn(with_factor, 1)]

    passed_on = 16 * dense_rows
    *again, pair = run(
        functools.partial(again_body, length),
        [
            kept((slot_count, length + passed_on)),
            kept((slot_count, length + passed_on + 256 * len(tiles(rank, rows)))),
            kept((rank, rows)),
        ],
        [*halves, factor, dense[1], dense[2]],
        name="again",
    )
    (sign,) = run(
        cut_body, [kept((dense_rows + 2, 128))], [plain], after=dense[1:], name="gathered"
    )
    sign = swap(sign, "own", owner_count, 1)
    near1 = swap_in_turn(halves[0], 0)
    near2 = swap_in_turn(halves[1], 1)
    passed = [
        run(copies_body, [kept((slot_count, length + 128))], [near1], name="pass_first")[0],
        run(
            copies_body,
            [kept((slot_count, length))],
            [near2],
            after=[sign],
            name="pass_second",
        )[0],
    ]
    late2, late1 = swap_in_turn(again[1], 0), swap_in_turn(again[0], 1)
    last1, last2 = swap_in_turn(passed[0], 1), swap_in_turn(passed[1], 0)

    def finishing(body, halves, outs, operands, aliased=(), before=(), after=(), name=None):
        return pl.pallas_call(
            functools.partial(body, part, direct, halves),
            out_shape=[stored(shape) for shape in outs],
            in_specs=[anywhere] * len(aliased) + [vmem] * len(operands),
            out_specs=[anywhere] * len(outs),
            scratch_shapes=[
                *before,
                pltpu.SemaphoreType.DMA((len(halves), chips)),
                *after,
            ],
            input_output_aliases={i: out for i, (_, out) in enumerate(aliased)},
            compiler_params=pltpu.CompilerParams(vmem_limit_bytes=vmem_limit),
            name=name,
        )(*[x for x, _ in aliased], *[on_chip(x) for x in operands])

    held = momentum_dense.shape
    new_dense, new_momentum_dense = finishing(
        early_body,
        ((0, 0), (0, 1), (1, 0), (2, 1)),
        [anchor_dense.shape, held],
        [*dense, *halves, near1, near2],
        after=[
            pltpu.VMEM((groups - 1, blocks, part), f32),
            pltpu.SemaphoreType.DMA((groups - 1,)),
        ],
        name="early",
    )
    new_dense, new_emb, new_momentum_t, new_momentum_dense = finishing(
        late_body,
        ((1, 1), (2, 0)),
        [anchor_dense.shape, anchor_emb.shape, (rank, rows), held],
        [anchor_emb, momentum_emb.T, basis_t, pair, late1, late2],
        aliased=[(new_dense, 0), (new_momentum_dense, 3)],
        before=[pltpu.VMEM((rank, rows), f32), pltpu.SemaphoreType.DMA((3,))],
        after=[
            pltpu.VMEM((blocks, part), f32),
            pltpu.VMEM(anchor_emb.shape, f32),
            pltpu.VMEM((rank, rows), f32),
        ],
        name="late",
    )
    (new_momentum_dense,) = finishing(
        last_body,
        ((3, 0), (3, 1)),
        [held],
        [last1, last2],
        aliased=[(new_momentum_dense, 0)],
        name="last",
    )
    return (new_dense, new_momentum_dense, new_emb, new_momentum_t.T)


def solution(mesh):
    placed = (
        P(),
        P("rep", None, "own"),
        P(None, "own"),
        P("own", None),
        P("rep", "own", None),
        P("own", None),
        P("own", None),
        P(),
    )
    return jax.shard_map(
        per_device,
        mesh=mesh,
        in_specs=placed,
        out_specs=(P(None, "own"), P("own", None), P("own", None), P("own", None)),
        check_vma=False,
    )
```

```python
import functools

import jax
import jax.numpy as jnp
from jax import lax
from jax.experimental import pallas as pl
from jax.experimental.pallas import tpu as pltpu
from jax.sharding import PartitionSpec as P

outer_rate = 0.7
momentum_decay = 0.9
most_direct_chips = 8
f32 = jnp.float32
vmem_limit = 48 * 1024 * 1024

vmem = pl.BlockSpec(memory_space=pltpu.VMEM)
smem = pl.BlockSpec(memory_space=pltpu.SMEM)
anywhere = pl.BlockSpec(memory_space=pl.ANY)


def on_chip(x):
    return pltpu.with_memory_space_constraint(x, pltpu.VMEM)


def in_scalars(x):
    return pltpu.with_memory_space_constraint(x, pltpu.SMEM)


def in_hbm(x):
    return pltpu.with_memory_space_constraint(x, pltpu.HBM)


def kept(shape):
    return pltpu.VMEM(shape, f32)


def stored(shape):
    return jax.ShapeDtypeStruct(shape, f32)


def run(
    body, outs, operands, scalars=(), scratch=(), far=(), after=(), out_specs=None, name=None
):
    skip = len(after)

    def whole(*refs):
        body(*refs[skip:])

    return pl.pallas_call(
        whole,
        out_shape=list(outs),
        in_specs=[anywhere] * skip
        + [smem] * len(scalars)
        + [anywhere] * len(far)
        + [vmem] * len(operands),
        out_specs=out_specs or [vmem] * len(outs),
        scratch_shapes=list(scratch),
        compiler_params=pltpu.CompilerParams(vmem_limit_bytes=vmem_limit),
        name=name,
    )(
        *[on_chip(x) for x in after],
        *[in_scalars(x) for x in scalars],
        *[in_hbm(x) for x in far],
        *[on_chip(x) for x in operands],
    )


def swap(x, axis, count, mask):
    return lax.ppermute(x, axis, [(i, i ^ mask) for i in range(count)])


def turn(step, core):
    return 1 + ((step + core) & 1)


def swap_in_turn(x, step):
    groups, owner_count = lax.axis_size("rep"), lax.axis_size("own")
    pairs = [
        (rep * owner_count + own, (rep ^ turn(step, own & 1)) * owner_count + own)
        for rep in range(groups)
        for own in range(owner_count)
    ]
    return lax.ppermute(x, ("rep", "own"), pairs)


def member(rep, core, k):
    return rep ^ (k if k in (0, 3) else turn(k - 1, core))


def place():
    position = lax.axis_index("own")
    return lax.axis_index("rep"), lax.shift_right_logical(position, 1), position & 1


def column(index, part):
    return pl.ds(pl.multiple_of(index * part, 128), part)


def tiles(rows, columns):
    return [
        (i, min(8, rows - i), j, min(128, columns - j))
        for i in range(0, rows, 8)
        for j in range(0, columns, 128)
    ]


def two_parts(x):
    high = x.astype(jnp.bfloat16)
    return high, (x - high.astype(f32)).astype(jnp.bfloat16)


def dot(a, b, contract):
    return lax.dot_general(a, b, (contract, ((), ())), preferred_element_type=f32)


def name_places(slots, owners, row_of, block_of, owned):
    blocks, owner_count = row_of.shape[0], owned.shape[0]

    def clear(i, carry):
        block_of[i] = 0
        return carry

    def clear_count(i, carry):
        owned[i] = 0
        return carry

    def name(u, carry):
        owner = owners[u]
        slot = owned[owner]
        row = owner * slots + slot
        row_of[u] = row
        block_of[row] = u
        owned[owner] = slot + 1
        return carry

    short = blocks <= 16
    lax.fori_loop(0, block_of.shape[0], clear, 0, unroll=short)
    lax.fori_loop(0, owner_count, clear_count, 0, unroll=short)
    lax.fori_loop(0, blocks, name, 0, unroll=short)


def start_body(groups, part, owners, anchor, inner, momentum, *refs):
    outs, (quarter, same, other), named, scratch = (
        refs[:groups],
        refs[groups : groups + 3],
        refs[groups + 3 : groups + 6],
        refs[groups + 6 :],
    )
    own, far, near, sem, piece_sem = scratch
    rep, chip, core = place()
    blocks = quarter.shape[0]
    chips = same.shape[0]
    listed = pltpu.make_async_copy(owners, own, sem.at[2])
    listed.start()
    dense_moves = [
        pltpu.make_async_copy(anchor, far, sem.at[0]),
        pltpu.make_async_copy(inner.at[0], near, sem.at[1]),
    ]
    for move in dense_moves:
        move.start()
    pieces = [
        pltpu.make_async_copy(
            momentum.at[:, column((2 * to + (core ^ o)) * groups + rep, part)],
            out.at[to],
            piece_sem.at[2 * to + o],
        )
        for to in range(chips)
        for o, out in enumerate((same, other))
    ]
    for piece in pieces:
        piece.start()
    listed.wait()
    name_places(same.shape[1], own, *named)
    dense_tiles = tiles(blocks, part)
    for move in dense_moves:
        move.wait()
    for k in range(groups):
        for t, (i, height, j, width) in enumerate(dense_tiles):
            columns = pl.ds(pl.multiple_of((rep ^ k) * part + j, 128), width)
            rows = slice(i, i + height)
            outs[k][8 * t : 8 * t + height, :width] = far[rows, columns] - near[rows, columns]
            if k == 0:
                quarter[rows, j : j + width] = far[rows, columns]
    for piece in pieces:
        piece.wait()


def factor_body(anchor, inner, basis_t, out):
    rank = out.shape[0]
    high, low = two_parts(anchor[...] - inner[0])
    basis_high, basis_low = two_parts(basis_t[...])
    both = dot(jnp.concatenate([basis_high, basis_low], axis=0), high, ((1,), (1,)))
    out[...] = both[:rank] + (both[rank:] + dot(basis_high, low, ((1,), (1,))))


def mean_body(groups, direct, block_of, *refs):
    parts, (mean, *outs) = refs[:groups], refs[groups:]
    _, here, core = place()
    dense_tiles = tiles(*mean.shape)
    for t, (i, height, j, width) in enumerate(dense_tiles):
        at = slice(8 * t, 8 * t + height)
        total = parts[0][at, :width]
        for ref in parts[1:]:
            total = total + ref[at, :width]
        mean[i : i + height, j : j + width] = total / groups
    slots = outs[0].shape[-2]

    def fill(k, carry):
        for o in range(2):
            owner = 2 * (here ^ k if direct else k) + (core ^ o)
            for s in range(slots):
                row = mean[pl.ds(block_of[owner * slots + s], 1), :]
                if direct:
                    outs[k][o, pl.ds(s, 1), :] = row
                else:
                    outs[0][k, o, pl.ds(s, 1), :] = row
        return carry

    if direct:
        for k in range(len(outs)):
            fill(k, 0)
    else:
        lax.fori_loop(0, outs[0].shape[0], fill, 0)


def pack_body(direct, same, other, *outs):
    _, chip, _ = place()
    if direct:
        for k, out in enumerate(outs):
            out[0] = same[chip ^ k]
            out[1] = other[chip ^ k]
    else:
        outs[0][:, 0] = same[...]
        outs[0][:, 1] = other[...]


def rows_body(direct, *refs):
    *received, out = refs
    chips = len(received) if direct else received[0].shape[0]
    part = received[0].shape[-1]

    def fill(k, carry):
        out[:, column(k, part)] = received[k][1] if direct else received[0][k, 1]
        return carry

    if direct:
        for k in range(chips):
            fill(k, 0)
    else:
        lax.fori_loop(0, chips, fill, 0)
    spare = out.shape[1] - chips * part
    out[:, chips * part :] = jnp.zeros((out.shape[0], spare), f32)


def new_momentum_body(direct, o, owned, momentum, *refs):
    *received, out = refs
    rep, here, core = place()
    slots, groups = momentum.shape[0], lax.axis_size("rep")
    chips = lax.axis_size("own") // 2
    part = momentum.shape[1] // (2 * chips * groups)
    live = lax.broadcasted_iota(jnp.int32, (slots, part), 0) < owned[here * 2 + core]

    def fill(k, carry):
        piece = 2 * (here ^ k if direct else k) + (core ^ o)
        if o == 1:
            rows = received[0][:, column(k, part)]
        else:
            rows = received[k][0] if direct else received[0][k, 0]
        rows = momentum_decay * momentum[:, column(piece * groups + rep, part)] + rows
        out[:, column(k, part)] = jnp.where(live, rows, 0.0)
        return carry

    if direct:
        for k in range(chips):
            fill(k, 0)
    else:
        lax.fori_loop(0, chips, fill, 0)
    spare = out.shape[1] - chips * part
    out[:, chips * part :] = jnp.zeros((slots, spare), f32)


def cut_body(ref, out):
    out[...] = ref[: out.shape[0], :]


def fold(tile, out, lane):
    for h in range(0, tile.shape[0], 4):
        out[:, lane + 32 * h : lane + 32 * h + tile.shape[1]] = tile[h : h + 4, :]


def unfold(ref, lane, height, width):
    runs = [ref[:, lane + 32 * h : lane + 32 * h + width] for h in range(0, height, 4)]
    return jnp.concatenate(runs, axis=0)


def again_body(skip, first, second, factor, received1, received2, out1, out2, pair):
    out1[:, :skip] = first[:, :skip]
    out2[:, :skip] = second[:, :skip]
    factor_tiles = tiles(*factor.shape)
    at = received2.shape[0] - 8 * len(factor_tiles)
    count = at // 16
    for t in range(count):
        fold(received1[8 * t : 8 * t + 8, :], out1, skip + 256 * t)
        fold(received2[8 * (count + t) : 8 * (count + t) + 8, :], out2, skip + 256 * t)
    skip += 256 * count
    for t, (i, height, j, width) in enumerate(factor_tiles):
        total = factor[i : i + height, j : j + width] + received2[at : at + height, :width]
        pair[i : i + height, j : j + width] = total
        fold(total, out2, skip + 256 * t)
        at += 8


def copies_body(*refs):
    count = len(refs) // 2
    for ref, out in zip(refs[:count], refs[count:]):
        out[...] = ref[:, : out.shape[1]]


def dense_body(direct, row_of, quarter, mean, factor, *refs):
    *received, plain, with_factor, rows, work = refs
    _, here, core = place()
    slots = received[0].shape[-2]
    blocks = mean.shape[0]
    if direct:
        for k, ref in enumerate(received):
            rows[k] = ref[...]
        table = rows
    else:
        table = received[0]

    def update(block, carry):
        row = row_of[block]
        owner = row // slots
        chip = (owner // 2) ^ here if direct else owner // 2
        momentum = table[chip, (owner % 2) ^ core, pl.ds(row % slots, 1), :]
        mean_row = mean[pl.ds(block, 1), :]
        new_momentum = momentum_decay * momentum + mean_row
        work[pl.ds(block, 1), :] = quarter[pl.ds(block, 1), :] - outer_rate * (
            mean_row + momentum_decay * new_momentum
        )
        return carry

    lax.fori_loop(0, blocks, update, 0, unroll=blocks <= 16)
    dense_tiles = tiles(*work.shape)
    for t, (i, height, j, width) in enumerate(dense_tiles):
        tile = work[i : i + height, j : j + width]
        plain[8 * t : 8 * t + height, :width] = tile
        with_factor[8 * t : 8 * t + height, :width] = tile
    skip = 8 * len(dense_tiles)
    plain[skip:, :] = jnp.zeros((plain.shape[0] - skip, 128), f32)
    for t, (i, height, j, width) in enumerate(tiles(*factor.shape)):
        at = slice(skip + 8 * t, skip + 8 * t + height)
        with_factor[at, :width] = factor[i : i + height, j : j + width]


class Pieces:
    def __init__(self, part, direct, halves, gradient, result, sem):
        self.part, self.direct, self.halves = part, direct, halves
        self.gradient, self.result, self.sem = gradient, result, sem
        self.chips = sem.shape[1]
        self.groups = result.shape[1] // part // (2 * self.chips)
        self.rep, self.here, self.core = place()

    def each(self, act):
        def body(k, carry):
            for n, (g, o) in enumerate(self.halves):
                piece = 2 * (self.here ^ k if self.direct else k) + (self.core ^ o)
                at = column(piece * self.groups + member(self.rep, self.core, g), self.part)
                source = self.gradient[n].at[:, column(k, self.part)]
                act(pltpu.make_async_copy(source, self.result.at[:, at], self.sem.at[n, k]))
            return carry

        lax.fori_loop(0, self.chips, body, 0, unroll=self.chips <= 8)

    def start(self):
        self.each(lambda copy: copy.start())

    def finish(self):
        self.each(lambda copy: copy.wait())


def early_body(part, direct, halves, *refs):
    *refs, result0, result1, piece_sem, new_dense, sem = refs
    parts, gradient = refs[: -len(halves)], refs[-len(halves) :]
    pieces = Pieces(part, direct, halves, gradient, result1, piece_sem)
    pieces.start()
    rep, _, core = place()
    blocks = new_dense.shape[1]
    copies = []
    for k, ref in enumerate(parts):
        for t, (i, height, j, width) in enumerate(tiles(blocks, part)):
            new_dense[k, i : i + height, j : j + width] = ref[8 * t : 8 * t + height, :width]
        target = result0.at[:, column(member(rep, core, k), part)]
        copies.append(pltpu.make_async_copy(new_dense.at[k], target, sem.at[k]))
        copies[-1].start()
    pieces.finish()
    for copy in copies:
        copy.wait()


def late_body(part, direct, halves, _, __, anchor, momentum_t, basis_t, *refs):
    pair, first, second, *refs = refs
    result0, result1, result2, result3, mean, sem, piece_sem, *whole = refs
    new_dense, new_emb, new_momentum_t = whole
    pieces = Pieces(part, direct, halves, (second, first), result3, piece_sem)
    pieces.start()
    rep, _, core = place()
    groups = pieces.groups
    target = result0.at[:, column(member(rep, core, groups - 1), part)]
    copies = [
        pltpu.make_async_copy(ref, result, sem.at[i])
        for i, (ref, result) in enumerate(
            ((new_dense, target), (new_emb, result1), (new_momentum_t, result2))
        )
    ]
    rank, rows = mean.shape
    skip = second.shape[1] - 256 * len(tiles(rank, rows))
    for t, (i, height, j, width) in enumerate(tiles(rank, rows)):
        here = (slice(i, i + height), slice(j, j + width))
        mean[here] = (pair[here] + unfold(second, skip + 256 * t, height, width)) / groups
    moved = momentum_decay * momentum_t[...] + mean[...]
    new_momentum_t[...] = moved
    copies[2].start()
    high, low = two_parts(mean[...] + momentum_decay * moved)
    basis_high, basis_low = two_parts(basis_t[...])
    back = dot(
        jnp.concatenate([high, low, high], axis=0),
        jnp.concatenate([basis_high, basis_high, basis_low], axis=0),
        ((0,), (0,)),
    )
    new_emb[...] = anchor[...] - outer_rate * back
    copies[1].start()

    dense_tiles = tiles(*new_dense.shape)
    count = len(dense_tiles) // 2
    skip = first.shape[1] - 256 * count
    for t, (i, height, j, width) in enumerate(dense_tiles):
        ref = first if t < count else second
        tile = unfold(ref, skip + 256 * (t % count), height, width)
        new_dense[i : i + height, j : j + width] = tile
    copies[0].start()
    pieces.finish()
    for copy in copies:
        copy.wait()


def last_body(part, direct, halves, _, *refs):
    *gradient, result, sem = refs
    pieces = Pieces(part, direct, halves, gradient, result, sem)
    pieces.start()
    pieces.finish()


def over_chips(outs, direct, owner_count):
    if direct:
        return [outs[0]] + [swap(outs[k], "own", owner_count, 2 * k) for k in range(1, len(outs))]
    groups = [list(range(core, owner_count, 2)) for core in range(2)]
    return [
        lax.all_to_all(
            outs[0], "own", split_axis=0, concat_axis=0, axis_index_groups=groups, tiled=True
        )
    ]


def per_device(
    owners, inner_dense, anchor_dense, momentum_dense, inner_emb, anchor_emb, momentum_emb, basis
):
    owner_count = lax.axis_size("own")
    groups = lax.axis_size("rep")
    chips = owner_count // 2
    direct = chips <= most_direct_chips
    slot_count = momentum_dense.shape[0]
    blocks, piece_len = anchor_dense.shape
    part = piece_len // groups
    rows, rank = momentum_emb.shape
    basis_t = basis.T
    chunk = (chips, slot_count, part)
    table = (chips, 2, slot_count, part)
    parted = [kept(table[1:])] * chips if direct else [kept(table)]

    *parts, quarter, same, other, row_of, block_of, owned = run(
        functools.partial(start_body, groups, part),
        [kept((8 * len(tiles(blocks, part)), 128))] * groups
        + [kept((blocks, part))]
        + [kept(chunk)] * 2
        + [pltpu.SMEM((n,), jnp.int32) for n in (blocks, owner_count * slot_count, owner_count)],
        [],
        far=[
            owners[:, 0],
            anchor_dense,
            inner_dense,
            momentum_dense,
        ],
        out_specs=[vmem] * (groups + 3) + [smem] * 3,
        scratch=[
            pltpu.SMEM((blocks,), jnp.int32),
            pltpu.VMEM(anchor_dense.shape, f32),
            pltpu.VMEM(anchor_dense.shape, f32),
            pltpu.SemaphoreType.DMA((3,)),
            pltpu.SemaphoreType.DMA((owner_count,)),
        ],
        name="start",
    )
    parts = [parts[0]] + [swap(parts[k], "rep", groups, k) for k in range(1, groups)]

    other = swap(other, "own", owner_count, 1)
    packed = run(functools.partial(pack_body, direct), parted, [same, other], name="pack")
    momentum_rows = over_chips(packed, direct, owner_count)

    (factor,) = run(
        factor_body, [kept((rank, rows))], [anchor_emb, inner_emb, basis_t], name="factor"
    )
    mean, *sent = run(
        functools.partial(mean_body, groups, direct),
        [kept((blocks, part))] + parted,
        parts,
        [block_of],
        after=[factor],
        name="mean",
    )
    gradient_rows = over_chips(sent, direct, owner_count)
    length = chips * part
    (other,) = run(
        functools.partial(rows_body, direct),
        [kept((slot_count, length + 256))],
        gradient_rows,
        after=[gradient_rows[k] for k in (3, 2, 1)] if direct else (),
        name="other",
    )
    momentum = on_chip(momentum_dense)
    (mine,) = run(
        functools.partial(new_momentum_body, direct, 0),
        [kept((slot_count, length + 512))],
        [momentum, *gradient_rows],
        [owned],
        after=[gradient_rows[k] for k in (3, 2, 1)] if direct else (),
        name="mine",
    )
    (crossed,) = run(
        functools.partial(new_momentum_body, direct, 1),
        [kept((slot_count, length + 256))],
        [momentum, swap(other, "own", owner_count, 1)],
        [owned],
        name="crossed",
    )
    halves = [mine, crossed]

    dense_rows = 8 * len(tiles(blocks, part))
    plain, with_factor = run(
        functools.partial(dense_body, direct),
        [kept((dense_rows + 16, 128)), kept((dense_rows + 8 * len(tiles(rank, rows)), 128))],
        [quarter, mean, factor, *momentum_rows],
        [row_of],
        [
            pltpu.VMEM(table if direct else (8, 128), f32),
            pltpu.VMEM((blocks, part), f32),
        ],
        after=[*([momentum_rows[k] for k in (2, 3, 1)] if direct else []), momentum],
        name="dense",
    )
    dense = [plain, swap_in_turn(plain, 0), swap_in_turn(with_factor, 1)]

    passed_on = 16 * dense_rows
    *again, pair = run(
        functools.partial(again_body, length),
        [
            kept((slot_count, length + passed_on)),
            kept((slot_count, length + passed_on + 256 * len(tiles(rank, rows)))),
            kept((rank, rows)),
        ],
        [*halves, factor, dense[1], dense[2]],
        name="again",
    )
    (sign,) = run(
        cut_body, [kept((dense_rows + 4, 128))], [plain], after=dense[1:], name="gathered"
    )
    sign = swap(sign, "own", owner_count, 1)
    near1 = swap_in_turn(halves[0], 0)
    near2 = swap_in_turn(halves[1], 1)
    passed = run(
        copies_body,
        [kept((slot_count, length))] * 2,
        [near1, near2],
        after=[sign],
        name="pass_on",
    )
    late2, late1 = swap_in_turn(again[1], 0), swap_in_turn(again[0], 1)
    last1, last2 = swap_in_turn(passed[0], 1), swap_in_turn(passed[1], 0)

    def finishing(body, halves, outs, operands, aliased=(), before=(), after=(), name=None):
        return pl.pallas_call(
            functools.partial(body, part, direct, halves),
            out_shape=[stored(shape) for shape in outs],
            in_specs=[anywhere] * len(aliased) + [vmem] * len(operands),
            out_specs=[anywhere] * len(outs),
            scratch_shapes=[
                *before,
                pltpu.SemaphoreType.DMA((len(halves), chips)),
                *after,
            ],
            input_output_aliases={i: out for i, (_, out) in enumerate(aliased)},
            compiler_params=pltpu.CompilerParams(vmem_limit_bytes=vmem_limit),
            name=name,
        )(*[x for x, _ in aliased], *[on_chip(x) for x in operands])

    held = momentum_dense.shape
    new_dense, new_momentum_dense = finishing(
        early_body,
        ((0, 0), (0, 1), (1, 0), (2, 1)),
        [anchor_dense.shape, held],
        [*dense, *halves, near1, near2],
        after=[
            pltpu.VMEM((groups - 1, blocks, part), f32),
            pltpu.SemaphoreType.DMA((groups - 1,)),
        ],
        name="early",
    )
    new_dense, new_emb, new_momentum_t, new_momentum_dense = finishing(
        late_body,
        ((1, 1), (2, 0)),
        [anchor_dense.shape, anchor_emb.shape, (rank, rows), held],
        [anchor_emb, momentum_emb.T, basis_t, pair, late1, late2],
        aliased=[(new_dense, 0), (new_momentum_dense, 3)],
        before=[pltpu.VMEM((rank, rows), f32), pltpu.SemaphoreType.DMA((3,))],
        after=[
            pltpu.VMEM((blocks, part), f32),
            pltpu.VMEM(anchor_emb.shape, f32),
            pltpu.VMEM((rank, rows), f32),
        ],
        name="late",
    )
    (new_momentum_dense,) = finishing(
        last_body,
        ((3, 0), (3, 1)),
        [held],
        [last1, last2],
        aliased=[(new_momentum_dense, 0)],
        name="last",
    )
    return (new_dense, new_momentum_dense, new_emb, new_momentum_t.T)


def solution(mesh):
    placed = (
        P(),
        P("rep", None, "own"),
        P(None, "own"),
        P("own", None),
        P("rep", "own", None),
        P("own", None),
        P("own", None),
        P(),
    )
    return jax.shard_map(
        per_device,
        mesh=mesh,
        in_specs=placed,
        out_specs=(P(None, "own"), P("own", None), P("own", None), P("own", None)),
        check_vma=False,
    )
```
